32 devices in a mesh: groups: 2 (over x), shard: 8 (over z, y), sub: 2 (over core).
Axes of the slice: x: 2, y: 2, z: 4, core: 2. Of those that a mesh axis runs over, the one named last changes fastest.
Arguments:
- queries: bfloat16 [256, 32, 128], P(('groups', 'shard', 'sub')), parts along dimension 0, may hold values from -1.796875 to 1.796875
- passages: bfloat16 [2048, 128, 128], P(('shard', 'sub')), may hold values from -1.796875 to 1.796875
- passage_len: int32 [2048], P(('shard', 'sub')), may hold values from 16 to 128, as said below
- slot_query: int32 [32, 16, 24], P('groups', ('shard', 'sub')), parts along dimension 0, may hold values from 0 to 7
- slot_passage: int32 [32, 16, 24], P('groups', ('shard', 'sub')), parts along dimension 0, may hold values from 0 to 127
- slot_count: int32 [32, 16], P('groups', ('shard', 'sub')), parts along dimension 0, may hold values from 1 to 24, as said below
Outputs:
- slot_score: float32 [32, 16, 24], P(('groups', 'shard', 'sub')), parts along dimension 0
The draws below stay inside these ranges and needn't reach their ends.
There are 2 independent parts, one for each index of `groups`. The reference program is written for one: setup_inputs(seed, part) draws one part's arguments, and reference() takes and returns one part's arrays. A program takes and returns all parts, laid end to end along the dimension named above; an argument that names none is the same for every part. Nothing has to cross between parts.
Inputs may be any that keep to these rules, and one draw needn't show every extreme that they name: `passage_len`: live tokens of a passage; some passage has all 128. Live slots from one source to one owner are its first slot_count entries; some owner receives 24 live slots from every source.
All inputs are finite; a program needn't handle non-finite values.
Results may differ from the reference program's by a relative error of at most 0.0003.
Values may be sent and summed in bfloat16 or wider, within the bound.
No kernel may reach another device: no remote copies, remote signals or barrier semaphores. Data moves between devices by JAX's collectives and lax.ppermute only.
A program may use at most 64 MiB of HBM per device.

```python
import jax
import jax.numpy as jnp
from jax import lax

DIM = 128
QT = 32
PT = 128
Q_DEV = 8
PASS_DEV = 128
CAP = 24
DEV = 16
NQ = 128
NP = 2048


def draw_slot_count(key, part):
    key = jax.random.fold_in(key, 11)
    ranking = jax.random.permutation(jax.random.fold_in(key, 1), DEV)
    heated = ranking < max(1, DEV // 8)
    light = jax.random.randint(jax.random.fold_in(key, 2), (DEV, DEV), 1, CAP // 2 + 1)
    return jnp.where(heated[None, :], CAP, light).astype(jnp.int32)


def draw_passage_len(key, part):
    key = jax.random.fold_in(key, 23)
    lengths = jax.random.randint(jax.random.fold_in(key, 1), (NP,), PT // 8, PT + 1)
    marked = jax.random.randint(jax.random.fold_in(key, 2), (), 0, NP)
    return lengths.at[marked].set(PT).astype(jnp.int32)


def set_ends(entries, key, smallest, largest):
    longest = entries.shape.index(max(entries.shape))
    spots = []
    for shift in (0, 1):
        where = [jax.random.randint(jax.random.fold_in(key, axis), (), 0, length) for axis, length in enumerate(entries.shape)]
        where[longest] = (where[longest] + shift) % entries.shape[longest]
        spots.append(tuple(where))
    return entries.at[spots[0]].set(smallest).at[spots[1]].set(largest)


def levels(rng, dims, cuts, least, top_value):
    level, own = 1.0, jax.random.fold_in(rng, 6)
    for position, shards_of in cuts:
        steps = jnp.exp(jax.random.uniform(jax.random.fold_in(own, position), (shards_of,), jnp.float32, least / len(cuts), top_value / len(cuts)))
        level = level * jnp.repeat(steps, dims[position] // shards_of).reshape([-1 if axis == position else 1 for axis in range(len(dims))])
    return level


def noise(rng, extent, width, most, cuts=(), kind=jnp.bfloat16):
    array = jax.random.normal(rng, extent, jnp.float32) * width
    if len(cuts) > 0:
        array = levels(rng, extent, cuts, -0.22, 0.18) * array
    return jnp.clip(array, min=-most, max=most).astype(kind)


def setup_inputs(seed: int = 0, part: int = 0) -> dict:
    streams_of = jax.random.split(jax.random.key(seed), 7)
    part_keys = jax.random.split(jax.random.fold_in(streams_of[6], part), 7)
    queries = noise(part_keys[0], (NQ, QT, DIM), 0.3, 1.796875, ((0, 16),))
    passages = noise(streams_of[1], (NP, PT, DIM), 0.3, 1.796875, ((0, 16),))
    passage_len = draw_passage_len(jax.random.fold_in(streams_of[6], 71), part)
    slot_query = set_ends(jax.random.randint(part_keys[3], (DEV, DEV, CAP), 0, Q_DEV), jax.random.fold_in(part_keys[3], 1), 0, Q_DEV - 1).astype(jnp.int32)
    slot_passage = set_ends(jax.random.randint(part_keys[4], (DEV, DEV, CAP), 0, PASS_DEV), jax.random.fold_in(part_keys[4], 1), 0, PASS_DEV - 1).astype(jnp.int32)
    slot_count = draw_slot_count(jax.random.fold_in(jax.random.fold_in(streams_of[6], part), 71), part)
    return dict(queries=queries, passages=passages, passage_len=passage_len, slot_query=slot_query, slot_passage=slot_passage, slot_count=slot_count)


def reference(queries, passages, passage_len, slot_query, slot_passage, slot_count):
    slot_pos = jnp.arange(CAP, dtype=jnp.int32)
    owner_base = (jnp.arange(DEV, dtype=jnp.int32) * PASS_DEV)[:, None]
    token_pos = jnp.arange(PT, dtype=jnp.int32)

    def per_source(source):
        first = (source * Q_DEV).astype(jnp.int32)
        own_queries = lax.dynamic_slice_in_dim(queries, first, Q_DEV, 0).astype(jnp.float32)
        query_rows = jnp.take(own_queries, slot_query[source], axis=0)
        passage_rows = owner_base + slot_passage[source]
        chosen = jnp.take(passages, passage_rows, axis=0).astype(jnp.float32)
        sims = jnp.einsum("ocqd,ockd->ocqk", query_rows, chosen)
        limit = jnp.take(passage_len, passage_rows)
        best = jnp.max(jnp.where(token_pos[None, None, None, :] < limit[:, :, None, None], sims, -1e30), axis=3)
        score = jnp.sum(best, axis=2) / QT
        return jnp.where(slot_pos[None, :] < slot_count[source][:, None], score, jnp.zeros_like(score))

    return lax.map(per_source, jnp.arange(DEV, dtype=jnp.int32))
```

```python
import functools

import jax
import jax.numpy as jnp
from jax import lax
from jax.experimental import pallas as pl
from jax.experimental.pallas import tpu as pltpu
from jax.sharding import PartitionSpec as P

STEP = 8


def score_kernel(shards, cap, where_ref, meta_ref, *refs):
    pieces = refs[:shards]
    own_ref, other_ref, out_ref, query_ref, total_ref = refs[shards:]
    q_dev = query_ref.shape[1]
    pass_dev, tok_slots, _ = own_ref.shape
    sources = shards * 2
    me, core = where_ref[0], where_ref[1]
    owner_size = sources * cap * 2 + sources + pass_dev
    for d in range(shards):
        query_ref[d] = pieces[d][...]
    total_ref[...] = jnp.zeros_like(total_ref)
    token = lax.broadcasted_iota(jnp.int32, (tok_slots, query_ref.shape[2]), 0)
    slot = lax.broadcasted_iota(jnp.int32, (STEP, 1), 0)
    lane = lax.broadcasted_iota(jnp.int32, (STEP, total_ref.shape[1]), 1)

    for which, passages in enumerate((own_ref, other_ref)):
        owner = core if which == 0 else 1 - core
        base = which * owner_size

        def one_source(d, carry):
            shard = jnp.bitwise_xor(me, d)
            source = shard * 2 + core
            live = meta_ref[base + sources * cap * 2 + source]

            def one_step(step, carry):
                best = []
                for k in range(STEP):
                    at = base + source * cap + step * STEP + k
                    query = meta_ref[at]
                    passage = meta_ref[at + sources * cap]
                    limit = meta_ref[base + sources * cap * 2 + sources + passage]
                    sims = lax.dot_general(
                        passages[passage], query_ref[d, query],
                        (((1,), (1,)), ((), ())), preferred_element_type=jnp.float32,
                    )
                    best.append(jnp.max(jnp.where(token < limit, sims, -1e30), axis=0, keepdims=True))
                score = jnp.sum(jnp.concatenate(best, axis=0), axis=1, keepdims=True) / query_ref.shape[2]
                score = jnp.where(slot + step * STEP < live, score, 0.0)
                rows = pl.ds(pl.multiple_of(step * STEP, STEP), STEP)
                total_ref[rows, :] = jnp.where(lane == shard * 2 + owner, score, total_ref[rows, :])
                return carry

            lax.fori_loop(0, (live + STEP - 1) // STEP, one_step, 0)
            return carry

        lax.fori_loop(0, shards, one_source, 0)
    out_ref[...] = total_ref[...].T[:sources, :cap]


def on_device(shards, queries, passages, passage_len, slot_query, slot_passage, slot_count):
    sources, _, cap = slot_query.shape
    me, core = lax.axis_index("shard"), lax.axis_index("sub")
    swap = [(0, 1), (1, 0)]
    meta = jnp.concatenate([slot_query.reshape(-1), slot_passage.reshape(-1), slot_count.reshape(-1), passage_len])
    other_passages = lax.ppermute(passages, "sub", swap)
    other_meta = lax.ppermute(meta, "sub", swap)

    def swapped(piece, d):
        return lax.ppermute(piece, "shard", [(i, i ^ d) for i in range(shards)])

    pieces = [queries] + [None] * (shards - 1)
    for d in range(2, shards, 2):
        pieces[d] = swapped(queries, d)
    for d in range(1, shards, 2):
        pieces[d] = swapped(pieces[d - 1], 1)

    vmem, smem = pl.BlockSpec(memory_space=pltpu.VMEM), pl.BlockSpec(memory_space=pltpu.SMEM)
    scores = pl.pallas_call(
        functools.partial(score_kernel, shards, cap),
        out_shape=jax.ShapeDtypeStruct((sources, cap), jnp.float32),
        in_specs=[smem, smem] + [vmem] * (shards + 2),
        out_specs=vmem,
        scratch_shapes=[
            pltpu.VMEM((shards, *queries.shape), queries.dtype),
            pltpu.VMEM((-(-cap // STEP) * STEP, 128), jnp.float32),
        ],
        compiler_params=pltpu.CompilerParams(vmem_limit_bytes=48 * 1024 * 1024),
        cost_estimate=pl.CostEstimate(flops=400_000_000, bytes_accessed=9_000_000, transcendentals=0),
    )(jnp.stack([me, core]).astype(jnp.int32), jnp.concatenate([meta, other_meta]), *pieces, passages, other_passages)
    returned = lax.all_to_all(scores, "shard", split_axis=0, concat_axis=0, tiled=True)
    return returned[None]


def solution(mesh):
    return jax.shard_map(
        functools.partial(on_device, mesh.shape["shard"]),
        mesh=mesh,
        in_specs=(
            P(("groups", "shard", "sub"), None, None),
            P(("shard", "sub"), None, None),
            P(("shard", "sub")),
            P("groups", ("shard", "sub"), None),
            P("groups", ("shard", "sub"), None),
            P("groups", ("shard", "sub")),
        ),
        out_specs=P(("groups", "shard", "sub"), None, None),
        check_vma=False,
    )
```

```python
import functools

import jax
import jax.numpy as jnp
from jax import lax
from jax.experimental import pallas as pl
from jax.experimental.pallas import tpu as pltpu
from jax.sharding import PartitionSpec as P

GROUPS = 8


def score_kernel(shards, pack, *refs):
    owners = (refs[:4], refs[4:8])
    pieces = refs[8 : 8 + shards]
    own_ref, other_ref, out_ref, query_ref, best_ref, work_ref = refs[8 + shards :]
    q_tok, width = query_ref.shape[2:]
    tok_slots = own_ref.shape[1]
    cap = out_ref.shape[1]
    per_source = best_ref.shape[0]
    lanes = pack * q_tok
    me, core = lax.axis_index("shard"), lax.axis_index("sub")
    for d in range(shards):
        query_ref[d] = pieces[d][...]
    best_ref[...] = jnp.zeros_like(best_ref)
    token = lax.broadcasted_iota(jnp.int32, (tok_slots, lanes), 0)
    place = lax.broadcasted_iota(jnp.int32, (1, lanes), 1) // q_tok
    blank = jnp.zeros((q_tok, width), query_ref.dtype)

    for which, passages in enumerate((own_ref, other_ref)):
        slot_query, slot_passage, slot_count, passage_len = owners[which]
        owner = core if which == 0 else 1 - core

        def list_source(d, total):
            live = slot_count[jnp.bitwise_xor(me, d) * 2 + core]
            for g in range(per_source):
                work_ref[total + g] = d * per_source + g
            return total + (live + pack - 1) // pack

        total = lax.fori_loop(0, shards, list_source, 0)
        for g in range(GROUPS):
            work_ref[total + g] = 0

        def one_step(step, carry):
            for j in range(GROUPS):
                work = work_ref[step * GROUPS + j]
                d, g = work // per_source, work % per_source
                shard = jnp.bitwise_xor(me, d)
                source = shard * 2 + core
                rows, cols, limit = [], [], jnp.zeros((1, lanes), jnp.int32)
                for a in range(pack):
                    slot = jnp.minimum(g * pack + a, cap - 1)
                    query, passage = slot_query[source, slot], slot_passage[source, slot]
                    rows.append(jnp.concatenate([blank] * a + [query_ref[d, query]] + [blank] * (pack - 1 - a), axis=1))
                    cols.append(passages[passage])
                    limit = jnp.where(place == a, passage_len[passage], limit)
                sims = lax.dot_general(
                    jnp.concatenate(cols, axis=1), jnp.concatenate(rows, axis=0),
                    (((1,), (1,)), ((), ())), preferred_element_type=jnp.float32,
                )
                best = jnp.max(jnp.where(token < limit, sims, -1e30), axis=0, keepdims=True)
                best = jnp.where(place + g * pack < slot_count[source], best, 0.0)
                best_ref[g, pl.ds(shard * 2 + owner, 1), :] = best
            return carry

        lax.fori_loop(0, (total + GROUPS - 1) // GROUPS, one_step, 0)

    best = jnp.concatenate([best_ref[g] for g in range(per_source)], axis=1)
    high = best.astype(jnp.bfloat16)
    rest = best - high.astype(jnp.float32)
    middle = rest.astype(jnp.bfloat16)
    low = (rest - middle.astype(jnp.float32)).astype(jnp.bfloat16)
    row = lax.broadcasted_iota(jnp.int32, (per_source * lanes, 128), 0)
    col = lax.broadcasted_iota(jnp.int32, (per_source * lanes, 128), 1)
    add = jnp.where(row // q_tok == col, 1.0, 0.0).astype(jnp.bfloat16)
    parts = jnp.dot(jnp.concatenate([high, middle, low], axis=0), add, preferred_element_type=jnp.float32)
    n = best.shape[0]
    out_ref[...] = ((parts[:n] + parts[n : 2 * n] + parts[2 * n :]) / q_tok)[:, :cap]


def on_device(shards, queries, passages, passage_len, slot_query, slot_passage, slot_count):
    sources, _, cap = slot_query.shape
    q_tok = queries.shape[1]
    pack = 128 // q_tok
    per_source = -(-cap // pack)
    swap = [(0, 1), (1, 0)]

    def swapped(piece, d):
        return lax.ppermute(piece, "shard", [(i, i ^ d) for i in range(shards)])

    other_passages = lax.ppermute(passages, "sub", swap)
    pieces = [queries] + [None] * (shards - 1)
    for d in range(2, shards, 2):
        pieces[d] = swapped(queries, d)
    for d in range(1, shards, 2):
        pieces[d] = swapped(pieces[d - 1], 1)
    own = (slot_query, slot_passage, slot_count, passage_len)
    other = [lax.ppermute(x, "sub", swap) for x in own]
    own, other = (
        [q.reshape(sources, cap), p.reshape(sources, cap), c.reshape(sources), n] for q, p, c, n in (own, other)
    )

    vmem, smem = pl.BlockSpec(memory_space=pltpu.VMEM), pl.BlockSpec(memory_space=pltpu.SMEM)
    scores = pl.pallas_call(
        functools.partial(score_kernel, shards, pack),
        out_shape=jax.ShapeDtypeStruct((sources, cap), jnp.float32),
        in_specs=[smem] * 8 + [vmem] * (shards + 2),
        out_specs=vmem,
        scratch_shapes=[
            pltpu.VMEM((shards, *queries.shape), queries.dtype),
            pltpu.VMEM((per_source, sources, 128), jnp.float32),
            pltpu.SMEM((shards * per_source + 2 * GROUPS,), jnp.int32),
        ],
        compiler_params=pltpu.CompilerParams(vmem_limit_bytes=32 * 1024 * 1024),
        cost_estimate=pl.CostEstimate(flops=400_000_000, bytes_accessed=9_000_000, transcendentals=0),
    )(*own, *other, *pieces, passages, other_passages)
    returned = lax.all_to_all(scores, "shard", split_axis=0, concat_axis=0, tiled=True)
    return returned[None]


def solution(mesh):
    return jax.shard_map(
        functools.partial(on_device, mesh.shape["shard"]),
        mesh=mesh,
        in_specs=(
            P(("groups", "shard", "sub"), None, None),
            P(("shard", "sub"), None, None),
            P(("shard", "sub")),
            P("groups", ("shard", "sub"), None),
            P("groups", ("shard", "sub"), None),
            P("groups", ("shard", "sub")),
        ),
        out_specs=P(("groups", "shard", "sub"), None, None),
        check_vma=False,
    )
```

```python
import functools

import jax
import jax.numpy as jnp
from jax import lax
from jax.experimental import pallas as pl
from jax.experimental.pallas import tpu as pltpu
from jax.sharding import PartitionSpec as P

GROUPS = 8
CHUNKS = 4


def pack_kernel(query_hbm, passage_hbm, count_hbm, length_hbm, out_ref, query_ref, passage_ref, count_ref, length_ref, sems):
    copies = [
        pltpu.make_async_copy(src, dst, sems.at[i])
        for i, (src, dst) in enumerate(
            ((query_hbm, query_ref), (passage_hbm, passage_ref), (count_hbm, count_ref), (length_hbm, length_ref))
        )
    ]
    for copy in copies:
        copy.start()
    for copy in copies:
        copy.wait()
    sources, cap = query_ref.shape
    out_ref[:sources, :cap] = query_ref[...]
    out_ref[sources : 2 * sources, :cap] = passage_ref[...]
    out_ref[2 * sources : 2 * sources + 1, :sources] = count_ref[...].reshape(1, sources)
    out_ref[2 * sources + 1 : 2 * sources + 2, : length_ref.shape[0]] = length_ref[...].reshape(1, -1)


def score_kernel(shards, distances, first, pack, cap, *refs):
    meta_hbm, refs = refs[:2], refs[2:]
    pieces, refs = refs[: len(distances)], refs[len(distances) :]
    own_hbm, other_ref, refs = refs[0], refs[1], refs[2:]
    earlier_ref, refs = (None, refs) if first else (refs[0], refs[1:])
    out_ref, refs = refs[0], refs[1:]
    own_ref, refs = (refs[0], refs[1:]) if first else (own_hbm, refs)
    query_ref, best_ref, meta_ref, work_ref, meta_sems, own_sems, piece_sems = refs
    q_tok, width = query_ref.shape[2:]
    pass_dev, tok_slots = own_ref.shape[:2]
    sources = shards * 2
    per_source = best_ref.shape[0]
    lanes = pack * q_tok
    me, core = lax.axis_index("shard"), lax.axis_index("sub")
    copies = [pltpu.make_async_copy(meta_hbm[i], meta_ref.at[i], meta_sems.at[i]) for i in range(2)]
    copies += [pltpu.make_async_copy(piece, query_ref.at[i], piece_sems.at[i]) for i, piece in enumerate(pieces)]
    own_copies = []
    if first:
        size = pass_dev // CHUNKS
        own_copies = [
            pltpu.make_async_copy(own_hbm.at[pl.ds(i * size, size)], own_ref.at[pl.ds(i * size, size)], own_sems.at[i])
            for i in range(CHUNKS)
        ]
    for copy in copies + own_copies:
        copy.start()
    best_ref[...] = jnp.zeros_like(best_ref)
    token = lax.broadcasted_iota(jnp.int32, (tok_slots, lanes), 0)
    place = lax.broadcasted_iota(jnp.int32, (1, lanes), 1) // q_tok
    blank = jnp.zeros((q_tok, width), query_ref.dtype)
    for copy in copies:
        copy.wait()

    for which, passages in ((1, other_ref), (0, own_ref)):
        owner = core if which == 0 else 1 - core
        if which == 0:
            for copy in own_copies:
                copy.wait()

        def shard_of(i):
            return jnp.bitwise_xor(me, i * 2 + distances[0])

        def list_source(i, total):
            live = meta_ref[which, 2 * sources, shard_of(i) * 2 + core]
            for g in range(per_source):
                work_ref[total + g] = i * per_source + g
            return total + (live + pack - 1) // pack

        total = lax.fori_loop(0, len(distances), list_source, 0)
        for g in range(GROUPS):
            work_ref[total + g] = 0

        def one_step(step, carry):
            for j in range(GROUPS):
                work = work_ref[step * GROUPS + j]
                i, g = work // per_source, work % per_source
                source = shard_of(i) * 2 + core
                rows, cols, limit = [], [], jnp.zeros((1, lanes), jnp.int32)
                for a in range(pack):
                    slot = jnp.minimum(g * pack + a, cap - 1)
                    query, passage = meta_ref[which, source, slot], meta_ref[which, sources + source, slot]
                    rows.append(jnp.concatenate([blank] * a + [query_ref[i, query]] + [blank] * (pack - 1 - a), axis=1))
                    cols.append(passages[passage])
                    limit = jnp.where(place == a, meta_ref[which, 2 * sources + 1, passage], limit)
                sims = lax.dot_general(
                    jnp.concatenate(cols, axis=1), jnp.concatenate(rows, axis=0),
                    (((1,), (1,)), ((), ())), preferred_element_type=jnp.float32,
                )
                best = jnp.max(jnp.where(token < limit, sims, -1e30), axis=0, keepdims=True)
                best = jnp.where(place + g * pack < meta_ref[which, 2 * sources, source], best, 0.0)
                best_ref[g, pl.ds(shard_of(i) * 2 + owner, 1), :] = best
            return carry

        lax.fori_loop(0, (total + GROUPS - 1) // GROUPS, one_step, 0)

    best = jnp.concatenate([best_ref[g] for g in range(per_source)], axis=1)
    high = best.astype(jnp.bfloat16)
    rest = best - high.astype(jnp.float32)
    middle = rest.astype(jnp.bfloat16)
    low = (rest - middle.astype(jnp.float32)).astype(jnp.bfloat16)
    row = lax.broadcasted_iota(jnp.int32, (per_source * lanes, 128), 0)
    col = lax.broadcasted_iota(jnp.int32, (per_source * lanes, 128), 1)
    add = jnp.where(row // q_tok == col, 1.0, 0.0).astype(jnp.bfloat16)
    parts = jnp.dot(jnp.concatenate([high, middle, low], axis=0), add, preferred_element_type=jnp.float32)
    n = best.shape[0]
    score = ((parts[:n] + parts[n : 2 * n] + parts[2 * n :]) / q_tok)[:, :cap]
    out_ref[...] = score if first else earlier_ref[...] + score


def on_device(shards, queries, passages, passage_len, slot_query, slot_passage, slot_count):
    sources, _, cap = slot_query.shape
    q_dev, q_tok, width = queries.shape
    pack = 128 // q_tok
    per_source = -(-cap // pack)
    swap = [(0, 1), (1, 0)]
    vmem, hbm, anywhere = (pl.BlockSpec(memory_space=space) for space in (pltpu.VMEM, pltpu.HBM, pl.ANY))

    def swapped(piece, d):
        return lax.ppermute(piece, "shard", [(i, i ^ d) for i in range(shards)])

    def in_hbm(x):
        return pltpu.with_memory_space_constraint(x, pltpu.HBM)

    other_passages = lax.ppermute(passages, "sub", swap)
    pieces = [queries] + [None] * (shards - 1)
    for d in range(2, shards, 2):
        pieces[d] = swapped(queries, d)
    for d in range(1, shards, 2):
        pieces[d] = swapped(pieces[d - 1], 1)

    meta_rows = -(-(2 * sources + 2) // 8) * 8
    meta = pl.pallas_call(
        pack_kernel,
        out_shape=jax.ShapeDtypeStruct((meta_rows, 128), jnp.int32),
        in_specs=[hbm] * 4,
        out_specs=vmem,
        scratch_shapes=[
            pltpu.VMEM((sources, cap), jnp.int32),
            pltpu.VMEM((sources, cap), jnp.int32),
            pltpu.VMEM((sources,), jnp.int32),
            pltpu.VMEM(passage_len.shape, jnp.int32),
            pltpu.SemaphoreType.DMA((4,)),
        ],
        compiler_params=pltpu.CompilerParams(vmem_limit_bytes=4 * 1024 * 1024),
    )(*map(in_hbm, (slot_query.reshape(sources, cap), slot_passage.reshape(sources, cap), slot_count.reshape(sources), passage_len)))
    other_meta = lax.ppermute(meta, "sub", swap)

    def scored(first, own_passages, earlier):
        distances = range(0 if first else 1, shards, 2)
        scores = jax.ShapeDtypeStruct((sources, cap), jnp.float32)
        return pl.pallas_call(
            functools.partial(score_kernel, shards, distances, first, pack, cap),
            out_shape=(scores, jax.ShapeDtypeStruct(passages.shape, passages.dtype)) if first else scores,
            in_specs=[anywhere] * (2 + len(distances)) + [hbm if first else vmem, vmem] + [vmem] * len(earlier),
            out_specs=(vmem, vmem) if first else vmem,
            scratch_shapes=[
                pltpu.VMEM((len(distances), *queries.shape), queries.dtype),
                pltpu.VMEM((per_source, sources, 128), jnp.float32),
                pltpu.SMEM((2, meta_rows, 128), jnp.int32),
                pltpu.SMEM((len(distances) * per_source + 2 * GROUPS,), jnp.int32),
                pltpu.SemaphoreType.DMA((2,)),
                pltpu.SemaphoreType.DMA((CHUNKS,)),
                pltpu.SemaphoreType.DMA((len(distances),)),
            ],
            compiler_params=pltpu.CompilerParams(vmem_limit_bytes=20 * 1024 * 1024),
            cost_estimate=pl.CostEstimate(flops=1_000_000_000, bytes_accessed=9_000_000, transcendentals=0),
        )(meta, other_meta, *(pieces[d] for d in distances), own_passages, other_passages, *earlier)

    pieces[0] = in_hbm(queries)
    scores, own_passages = scored(True, in_hbm(passages), ())
    scores = scored(False, own_passages, (scores,))
    returned = lax.all_to_all(scores, "shard", split_axis=0, concat_axis=0, tiled=True)
    return returned[None]


def solution(mesh):
    return jax.shard_map(
        functools.partial(on_device, mesh.shape["shard"]),
        mesh=mesh,
        in_specs=(
            P(("groups", "shard", "sub"), None, None),
            P(("shard", "sub"), None, None),
            P(("shard", "sub")),
            P("groups", ("shard", "sub"), None),
            P("groups", ("shard", "sub"), None),
            P("groups", ("shard", "sub")),
        ),
        out_specs=P(("groups", "shard", "sub"), None, None),
        check_vma=False,
    )
```

```python
import functools

import jax
import jax.numpy as jnp
from jax import lax
from jax.experimental import pallas as pl
from jax.experimental.pallas import tpu as pltpu
from jax.sharding import PartitionSpec as P

GROUPS = 8
CHUNKS = 8
SHIFT = 8


def pack_kernel(query_hbm, passage_hbm, count_hbm, length_hbm, out_ref, query_ref, passage_ref, count_ref, length_ref, sems):
    copies = [
        pltpu.make_async_copy(src, dst, sems.at[i])
        for i, (src, dst) in enumerate(
            ((query_hbm, query_ref), (passage_hbm, passage_ref), (count_hbm, count_ref), (length_hbm, length_ref))
        )
    ]
    for copy in copies:
        copy.start()
    for copy in copies:
        copy.wait()
    sources, cap = query_ref.shape
    out_ref[:sources, :cap] = query_ref[...]
    out_ref[sources : 2 * sources, :cap] = passage_ref[...]
    out_ref[2 * sources : 2 * sources + 1, :sources] = count_ref[...].reshape(1, sources)
    out_ref[2 * sources + 1 : 2 * sources + 2, : length_ref.shape[0]] = length_ref[...].reshape(1, -1)


def score_kernel(shards, distances, pack, cap, first, *refs):
    n = len(distances)
    meta_hbm, pieces, (own_hbm, other_ref), refs = refs[:2], refs[2 : 2 + n], refs[2 + n : 4 + n], refs[4 + n :]
    outs, refs = refs[:n], refs[n:]
    own_ref, refs = (refs[0], refs[1:]) if first else (own_hbm, refs)
    query_ref, best_ref, meta_ref, work_ref, meta_sems, piece_sems, own_sems = refs
    q_tok, width = query_ref.shape[2:]
    pass_dev, tok_slots = other_ref.shape[:2]
    sources = shards * 2
    per_source = best_ref.shape[0]
    lanes = pack * q_tok
    q_bits = q_tok.bit_length() - 1
    me, core = lax.axis_index("shard"), lax.axis_index("sub")
    copies = [pltpu.make_async_copy(meta_hbm[i], meta_ref.at[i], meta_sems.at[i]) for i in range(2)]
    copies += [pltpu.make_async_copy(piece, query_ref.at[i], piece_sems.at[i]) for i, piece in enumerate(pieces)]
    size = pass_dev // CHUNKS
    own_copies = [
        pltpu.make_async_copy(own_hbm.at[pl.ds(i * size, size)], own_ref.at[pl.ds(i * size, size)], own_sems.at[i])
        for i in range(CHUNKS if first else 0)
    ]
    for copy in copies + own_copies:
        copy.start()
    best_ref[...] = jnp.zeros_like(best_ref)
    token = lax.broadcasted_iota(jnp.int32, (tok_slots, lanes), 0)
    place = lax.shift_right_logical(lax.broadcasted_iota(jnp.int32, (1, lanes), 1), q_bits)
    blank = jnp.zeros((q_tok, width), query_ref.dtype)
    for copy in copies:
        copy.wait()

    for which, passages in ((1, other_ref), (0, own_ref)):
        owner = core if which == 0 else 1 - core
        if which == 0:
            for copy in own_copies:
                copy.wait()

        def source_of(i):
            return jnp.bitwise_xor(me, i * 2 + distances[0]) * 2 + core

        def list_source(i, total):
            live = meta_ref[which, 2 * sources, source_of(i)]
            for g in range(per_source):
                work_ref[total + g] = (i << SHIFT) + g
            return total + lax.shift_right_logical(live + pack - 1, pack.bit_length() - 1)

        total = lax.fori_loop(0, n, list_source, 0)
        for g in range(GROUPS):
            work_ref[total + g] = 0

        def one_step(step, carry):
            for j in range(GROUPS):
                work = work_ref[step * GROUPS + j]
                i, g = lax.shift_right_logical(work, SHIFT), jnp.bitwise_and(work, (1 << SHIFT) - 1)
                source = source_of(i)
                rows, cols, limit = [], [], jnp.zeros((1, lanes), jnp.int32)
                for a in range(pack):
                    slot = g * pack + a
                    if cap % pack:
                        slot = jnp.minimum(slot, cap - 1)
                    query, passage = meta_ref[which, source, slot], meta_ref[which, sources + source, slot]
                    rows.append(jnp.concatenate([blank] * a + [query_ref[i, query]] + [blank] * (pack - 1 - a), axis=1))
                    cols.append(passages[passage])
                    limit = jnp.where(place == a, meta_ref[which, 2 * sources + 1, passage], limit)
                sims = lax.dot_general(
                    jnp.concatenate(cols, axis=1), jnp.concatenate(rows, axis=0),
                    (((1,), (1,)), ((), ())), preferred_element_type=jnp.float32,
                )
                best = jnp.max(jnp.where(token < limit, sims, -1e30), axis=0, keepdims=True)
                best = jnp.where(place + g * pack < meta_ref[which, 2 * sources, source], best, 0.0)
                best_ref[g, pl.ds(i * 2 + owner, 1), :] = best
            return carry

        lax.fori_loop(0, lax.shift_right_logical(total + GROUPS - 1, GROUPS.bit_length() - 1), one_step, 0)

    best = jnp.concatenate([best_ref[g] for g in range(per_source)], axis=1)
    high = best.astype(jnp.bfloat16)
    rest = best - high.astype(jnp.float32)
    middle = rest.astype(jnp.bfloat16)
    low = (rest - middle.astype(jnp.float32)).astype(jnp.bfloat16)
    row = lax.broadcasted_iota(jnp.int32, (per_source * lanes, 128), 0)
    col = lax.broadcasted_iota(jnp.int32, (per_source * lanes, 128), 1)
    add = jnp.where(lax.shift_right_logical(row, q_bits) == col, 1.0, 0.0).astype(jnp.bfloat16)
    parts = jnp.dot(jnp.concatenate([high, middle, low], axis=0), add, preferred_element_type=jnp.float32)
    rows = best.shape[0]
    score = (parts[:rows] + parts[rows : 2 * rows] + parts[2 * rows :]) * (1.0 / q_tok)
    for i, out in enumerate(outs):
        out[...] = score[2 * i : 2 * i + 2, :cap]


def order_kernel(shards, *refs):
    refs, out_ref = list(refs[:-1]), refs[-1]
    me = lax.axis_index("shard")
    odd = jnp.bitwise_and(me, 1) == 1
    for d in range(shards):
        piece = refs.pop(0)[...]
        if d % 2:
            piece = jnp.where(odd, piece, refs.pop(0)[...])
        out_ref[0, pl.ds(jnp.bitwise_xor(me, d) * 2, 2), :] = piece


def on_device(shards, queries, passages, passage_len, slot_query, slot_passage, slot_count):
    sources, _, cap = slot_query.shape
    q_dev, q_tok, width = queries.shape
    pack = 128 // q_tok
    per_source = -(-cap // pack)
    swap = [(0, 1), (1, 0)]
    vmem, hbm, anywhere = (pl.BlockSpec(memory_space=space) for space in (pltpu.VMEM, pltpu.HBM, pl.ANY))
    params = pltpu.CompilerParams(vmem_limit_bytes=12 * 1024 * 1024)

    def placed(space, *arrays):
        return [pltpu.with_memory_space_constraint(x, space) for x in arrays]

    def swapped(piece, d, senders=range(shards)):
        return lax.ppermute(piece, "shard", [(i, i ^ d) for i in senders])

    meta_rows = -(-(2 * sources + 2) // 8) * 8
    meta = pl.pallas_call(
        pack_kernel,
        out_shape=jax.ShapeDtypeStruct((meta_rows, 128), jnp.int32),
        in_specs=[hbm] * 4,
        out_specs=vmem,
        scratch_shapes=[
            pltpu.VMEM((sources, cap), jnp.int32),
            pltpu.VMEM((sources, cap), jnp.int32),
            pltpu.VMEM((sources,), jnp.int32),
            pltpu.VMEM(passage_len.shape, jnp.int32),
            pltpu.SemaphoreType.DMA((4,)),
        ],
        compiler_params=params,
    )(*placed(pltpu.HBM, slot_query.reshape(sources, cap), slot_passage.reshape(sources, cap), slot_count.reshape(sources), passage_len))
    other_passages = lax.ppermute(passages, "sub", swap)

    pieces = [queries] + [None] * (shards - 1)
    for d in range(2, shards, 2):
        pieces[d] = swapped(queries, d)
    sent_meta, pieces[2] = lax.optimization_barrier((meta, pieces[2]))
    other_meta = lax.ppermute(sent_meta, "sub", swap)
    for d in range(1, shards, 2):
        pieces[d] = swapped(pieces[d - 1], 1)

    def scored(distances, own_passages, first):
        n = len(distances)
        scores = [jax.ShapeDtypeStruct((2, cap), jnp.float32)] * n
        loaded = [jax.ShapeDtypeStruct(passages.shape, passages.dtype)] if first else []
        return pl.pallas_call(
            functools.partial(score_kernel, shards, distances, pack, cap, first),
            out_shape=scores + loaded,
            in_specs=[anywhere] * (2 + n) + [hbm if first else vmem, vmem],
            out_specs=[vmem] * (n + len(loaded)),
            scratch_shapes=[
                pltpu.VMEM((n, *queries.shape), queries.dtype),
                pltpu.VMEM((per_source, 2 * n, 128), jnp.float32),
                pltpu.SMEM((2, meta_rows, 128), jnp.int32),
                pltpu.SMEM((n * per_source + 2 * GROUPS,), jnp.int32),
                pltpu.SemaphoreType.DMA((2,)),
                pltpu.SemaphoreType.DMA((n,)),
                pltpu.SemaphoreType.DMA((CHUNKS,)),
            ],
            compiler_params=params,
            cost_estimate=pl.CostEstimate(flops=1_000_000_000, bytes_accessed=9_000_000, transcendentals=0),
        )(meta, other_meta, *(pieces[d] for d in distances), own_passages, *placed(pltpu.VMEM, other_passages))

    pieces[0] = placed(pltpu.HBM, queries)[0]
    even, odd = range(0, shards, 2), range(1, shards, 2)
    returned = [None] * shards
    *scores, own_passages = scored(even, *placed(pltpu.HBM, passages), True)
    for d, score in zip(even, scores):
        returned[d] = [swapped(score, d) if d else score]
    scores = scored(odd, *placed(pltpu.VMEM, own_passages), False)
    for d, score in zip(odd, scores):
        returned[d] = [swapped(score, d, even)]
    scores, returned[1][0] = lax.optimization_barrier((scores, returned[1][0]))
    for d, score in zip(odd, scores):
        returned[d] += [swapped(score, d, odd)]
    returned = [x for at in returned for x in at]
    return pl.pallas_call(
        functools.partial(order_kernel, shards),
        out_shape=jax.ShapeDtypeStruct((1, sources, cap), jnp.float32),
        in_specs=[vmem] * len(returned),
        out_specs=vmem,
        compiler_params=params,
    )(*returned)


def solution(mesh):
    return jax.shard_map(
        functools.partial(on_device, mesh.shape["shard"]),
        mesh=mesh,
        in_specs=(
            P(("groups", "shard", "sub"), None, None),
            P(("shard", "sub"), None, None),
            P(("shard", "sub")),
            P("groups", ("shard", "sub"), None),
            P("groups", ("shard", "sub"), None),
            P("groups", ("shard", "sub")),
        ),
        out_specs=P(("groups", "shard", "sub"), None, None),
        check_vma=False,
    )
```

```python
import functools

import jax
import jax.numpy as jnp
from jax import lax
from jax.experimental import pallas as pl
from jax.experimental.pallas import tpu as pltpu
from jax.sharding import PartitionSpec as P

GROUPS = 8
CHUNKS = 8
SHIFT = 8
QUERY, PASSAGE, LENGTH, COUNT = 0, 32, 64, 96


def pack_kernel(shards, query_hbm, passage_hbm, count_hbm, length_hbm, own_hbm, mine_ref, theirs_ref, own_ref, query_ref, passage_ref, count_ref, length_ref, sems, own_sems):
    copies = [
        pltpu.make_async_copy(src, dst, sems.at[i])
        for i, (src, dst) in enumerate(
            ((query_hbm, query_ref), (passage_hbm, passage_ref), (count_hbm, count_ref), (length_hbm, length_ref))
        )
    ]
    size = own_ref.shape[0] // CHUNKS
    own_copies = [
        pltpu.make_async_copy(own_hbm.at[pl.ds(i * size, size)], own_ref.at[pl.ds(i * size, size)], own_sems.at[i])
        for i in range(CHUNKS)
    ]
    for copy in copies + own_copies:
        copy.start()
    for copy in copies:
        copy.wait()
    cap = query_ref.shape[1]
    lengths = length_ref[...].reshape(1, -1)
    counts = jnp.broadcast_to(count_ref[...].reshape(1, -1), (2 * shards, 2 * shards))
    row = lax.broadcasted_iota(jnp.int32, counts.shape, 0)
    col = lax.broadcasted_iota(jnp.int32, counts.shape, 1)
    counts = jnp.sum(jnp.where(row == col, counts, 0), axis=1, keepdims=True)
    blank = jnp.zeros((2 * shards, 32 - cap), jnp.int32)
    passage = jnp.concatenate([passage_ref[...], blank], axis=1)
    passage = jnp.concatenate([passage] * 4, axis=1)
    length = jnp.take_along_axis(jnp.broadcast_to(lengths, passage.shape), passage, axis=1)
    query = jnp.concatenate([jnp.concatenate([query_ref[...], blank], axis=1)] * 4, axis=1)
    lane = lax.broadcasted_iota(jnp.int32, passage.shape, 1)
    packed = jnp.where(lane < PASSAGE, query, jnp.where(lane < LENGTH, passage, jnp.where(lane < COUNT, length, counts)))
    packed = packed.reshape(shards, 2, 128)
    first = lax.axis_index("sub") == 0
    mine_ref[...] = jnp.where(first, packed[:, 0], packed[:, 1])
    theirs_ref[...] = jnp.where(first, packed[:, 1], packed[:, 0])
    for copy in own_copies:
        copy.wait()


def score_kernel(shards, distances, pack, cap, *refs):
    n = len(distances)
    meta_hbm, pieces, passage_refs, refs = refs[:2], refs[2 : 2 + n], refs[2 + n : 4 + n], refs[-7:]
    out_ref, query_ref, best_ref, meta_ref, work_ref, meta_sems, piece_sems = refs
    q_tok, width = query_ref.shape[2:]
    tok_slots = passage_refs[0].shape[1]
    per_source = best_ref.shape[0]
    lanes = pack * q_tok
    q_bits = q_tok.bit_length() - 1
    me, core = lax.axis_index("shard"), lax.axis_index("sub")
    copies = [pltpu.make_async_copy(meta_hbm[i], meta_ref.at[i], meta_sems.at[i]) for i in range(2)]
    copies += [pltpu.make_async_copy(piece, query_ref.at[i], piece_sems.at[i]) for i, piece in enumerate(reversed(pieces))]
    for copy in copies:
        copy.start()
    best_ref[...] = jnp.zeros_like(best_ref)
    token = lax.broadcasted_iota(jnp.int32, (tok_slots, lanes), 0)
    place = lax.shift_right_logical(lax.broadcasted_iota(jnp.int32, (1, lanes), 1), q_bits)
    blank = jnp.zeros((q_tok, width), query_ref.dtype)
    for copy in copies:
        copy.wait()

    for which, passages in ((0, passage_refs[0]), (1, passage_refs[1])):
        owner = core if which == 0 else 1 - core

        def shard_of(i):
            return jnp.bitwise_xor(me, i * 2 + distances[0])

        def list_source(i, total):
            live = meta_ref[which, shard_of(i), COUNT]
            for g in range(per_source):
                work_ref[total + g] = (i << SHIFT) + g
            return total + lax.shift_right_logical(live + pack - 1, pack.bit_length() - 1)

        total = lax.fori_loop(0, n, list_source, 0)
        for g in range(GROUPS):
            work_ref[total + g] = 0

        def one_step(step, carry):
            for j in range(GROUPS):
                work = work_ref[step * GROUPS + j]
                i, g = lax.shift_right_logical(work, SHIFT), jnp.bitwise_and(work, (1 << SHIFT) - 1)
                shard = shard_of(i)
                rows, cols, limit = [], [], jnp.zeros((1, lanes), jnp.int32)
                for a in range(pack):
                    slot = g * pack + a
                    query, passage = meta_ref[which, shard, QUERY + slot], meta_ref[which, shard, PASSAGE + slot]
                    rows.append(jnp.concatenate([blank] * a + [query_ref[i, query]] + [blank] * (pack - 1 - a), axis=1))
                    cols.append(passages[passage])
                    limit = jnp.where(place == a, meta_ref[which, shard, LENGTH + slot], limit)
                sims = lax.dot_general(
                    jnp.concatenate(cols, axis=1), jnp.concatenate(rows, axis=0),
                    (((1,), (1,)), ((), ())), preferred_element_type=jnp.float32,
                )
                best = jnp.max(jnp.where(token < limit, sims, -1e30), axis=0, keepdims=True)
                best = jnp.where(place + g * pack < meta_ref[which, shard, COUNT], best, 0.0)
                best_ref[g, pl.ds(i * 2 + owner, 1), :] = best
            return carry

        lax.fori_loop(0, lax.shift_right_logical(total + GROUPS - 1, GROUPS.bit_length() - 1), one_step, 0)

    best = jnp.concatenate([best_ref[g] for g in range(per_source)], axis=1)
    high = best.astype(jnp.bfloat16)
    rest = best - high.astype(jnp.float32)
    middle = rest.astype(jnp.bfloat16)
    low = (rest - middle.astype(jnp.float32)).astype(jnp.bfloat16)
    row = lax.broadcasted_iota(jnp.int32, (per_source * lanes, 128), 0)
    col = lax.broadcasted_iota(jnp.int32, (per_source * lanes, 128), 1)
    add = jnp.where(lax.shift_right_logical(row, q_bits) == col, 1.0, 0.0).astype(jnp.bfloat16)
    parts = jnp.dot(jnp.concatenate([high, middle, low], axis=0), add, preferred_element_type=jnp.float32)
    rows = best.shape[0]
    score = (parts[:rows] + parts[rows : 2 * rows] + parts[2 * rows :]) * (1.0 / q_tok)
    out_ref[...] = score[:, :cap]


def merge_kernel(here_ref, there_ref, *outs):
    for i, out in enumerate(outs):
        out[:2] = here_ref[2 * i : 2 * i + 2]
        out[2:] = there_ref[2 * i : 2 * i + 2]


def order_kernel(*refs):
    refs, out_ref = refs[:-1], refs[-1]
    me = lax.axis_index("shard")
    for i, piece in enumerate(refs):
        shard = jnp.bitwise_xor(me, 2 * i)
        out_ref[0, pl.ds(shard * 2, 2), :] = piece[:2]
        out_ref[0, pl.ds(jnp.bitwise_xor(shard, 1) * 2, 2), :] = piece[2:]


def on_device(shards, queries, passages, passage_len, slot_query, slot_passage, slot_count):
    sources, _, cap = slot_query.shape
    q_dev, q_tok, width = queries.shape
    pack = 128 // q_tok
    per_source = -(-cap // pack)
    swap = [(0, 1), (1, 0)]
    vmem, hbm, anywhere = (pl.BlockSpec(memory_space=space) for space in (pltpu.VMEM, pltpu.HBM, pl.ANY))
    params = pltpu.CompilerParams(vmem_limit_bytes=12 * 1024 * 1024)
    row = jax.ShapeDtypeStruct((shards, 128), jnp.int32)

    def placed(space, *arrays):
        return [pltpu.with_memory_space_constraint(x, space) for x in arrays]

    def swapped(piece, d):
        return lax.ppermute(piece, "shard", [(i, i ^ d) for i in range(shards)])

    pieces = [queries] + [None] * (shards - 1)
    for d in reversed(range(2, shards, 2)):
        pieces[d] = swapped(queries, d)
    other_passages = lax.ppermute(passages, "sub", swap)

    mine, theirs, own_passages = pl.pallas_call(
        functools.partial(pack_kernel, shards),
        out_shape=[row, row, jax.ShapeDtypeStruct(passages.shape, passages.dtype)],
        in_specs=[hbm] * 5,
        out_specs=[vmem] * 3,
        scratch_shapes=[
            pltpu.VMEM((sources, cap), jnp.int32),
            pltpu.VMEM((sources, cap), jnp.int32),
            pltpu.VMEM((sources,), jnp.int32),
            pltpu.VMEM(passage_len.shape, jnp.int32),
            pltpu.SemaphoreType.DMA((4,)),
            pltpu.SemaphoreType.DMA((CHUNKS,)),
        ],
        compiler_params=params,
    )(*placed(pltpu.HBM, slot_query.reshape(sources, cap), slot_passage.reshape(sources, cap), slot_count.reshape(sources), passage_len, passages))
    theirs, pieces[-2] = lax.optimization_barrier((theirs, pieces[-2]))
    other = lax.ppermute(theirs, "sub", swap)
    for d in range(1, shards, 2):
        pieces[d] = swapped(pieces[d - 1], 1)

    def scored(distances, after):
        n = len(distances)
        return pl.pallas_call(
            functools.partial(score_kernel, shards, distances, pack, cap),
            out_shape=jax.ShapeDtypeStruct((2 * n, cap), jnp.float32),
            in_specs=[anywhere] * (2 + n) + [vmem] * 2 + [anywhere] * len(after),
            out_specs=vmem,
            scratch_shapes=[
                pltpu.VMEM((n, *queries.shape), queries.dtype),
                pltpu.VMEM((per_source, 2 * n, 128), jnp.float32),
                pltpu.SMEM((2, shards, 128), jnp.int32),
                pltpu.SMEM((n * per_source + 2 * GROUPS,), jnp.int32),
                pltpu.SemaphoreType.DMA((2,)),
                pltpu.SemaphoreType.DMA((n,)),
            ],
            compiler_params=params,
            cost_estimate=pl.CostEstimate(flops=1_000_000_000, bytes_accessed=9_000_000, transcendentals=0),
        )(mine, other, *(pieces[d] for d in reversed(distances)), *placed(pltpu.VMEM, own_passages, other_passages), *after)

    pieces[0] = placed(pltpu.HBM, queries)[0]
    even, odd = range(0, shards, 2), range(1, shards, 2)
    here = scored(even, ())
    there = swapped(scored(odd, (here,)), 1)
    merged = pl.pallas_call(
        merge_kernel,
        out_shape=[jax.ShapeDtypeStruct((4, cap), jnp.float32)] * len(even),
        in_specs=[vmem] * 2,
        out_specs=[vmem] * len(even),
        compiler_params=params,
    )(here, there)
    return pl.pallas_call(
        order_kernel,
        out_shape=jax.ShapeDtypeStruct((1, sources, cap), jnp.float32),
        in_specs=[vmem] * len(even),
        out_specs=vmem,
        compiler_params=params,
    )(*(swapped(piece, d) if d else piece for d, piece in zip(even, merged)))


def solution(mesh):
    return jax.shard_map(
        functools.partial(on_device, mesh.shape["shard"]),
        mesh=mesh,
        in_specs=(
            P(("groups", "shard", "sub"), None, None),
            P(("shard", "sub"), None, None),
            P(("shard", "sub")),
            P("groups", ("shard", "sub"), None),
            P("groups", ("shard", "sub"), None),
            P("groups", ("shard", "sub")),
        ),
        out_specs=P(("groups", "shard", "sub"), None, None),
        check_vma=False,
    )
```

```python
import functools

import jax
import jax.numpy as jnp
from jax import lax
from jax.experimental import pallas as pl
from jax.experimental.pallas import tpu as pltpu
from jax.sharding import PartitionSpec as P

GROUPS = 8
CHUNKS = 8
SHIFT = 8
QUERY, PASSAGE, LENGTH, COUNT = 0, 32, 64, 96


def pack_kernel(shards, query_hbm, passage_hbm, count_hbm, length_hbm, mine_ref, theirs_ref, query_ref, passage_ref, count_ref, length_ref, sems):
    copies = [
        pltpu.make_async_copy(src, dst, sems.at[i])
        for i, (src, dst) in enumerate(
            ((query_hbm, query_ref), (passage_hbm, passage_ref), (count_hbm, count_ref), (length_hbm, length_ref))
        )
    ]
    for copy in copies:
        copy.start()
    for copy in copies:
        copy.wait()
    cap = query_ref.shape[1]
    lengths = length_ref[...].reshape(1, -1)
    counts = jnp.broadcast_to(count_ref[...].reshape(1, -1), (2 * shards, 2 * shards))
    row = lax.broadcasted_iota(jnp.int32, counts.shape, 0)
    col = lax.broadcasted_iota(jnp.int32, counts.shape, 1)
    counts = jnp.sum(jnp.where(row == col, counts, 0), axis=1, keepdims=True)
    blank = jnp.zeros((2 * shards, 32 - cap), jnp.int32)
    passage = jnp.concatenate([passage_ref[...], blank], axis=1)
    passage = jnp.concatenate([passage] * 4, axis=1)
    length = jnp.take_along_axis(jnp.broadcast_to(lengths, passage.shape), passage, axis=1)
    query = jnp.concatenate([jnp.concatenate([query_ref[...], blank], axis=1)] * 4, axis=1)
    lane = lax.broadcasted_iota(jnp.int32, passage.shape, 1)
    packed = jnp.where(lane < PASSAGE, query, jnp.where(lane < LENGTH, passage, jnp.where(lane < COUNT, length, counts)))
    packed = packed.reshape(shards, 2, 128)
    first = lax.axis_index("sub") == 0
    mine_ref[...] = jnp.where(first, packed[:, 0], packed[:, 1])
    theirs_ref[...] = jnp.where(first, packed[:, 1], packed[:, 0])


def score_kernel(shards, distances, pack, cap, first, *refs):
    n = len(distances)
    meta_hbm, pieces, (own_hbm, other_ref), refs = refs[:2], refs[2 : 2 + n], refs[2 + n : 4 + n], refs[4 + n :]
    if first:
        out_ref, own_ref = refs[:2]
    else:
        (earlier_ref, out_ref), own_ref = refs[:2], own_hbm
    query_ref, best_ref, meta_ref, work_ref, meta_sems, piece_sems, own_sems = refs[2:]
    q_tok, width = query_ref.shape[2:]
    pass_dev, tok_slots = other_ref.shape[:2]
    per_source = best_ref.shape[0]
    lanes = pack * q_tok
    q_bits = q_tok.bit_length() - 1
    me, core = lax.axis_index("shard"), lax.axis_index("sub")
    copies = [pltpu.make_async_copy(meta_hbm[i], meta_ref.at[i], meta_sems.at[i]) for i in range(2)]
    copies += [pltpu.make_async_copy(piece, query_ref.at[i], piece_sems.at[i]) for i, piece in enumerate(reversed(pieces))]
    size = pass_dev // CHUNKS
    own_copies = [
        pltpu.make_async_copy(own_hbm.at[pl.ds(i * size, size)], own_ref.at[pl.ds(i * size, size)], own_sems.at[i])
        for i in range(CHUNKS if first else 0)
    ]
    for copy in copies + own_copies:
        copy.start()
    best_ref[...] = jnp.zeros_like(best_ref)
    token = lax.broadcasted_iota(jnp.int32, (tok_slots, lanes), 0)
    place = lax.shift_right_logical(lax.broadcasted_iota(jnp.int32, (1, lanes), 1), q_bits)
    blank = jnp.zeros((q_tok, width), query_ref.dtype)
    for copy in copies:
        copy.wait()

    for which, passages in ((1, other_ref), (0, own_ref)):
        owner = core if which == 0 else 1 - core
        if which == 0:
            for copy in own_copies:
                copy.wait()

        def shard_of(i):
            if first:
                return jnp.bitwise_xor(me, jnp.where(i == n - 1, 1, i * 2))
            return jnp.bitwise_xor(me, i * 2 + distances[0])

        def list_source(i, total):
            live = meta_ref[which, shard_of(i), COUNT]
            for g in range(per_source):
                work_ref[total + g] = (i << SHIFT) + g
            return total + lax.shift_right_logical(live + pack - 1, pack.bit_length() - 1)

        total = lax.fori_loop(0, n, list_source, 0)
        for g in range(GROUPS):
            work_ref[total + g] = 0

        def one_step(step, carry):
            for j in range(GROUPS):
                work = work_ref[step * GROUPS + j]
                i, g = lax.shift_right_logical(work, SHIFT), jnp.bitwise_and(work, (1 << SHIFT) - 1)
                shard = shard_of(i)
                rows, cols, limit = [], [], jnp.zeros((1, lanes), jnp.int32)
                for a in range(pack):
                    slot = g * pack + a
                    query, passage = meta_ref[which, shard, QUERY + slot], meta_ref[which, shard, PASSAGE + slot]
                    rows.append(jnp.concatenate([blank] * a + [query_ref[i, query]] + [blank] * (pack - 1 - a), axis=1))
                    cols.append(passages[passage])
                    limit = jnp.where(place == a, meta_ref[which, shard, LENGTH + slot], limit)
                sims = lax.dot_general(
                    jnp.concatenate(cols, axis=1), jnp.concatenate(rows, axis=0),
                    (((1,), (1,)), ((), ())), preferred_element_type=jnp.float32,
                )
                best = jnp.max(jnp.where(token < limit, sims, -1e30), axis=0, keepdims=True)
                best = jnp.where(place + g * pack < meta_ref[which, shard, COUNT], best, 0.0)
                best_ref[g, pl.ds(i * 2 + owner, 1), :] = best
            return carry

        lax.fori_loop(0, lax.shift_right_logical(total + GROUPS - 1, GROUPS.bit_length() - 1), one_step, 0)

    best = jnp.concatenate([best_ref[g] for g in range(per_source)], axis=1)
    high = best.astype(jnp.bfloat16)
    rest = best - high.astype(jnp.float32)
    middle = rest.astype(jnp.bfloat16)
    low = (rest - middle.astype(jnp.float32)).astype(jnp.bfloat16)
    row = lax.broadcasted_iota(jnp.int32, (per_source * lanes, 128), 0)
    col = lax.broadcasted_iota(jnp.int32, (per_source * lanes, 128), 1)
    add = jnp.where(lax.shift_right_logical(row, q_bits) == col, 1.0, 0.0).astype(jnp.bfloat16)
    parts = jnp.dot(jnp.concatenate([high, middle, low], axis=0), add, preferred_element_type=jnp.float32)
    rows = best.shape[0]
    score = (parts[:rows] + parts[rows : 2 * rows] + parts[2 * rows :]) * (1.0 / q_tok)
    if first:
        out_ref[...] = score[:, :cap]
        return
    for scores, at in ((earlier_ref[...], (*range(0, shards, 2), 1)), (score[:, :cap], distances)):
        for i, d in enumerate(at):
            out_ref[pl.ds((shards - 1 - jnp.bitwise_xor(me, d)) * 2, 2), :] = scores[2 * i : 2 * i + 2]


def order_kernel(back_ref, out_ref):
    shards = back_ref.shape[0] // 2
    for i in range(shards):
        out_ref[0, 2 * i : 2 * i + 2] = back_ref[2 * (shards - 1 - i) : 2 * (shards - i)]


def on_device(shards, queries, passages, passage_len, slot_query, slot_passage, slot_count):
    sources, _, cap = slot_query.shape
    q_dev, q_tok, width = queries.shape
    pack = 128 // q_tok
    per_source = -(-cap // pack)
    swap = [(0, 1), (1, 0)]
    vmem, hbm, anywhere = (pl.BlockSpec(memory_space=space) for space in (pltpu.VMEM, pltpu.HBM, pl.ANY))
    params = pltpu.CompilerParams(vmem_limit_bytes=12 * 1024 * 1024)
    row = jax.ShapeDtypeStruct((shards, 128), jnp.int32)

    def placed(space, *arrays):
        return [pltpu.with_memory_space_constraint(x, space) for x in arrays]

    def swapped(piece, d):
        return lax.ppermute(piece, "shard", [(i, i ^ d) for i in range(shards)])

    pieces = [queries] + [None] * (shards - 1)
    for d in reversed(range(2, shards, 2)):
        pieces[d] = swapped(queries, d)
    other_passages = lax.ppermute(passages, "sub", swap)

    mine, theirs = pl.pallas_call(
        functools.partial(pack_kernel, shards),
        out_shape=[row, row],
        in_specs=[hbm] * 4,
        out_specs=[vmem] * 2,
        scratch_shapes=[
            pltpu.VMEM((sources, cap), jnp.int32),
            pltpu.VMEM((sources, cap), jnp.int32),
            pltpu.VMEM((sources,), jnp.int32),
            pltpu.VMEM(passage_len.shape, jnp.int32),
            pltpu.SemaphoreType.DMA((4,)),
        ],
        compiler_params=params,
    )(*placed(pltpu.HBM, slot_query.reshape(sources, cap), slot_passage.reshape(sources, cap), slot_count.reshape(sources), passage_len))
    theirs, pieces[-4] = lax.optimization_barrier((theirs, pieces[-4]))
    other = lax.ppermute(theirs, "sub", swap)
    for d in range(1, shards, 2):
        pieces[d] = swapped(pieces[d - 1], 1)

    def scored(distances, own_passages, *earlier):
        n, first = len(distances), not earlier
        scores = jax.ShapeDtypeStruct((2 * n if first else sources, cap), jnp.float32)
        loaded = jax.ShapeDtypeStruct(passages.shape, passages.dtype)
        return pl.pallas_call(
            functools.partial(score_kernel, shards, distances, pack, cap, first),
            out_shape=[scores, loaded] if first else scores,
            in_specs=[anywhere] * (2 + n) + [hbm if first else vmem, vmem] + [vmem] * len(earlier),
            out_specs=[vmem] * 2 if first else vmem,
            scratch_shapes=[
                pltpu.VMEM((n, *queries.shape), queries.dtype),
                pltpu.VMEM((per_source, 2 * n, 128), jnp.float32),
                pltpu.SMEM((2, shards, 128), jnp.int32),
                pltpu.SMEM((n * per_source + 2 * GROUPS,), jnp.int32),
                pltpu.SemaphoreType.DMA((2,)),
                pltpu.SemaphoreType.DMA((n,)),
                pltpu.SemaphoreType.DMA((CHUNKS,)),
            ],
            compiler_params=params,
            cost_estimate=pl.CostEstimate(flops=1_000_000_000, bytes_accessed=9_000_000, transcendentals=0),
        )(mine, other, *(pieces[d] for d in reversed(distances)), own_passages, *placed(pltpu.VMEM, other_passages), *earlier)

    pieces[0] = placed(pltpu.HBM, queries)[0]
    scores, own_passages = scored((*range(0, shards, 2), 1), *placed(pltpu.HBM, passages))
    scores = scored(range(3, shards, 2), *placed(pltpu.VMEM, own_passages), scores)
    order = [list(reversed(range(shards)))]
    returned = lax.all_to_all(scores, "shard", split_axis=0, concat_axis=0, axis_index_groups=order, tiled=True)
    return pl.pallas_call(
        order_kernel,
        out_shape=jax.ShapeDtypeStruct((1, sources, cap), jnp.float32),
        in_specs=[vmem],
        out_specs=vmem,
        compiler_params=params,
    )(returned)


def solution(mesh):
    return jax.shard_map(
        functools.partial(on_device, mesh.shape["shard"]),
        mesh=mesh,
        in_specs=(
            P(("groups", "shard", "sub"), None, None),
            P(("shard", "sub"), None, None),
            P(("shard", "sub")),
            P("groups", ("shard", "sub"), None),
            P("groups", ("shard", "sub"), None),
            P("groups", ("shard", "sub")),
        ),
        out_specs=P(("groups", "shard", "sub"), None, None),
        check_vma=False,
    )
```

```python
import functools

import jax
import jax.numpy as jnp
from jax import lax
from jax.experimental import pallas as pl
from jax.experimental.pallas import tpu as pltpu
from jax.sharding import PartitionSpec as P

GROUPS = 8
CHUNKS = 8
SHIFT = 8
QUERY, PASSAGE, LENGTH, COUNT = 0, 32, 64, 96


def pack_kernel(
    shards, query_hbm, passage_hbm, count_hbm, length_hbm, own_hbm,
    mine_ref, theirs_ref, own_ref, query_ref, passage_ref, count_ref, length_ref, sems, own_sems,
):
    copies = [
        pltpu.make_async_copy(src, dst, sems.at[i])
        for i, (src, dst) in enumerate(
            ((query_hbm, query_ref), (passage_hbm, passage_ref), (count_hbm, count_ref), (length_hbm, length_ref))
        )
    ]
    size = own_ref.shape[0] // CHUNKS
    own_copies = [
        pltpu.make_async_copy(own_hbm.at[pl.ds(i * size, size)], own_ref.at[pl.ds(i * size, size)], own_sems.at[i])
        for i in range(CHUNKS)
    ]
    for copy in copies + own_copies:
        copy.start()
    for copy in copies:
        copy.wait()
    cap = query_ref.shape[1]
    lengths = length_ref[...].reshape(1, -1)
    counts = jnp.broadcast_to(count_ref[...].reshape(1, -1), (2 * shards, 2 * shards))
    row = lax.broadcasted_iota(jnp.int32, counts.shape, 0)
    col = lax.broadcasted_iota(jnp.int32, counts.shape, 1)
    counts = jnp.sum(jnp.where(row == col, counts, 0), axis=1, keepdims=True)
    blank = jnp.zeros((2 * shards, 32 - cap), jnp.int32)
    passage = jnp.concatenate([passage_ref[...], blank], axis=1)
    passage = jnp.concatenate([passage] * 4, axis=1)
    length = jnp.take_along_axis(jnp.broadcast_to(lengths, passage.shape), passage, axis=1)
    query = jnp.concatenate([jnp.concatenate([query_ref[...], blank], axis=1)] * 4, axis=1)
    lane = lax.broadcasted_iota(jnp.int32, passage.shape, 1)
    packed = jnp.where(lane < PASSAGE, query, jnp.where(lane < LENGTH, passage, jnp.where(lane < COUNT, length, counts)))
    packed = packed.reshape(shards, 2, 128)
    first = lax.axis_index("sub") == 0
    mine_ref[...] = jnp.where(first, packed[:, 0], packed[:, 1])
    theirs_ref[...] = jnp.where(first, packed[:, 1], packed[:, 0])
    for copy in own_copies:
        copy.wait()


def score_kernel(shards, distances, pack, cap, first, *refs):
    n = len(distances)
    meta_hbm, pieces, passage_refs, refs = refs[:2], refs[2 : 2 + n], refs[2 + n : 4 + n], refs[4 + n :]
    earlier_ref = None if first else refs[0]
    out_ref, query_ref, best_ref, meta_ref, work_ref, meta_sems, piece_sems = refs[-7:]
    q_tok, width = query_ref.shape[2:]
    tok_slots = passage_refs[0].shape[1]
    per_source = best_ref.shape[0]
    lanes = pack * q_tok
    q_bits = q_tok.bit_length() - 1
    me, core = lax.axis_index("shard"), lax.axis_index("sub")
    copies = [pltpu.make_async_copy(meta_hbm[i], meta_ref.at[i], meta_sems.at[i]) for i in range(2)]
    copies += [pltpu.make_async_copy(piece, query_ref.at[i], piece_sems.at[i]) for i, piece in enumerate(reversed(pieces))]
    for copy in copies:
        copy.start()
    best_ref[...] = jnp.zeros_like(best_ref)
    token = lax.broadcasted_iota(jnp.int32, (tok_slots, lanes), 0)
    place = lax.shift_right_logical(lax.broadcasted_iota(jnp.int32, (1, lanes), 1), q_bits)
    blank = jnp.zeros((q_tok, width), query_ref.dtype)
    for copy in copies:
        copy.wait()

    for which, passages in enumerate(passage_refs):
        owner = core if which == 0 else 1 - core

        def shard_of(i):
            if first:
                return jnp.bitwise_xor(me, jnp.where(i == n - 1, 1, i * 2))
            return jnp.bitwise_xor(me, i * 2 + distances[0])

        def list_source(i, total):
            live = meta_ref[which, shard_of(i), COUNT]
            for g in range(per_source):
                work_ref[total + g] = (i << SHIFT) + g
            return total + lax.shift_right_logical(live + pack - 1, pack.bit_length() - 1)

        total = lax.fori_loop(0, n, list_source, 0)
        for g in range(GROUPS):
            work_ref[total + g] = 0

        def one_step(step, carry):
            for j in range(GROUPS):
                work = work_ref[step * GROUPS + j]
                i, g = lax.shift_right_logical(work, SHIFT), jnp.bitwise_and(work, (1 << SHIFT) - 1)
                shard = shard_of(i)
                rows, cols, limit = [], [], jnp.zeros((1, lanes), jnp.int32)
                for a in range(pack):
                    slot = g * pack + a
                    query, passage = meta_ref[which, shard, QUERY + slot], meta_ref[which, shard, PASSAGE + slot]
                    rows.append(jnp.concatenate([blank] * a + [query_ref[i, query]] + [blank] * (pack - 1 - a), axis=1))
                    cols.append(passages[passage])
                    limit = jnp.where(place == a, meta_ref[which, shard, LENGTH + slot], limit)
                sims = lax.dot_general(
                    jnp.concatenate(cols, axis=1), jnp.concatenate(rows, axis=0),
                    (((1,), (1,)), ((), ())), preferred_element_type=jnp.float32,
                )
                best = jnp.max(jnp.where(token < limit, sims, -1e30), axis=0, keepdims=True)
                best = jnp.where(place + g * pack < meta_ref[which, shard, COUNT], best, 0.0)
                best_ref[g, pl.ds(i * 2 + owner, 1), :] = best
            return carry

        lax.fori_loop(0, lax.shift_right_logical(total + GROUPS - 1, GROUPS.bit_length() - 1), one_step, 0)

    best = jnp.concatenate([best_ref[g] for g in range(per_source)], axis=1)
    high = best.astype(jnp.bfloat16)
    rest = best - high.astype(jnp.float32)
    middle = rest.astype(jnp.bfloat16)
    low = (rest - middle.astype(jnp.float32)).astype(jnp.bfloat16)
    row = lax.broadcasted_iota(jnp.int32, (per_source * lanes, 128), 0)
    col = lax.broadcasted_iota(jnp.int32, (per_source * lanes, 128), 1)
    add = jnp.where(lax.shift_right_logical(row, q_bits) == col, 1.0, 0.0).astype(jnp.bfloat16)
    parts = jnp.dot(jnp.concatenate([high, middle, low], axis=0), add, preferred_element_type=jnp.float32)
    rows = best.shape[0]
    score = (parts[:rows] + parts[rows : 2 * rows] + parts[2 * rows :]) * (1.0 / q_tok)
    if first:
        out_ref[...] = score[:, :cap]
        return
    for scores, at in ((earlier_ref[...], (*range(0, shards, 2), 1)), (score[:, :cap], distances)):
        for i, d in enumerate(at):
            out_ref[pl.ds((shards - 1 - jnp.bitwise_xor(me, d)) * 2, 2), :] = scores[2 * i : 2 * i + 2]


def order_kernel(back_ref, out_ref):
    shards = back_ref.shape[0] // 2
    for i in range(shards):
        out_ref[0, 2 * i : 2 * i + 2] = back_ref[2 * (shards - 1 - i) : 2 * (shards - i)]


def on_device(shards, queries, passages, passage_len, slot_query, slot_passage, slot_count):
    sources, _, cap = slot_query.shape
    q_dev, q_tok, width = queries.shape
    pack = 128 // q_tok
    per_source = -(-cap // pack)
    swap = [(0, 1), (1, 0)]
    vmem, hbm, anywhere = (pl.BlockSpec(memory_space=space) for space in (pltpu.VMEM, pltpu.HBM, pl.ANY))
    params = pltpu.CompilerParams(vmem_limit_bytes=12 * 1024 * 1024)
    row = jax.ShapeDtypeStruct((shards, 128), jnp.int32)

    def placed(space, *arrays):
        return [pltpu.with_memory_space_constraint(x, space) for x in arrays]

    def swapped(piece, d):
        return lax.ppermute(piece, "shard", [(i, i ^ d) for i in range(shards)])

    pieces = [queries] + [None] * (shards - 1)
    for d in reversed(range(2, shards, 2)):
        pieces[d] = swapped(queries, d)
    other_passages = lax.ppermute(passages, "sub", swap)

    mine, theirs, own_passages = pl.pallas_call(
        functools.partial(pack_kernel, shards),
        out_shape=[row, row, jax.ShapeDtypeStruct(passages.shape, passages.dtype)],
        in_specs=[hbm] * 5,
        out_specs=[vmem] * 3,
        scratch_shapes=[
            pltpu.VMEM((sources, cap), jnp.int32),
            pltpu.VMEM((sources, cap), jnp.int32),
            pltpu.VMEM((sources,), jnp.int32),
            pltpu.VMEM(passage_len.shape, jnp.int32),
            pltpu.SemaphoreType.DMA((4,)),
            pltpu.SemaphoreType.DMA((CHUNKS,)),
        ],
        compiler_params=params,
    )(*placed(pltpu.HBM, slot_query.reshape(sources, cap), slot_passage.reshape(sources, cap), slot_count.reshape(sources), passage_len, passages))
    for d in range(1, shards, 2):
        pieces[d] = swapped(pieces[d - 1], 1)
    theirs, _ = lax.optimization_barrier((theirs, pieces[1]))
    other = lax.ppermute(theirs, "sub", swap)

    def scored(distances, *earlier):
        n, first = len(distances), not earlier
        return pl.pallas_call(
            functools.partial(score_kernel, shards, distances, pack, cap, first),
            out_shape=jax.ShapeDtypeStruct((2 * n if first else sources, cap), jnp.float32),
            in_specs=[anywhere] * (2 + n) + [vmem] * (2 + len(earlier)),
            out_specs=vmem,
            scratch_shapes=[
                pltpu.VMEM((n, *queries.shape), queries.dtype),
                pltpu.VMEM((per_source, 2 * n, 128), jnp.float32),
                pltpu.SMEM((2, shards, 128), jnp.int32),
                pltpu.SMEM((n * per_source + 2 * GROUPS,), jnp.int32),
                pltpu.SemaphoreType.DMA((2,)),
                pltpu.SemaphoreType.DMA((n,)),
            ],
            compiler_params=params,
            cost_estimate=pl.CostEstimate(flops=1_000_000_000, bytes_accessed=9_000_000, transcendentals=0),
        )(mine, other, *(pieces[d] for d in reversed(distances)), *placed(pltpu.VMEM, own_passages, other_passages), *earlier)

    pieces[0] = placed(pltpu.HBM, queries)[0]
    scores = scored((*range(0, shards, 2), 1))
    scores = scored(range(3, shards, 2), scores)
    order = [list(reversed(range(shards)))]
    returned = lax.all_to_all(scores, "shard", split_axis=0, concat_axis=0, axis_index_groups=order, tiled=True)
    return pl.pallas_call(
        order_kernel,
        out_shape=jax.ShapeDtypeStruct((1, sources, cap), jnp.float32),
        in_specs=[vmem],
        out_specs=vmem,
        compiler_params=params,
    )(returned)


def solution(mesh):
    return jax.shard_map(
        functools.partial(on_device, mesh.shape["shard"]),
        mesh=mesh,
        in_specs=(
            P(("groups", "shard", "sub"), None, None),
            P(("shard", "sub"), None, None),
            P(("shard", "sub")),
            P("groups", ("shard", "sub"), None),
            P("groups", ("shard", "sub"), None),
            P("groups", ("shard", "sub")),
        ),
        out_specs=P(("groups", "shard", "sub"), None, None),
        check_vma=False,
    )
```

```python
import functools

import jax
import jax.numpy as jnp
from jax import lax
from jax.experimental import pallas as pl
from jax.experimental.pallas import tpu as pltpu
from jax.sharding import PartitionSpec as P

GROUPS = 8
CHUNKS = 8
SHIFT = 8
QUERY, PASSAGE, LENGTH, COUNT = 0, 32, 64, 96


def pack_kernel(
    shards, query_hbm, passage_hbm, count_hbm, length_hbm, own_hbm,
    mine_ref, theirs_ref, own_ref, query_ref, passage_ref, count_ref, length_ref, sems, own_sems,
):
    copies = [
        pltpu.make_async_copy(src, dst, sems.at[i])
        for i, (src, dst) in enumerate(
            ((query_hbm, query_ref), (passage_hbm, passage_ref), (count_hbm, count_ref), (length_hbm, length_ref))
        )
    ]
    size = own_ref.shape[0] // CHUNKS
    own_copies = [
        pltpu.make_async_copy(own_hbm.at[pl.ds(i * size, size)], own_ref.at[pl.ds(i * size, size)], own_sems.at[i])
        for i in range(CHUNKS)
    ]
    for copy in copies + own_copies:
        copy.start()
    for copy in copies:
        copy.wait()
    cap = query_ref.shape[1]
    lengths = length_ref[...].reshape(1, -1)
    counts = jnp.broadcast_to(count_ref[...].reshape(1, -1), (2 * shards, 2 * shards))
    row = lax.broadcasted_iota(jnp.int32, counts.shape, 0)
    col = lax.broadcasted_iota(jnp.int32, counts.shape, 1)
    counts = jnp.sum(jnp.where(row == col, counts, 0), axis=1, keepdims=True)
    blank = jnp.zeros((2 * shards, 32 - cap), jnp.int32)
    passage = jnp.concatenate([passage_ref[...], blank], axis=1)
    passage = jnp.concatenate([passage] * 4, axis=1)
    length = jnp.take_along_axis(jnp.broadcast_to(lengths, passage.shape), passage, axis=1)
    query = jnp.concatenate([jnp.concatenate([query_ref[...], blank], axis=1)] * 4, axis=1)
    lane = lax.broadcasted_iota(jnp.int32, passage.shape, 1)
    packed = jnp.where(lane < PASSAGE, query, jnp.where(lane < LENGTH, passage, jnp.where(lane < COUNT, length, counts)))
    packed = packed.reshape(shards, 2, 128)
    first = lax.axis_index("sub") == 0
    mine_ref[...] = jnp.where(first, packed[:, 0], packed[:, 1])
    theirs_ref[...] = jnp.where(first, packed[:, 1], packed[:, 0])
    for copy in own_copies:
        copy.wait()


def score_kernel(shards, distances, pack, cap, first, *refs):
    n = len(distances)
    meta_hbm, pieces, passage_refs, refs = refs[:2], refs[2 : 2 + n], refs[2 + n : 4 + n], refs[4 + n :]
    earlier_ref = None if first else refs[0]
    out_ref, query_ref, best_ref, meta_ref, work_ref, meta_sems, piece_sems = refs[-7:]
    q_tok, width = query_ref.shape[2:]
    tok_slots = passage_refs[0].shape[1]
    per_source = best_ref.shape[0]
    me, core = lax.axis_index("shard"), lax.axis_index("sub")
    copies = [pltpu.make_async_copy(meta_hbm[i], meta_ref.at[i], meta_sems.at[i]) for i in range(2)]
    copies += [pltpu.make_async_copy(piece, query_ref.at[i], piece_sems.at[i]) for i, piece in enumerate(reversed(pieces))]
    for copy in copies:
        copy.start()
    best_ref[...] = jnp.zeros_like(best_ref)
    token = lax.broadcasted_iota(jnp.int32, (q_tok, tok_slots), 1)
    slot_lane = lax.broadcasted_iota(jnp.int32, best_ref.shape[2:], 1)
    blank = jnp.zeros((q_tok, width), query_ref.dtype)
    for copy in copies:
        copy.wait()

    for which, passages in enumerate(passage_refs):
        owner = core if which == 0 else 1 - core

        def shard_of(i):
            if first:
                return jnp.bitwise_xor(me, jnp.where(i == n - 1, 1, i * 2))
            return jnp.bitwise_xor(me, i * 2 + distances[0])

        def list_source(i, total):
            live = meta_ref[which, shard_of(i), COUNT]
            for g in range(per_source):
                work_ref[total + g] = (i << SHIFT) + g
            return total + lax.shift_right_logical(live + pack - 1, pack.bit_length() - 1)

        total = lax.fori_loop(0, n, list_source, 0)
        for g in range(GROUPS):
            work_ref[total + g] = 0

        def one_step(step, carry):
            for j in range(GROUPS):
                work = work_ref[step * GROUPS + j]
                i, g = lax.shift_right_logical(work, SHIFT), jnp.bitwise_and(work, (1 << SHIFT) - 1)
                shard = shard_of(i)
                best = jnp.zeros(best_ref.shape[2:], jnp.float32)
                for a in range(0, pack, 2):
                    slots = [g * pack + a, g * pack + a + 1]
                    query = [query_ref[i, meta_ref[which, shard, QUERY + slot]] for slot in slots]
                    passage = [passages[meta_ref[which, shard, PASSAGE + slot]] for slot in slots]
                    sims = lax.dot_general(
                        jnp.concatenate(
                            [jnp.concatenate([query[0], blank], axis=1), jnp.concatenate([blank, query[1]], axis=1)], axis=0
                        ),
                        jnp.concatenate(passage, axis=1),
                        (((1,), (1,)), ((), ())), preferred_element_type=jnp.float32,
                    )
                    for half, slot in enumerate(slots):
                        live = token < meta_ref[which, shard, LENGTH + slot]
                        most = jnp.max(jnp.where(live, sims[half * q_tok : (half + 1) * q_tok], -1e30), axis=1, keepdims=True)
                        most = sum(most[r : r + 8] for r in range(0, q_tok, 8))
                        best = jnp.where(slot_lane == slot, most, best)
                best_ref[g, i * 2 + owner] = jnp.where(slot_lane < meta_ref[which, shard, COUNT], best, 0.0)
            return carry

        lax.fori_loop(0, lax.shift_right_logical(total + GROUPS - 1, GROUPS.bit_length() - 1), one_step, 0)

    score = jnp.sum(sum(best_ref[g] for g in range(per_source)), axis=1) * (1.0 / q_tok)
    if first:
        out_ref[...] = score[:, :cap]
        return
    for scores, at in ((earlier_ref[...], (*range(0, shards, 2), 1)), (score[:, :cap], distances)):
        for i, d in enumerate(at):
            out_ref[pl.ds((shards - 1 - jnp.bitwise_xor(me, d)) * 2, 2), :] = scores[2 * i : 2 * i + 2]


def order_kernel(back_ref, out_ref):
    shards = back_ref.shape[0] // 2
    for i in range(shards):
        out_ref[0, 2 * i : 2 * i + 2] = back_ref[2 * (shards - 1 - i) : 2 * (shards - i)]


def on_device(shards, queries, passages, passage_len, slot_query, slot_passage, slot_count):
    sources, _, cap = slot_query.shape
    q_dev, q_tok, width = queries.shape
    pack = 4
    per_source = -(-cap // pack)
    swap = [(0, 1), (1, 0)]
    vmem, hbm, anywhere = (pl.BlockSpec(memory_space=space) for space in (pltpu.VMEM, pltpu.HBM, pl.ANY))
    params = pltpu.CompilerParams(vmem_limit_bytes=12 * 1024 * 1024)
    row = jax.ShapeDtypeStruct((shards, 128), jnp.int32)

    def placed(space, *arrays):
        return [pltpu.with_memory_space_constraint(x, space) for x in arrays]

    def swapped(piece, d):
        return lax.ppermute(piece, "shard", [(i, i ^ d) for i in range(shards)])

    pieces = [queries] + [None] * (shards - 1)
    for d in reversed(range(2, shards, 2)):
        pieces[d] = swapped(queries, d)
    other_passages = lax.ppermute(passages, "sub", swap)

    mine, theirs, own_passages = pl.pallas_call(
        functools.partial(pack_kernel, shards),
        out_shape=[row, row, jax.ShapeDtypeStruct(passages.shape, passages.dtype)],
        in_specs=[hbm] * 5,
        out_specs=[vmem] * 3,
        scratch_shapes=[
            pltpu.VMEM((sources, cap), jnp.int32),
            pltpu.VMEM((sources, cap), jnp.int32),
            pltpu.VMEM((sources,), jnp.int32),
            pltpu.VMEM(passage_len.shape, jnp.int32),
            pltpu.SemaphoreType.DMA((4,)),
            pltpu.SemaphoreType.DMA((CHUNKS,)),
        ],
        compiler_params=params,
    )(*placed(pltpu.HBM, slot_query.reshape(sources, cap), slot_passage.reshape(sources, cap), slot_count.reshape(sources), passage_len, passages))
    for d in range(1, shards, 2):
        pieces[d] = swapped(pieces[d - 1], 1)
    theirs, _ = lax.optimization_barrier((theirs, pieces[1]))
    other = lax.ppermute(theirs, "sub", swap)

    def scored(distances, *earlier):
        n, first = len(distances), not earlier
        return pl.pallas_call(
            functools.partial(score_kernel, shards, distances, pack, cap, first),
            out_shape=jax.ShapeDtypeStruct((2 * n if first else sources, cap), jnp.float32),
            in_specs=[anywhere] * (2 + n) + [vmem] * (2 + len(earlier)),
            out_specs=vmem,
            scratch_shapes=[
                pltpu.VMEM((n, *queries.shape), queries.dtype),
                pltpu.VMEM((per_source, 2 * n, 8, 128), jnp.float32),
                pltpu.SMEM((2, shards, 128), jnp.int32),
                pltpu.SMEM((n * per_source + 2 * GROUPS,), jnp.int32),
                pltpu.SemaphoreType.DMA((2,)),
                pltpu.SemaphoreType.DMA((n,)),
            ],
            compiler_params=params,
            cost_estimate=pl.CostEstimate(flops=1_000_000_000, bytes_accessed=9_000_000, transcendentals=0),
        )(mine, other, *(pieces[d] for d in reversed(distances)), *placed(pltpu.VMEM, own_passages, other_passages), *earlier)

    pieces[0] = placed(pltpu.HBM, queries)[0]
    scores = scored((*range(0, shards, 2), 1))
    scores = scored(range(3, shards, 2), scores)
    order = [list(reversed(range(shards)))]
    returned = lax.all_to_all(scores, "shard", split_axis=0, concat_axis=0, axis_index_groups=order, tiled=True)
    return pl.pallas_call(
        order_kernel,
        out_shape=jax.ShapeDtypeStruct((1, sources, cap), jnp.float32),
        in_specs=[vmem],
        out_specs=vmem,
        compiler_params=params,
    )(returned)


def solution(mesh):
    return jax.shard_map(
        functools.partial(on_device, mesh.shape["shard"]),
        mesh=mesh,
        in_specs=(
            P(("groups", "shard", "sub"), None, None),
            P(("shard", "sub"), None, None),
            P(("shard", "sub")),
            P("groups", ("shard", "sub"), None),
            P("groups", ("shard", "sub"), None),
            P("groups", ("shard", "sub")),
        ),
        out_specs=P(("groups", "shard", "sub"), None, None),
        check_vma=False,
    )
```

```python
import functools

import jax
import jax.numpy as jnp
from jax import lax
from jax.experimental import pallas as pl
from jax.experimental.pallas import tpu as pltpu
from jax.sharding import PartitionSpec as P

GROUPS = 8
CHUNKS = 8
SHIFT = 8
QUERY, PASSAGE, LENGTH, COUNT = 0, 32, 64, 96


def pack_kernel(
    shards, query_hbm, passage_hbm, count_hbm, length_hbm, own_hbm,
    mine_ref, theirs_ref, own_ref, query_ref, passage_ref, count_ref, length_ref, sems, own_sems,
):
    copies = [
        pltpu.make_async_copy(src, dst, sems.at[i])
        for i, (src, dst) in enumerate(
            ((query_hbm, query_ref), (passage_hbm, passage_ref), (count_hbm, count_ref), (length_hbm, length_ref))
        )
    ]
    size = own_ref.shape[0] // CHUNKS
    own_copies = [
        pltpu.make_async_copy(own_hbm.at[pl.ds(i * size, size)], own_ref.at[pl.ds(i * size, size)], own_sems.at[i])
        for i in range(CHUNKS)
    ]
    for copy in copies + own_copies:
        copy.start()
    for copy in copies:
        copy.wait()
    cap = query_ref.shape[1]
    lengths = length_ref[...].reshape(1, -1)
    counts = jnp.broadcast_to(count_ref[...].reshape(1, -1), (2 * shards, 2 * shards))
    row = lax.broadcasted_iota(jnp.int32, counts.shape, 0)
    col = lax.broadcasted_iota(jnp.int32, counts.shape, 1)
    counts = jnp.sum(jnp.where(row == col, counts, 0), axis=1, keepdims=True)
    blank = jnp.zeros((2 * shards, 32 - cap), jnp.int32)
    passage = jnp.concatenate([passage_ref[...], blank], axis=1)
    passage = jnp.concatenate([passage] * 4, axis=1)
    length = jnp.take_along_axis(jnp.broadcast_to(lengths, passage.shape), passage, axis=1)
    query = jnp.concatenate([jnp.concatenate([query_ref[...], blank], axis=1)] * 4, axis=1)
    lane = lax.broadcasted_iota(jnp.int32, passage.shape, 1)
    packed = jnp.where(lane < PASSAGE, query, jnp.where(lane < LENGTH, passage, jnp.where(lane < COUNT, length, counts)))
    packed = packed.reshape(shards, 2, 128)
    first = lax.axis_index("sub") == 0
    mine_ref[...] = jnp.where(first, packed[:, 0], packed[:, 1])
    theirs_ref[...] = jnp.where(first, packed[:, 1], packed[:, 0])
    for copy in own_copies:
        copy.wait()


def score_kernel(shards, distances, pack, cap, first, *refs):
    n = len(distances)
    meta_hbm, pieces, passage_refs, refs = refs[:2], refs[2 : 2 + n], refs[2 + n : 4 + n], refs[4 + n :]
    earlier_ref = None if first else refs[0]
    out_ref, query_ref, best_ref, wide_ref, meta_ref, work_ref, meta_sems, piece_sems = refs[-8:]
    q_tok, width = query_ref.shape[2:]
    tok_slots = passage_refs[0].shape[1]
    per_source = best_ref.shape[0]
    lanes = pack * q_tok
    q_bits = q_tok.bit_length() - 1
    me, core = lax.axis_index("shard"), lax.axis_index("sub")
    copies = [pltpu.make_async_copy(meta_hbm[i], meta_ref.at[i], meta_sems.at[i]) for i in range(2)]
    copies += [pltpu.make_async_copy(piece, query_ref.at[i], piece_sems.at[i]) for i, piece in enumerate(reversed(pieces))]
    for copy in copies:
        copy.start()
    best_ref[...] = jnp.zeros_like(best_ref)
    token = lax.broadcasted_iota(jnp.int32, (tok_slots, lanes), 0)
    place = lax.shift_right_logical(lax.broadcasted_iota(jnp.int32, (1, lanes), 1), q_bits)
    blank = jnp.zeros((q_tok, width), query_ref.dtype)
    for copy in copies:
        copy.wait()

    for which, passages in enumerate(passage_refs):
        owner = core if which == 0 else 1 - core

        def shard_of(i):
            if first:
                return jnp.bitwise_xor(me, jnp.where(i == n - 1, 1, i * 2))
            return jnp.bitwise_xor(me, i * 2 + distances[0])

        def list_source(i, total):
            live = meta_ref[which, shard_of(i), COUNT]
            for g in range(per_source):
                work_ref[total + g] = (i << SHIFT) + g
            return total + lax.shift_right_logical(live + pack - 1, pack.bit_length() - 1)

        total = lax.fori_loop(0, n, list_source, 0)
        for g in range(GROUPS):
            work_ref[total + g] = 0

        def one_step(step, carry):
            for j in range(GROUPS):
                work = work_ref[step * GROUPS + j]
                i, g = lax.shift_right_logical(work, SHIFT), jnp.bitwise_and(work, (1 << SHIFT) - 1)
                shard = shard_of(i)
                rows, cols, limit = [], [], jnp.zeros((1, lanes), jnp.int32)
                for a in range(pack):
                    slot = g * pack + a
                    query, passage = meta_ref[which, shard, QUERY + slot], meta_ref[which, shard, PASSAGE + slot]
                    rows.append(jnp.concatenate([blank] * a + [query_ref[i, query]] + [blank] * (pack - 1 - a), axis=1))
                    cols.append(passages[passage])
                    limit = jnp.where(place == a, meta_ref[which, shard, LENGTH + slot], limit)
                sims = lax.dot_general(
                    jnp.concatenate(cols, axis=1), jnp.concatenate(rows, axis=0),
                    (((1,), (1,)), ((), ())), preferred_element_type=jnp.float32,
                )
                best = jnp.max(jnp.where(token < limit, sims, -1e30), axis=0, keepdims=True)
                best = jnp.where(place + g * pack < meta_ref[which, shard, COUNT], best, 0.0)
                best_ref[g, pl.ds(i * 2 + owner, 1), :] = best
            return carry

        lax.fori_loop(0, lax.shift_right_logical(total + GROUPS - 1, GROUPS.bit_length() - 1), one_step, 0)

    best = jnp.concatenate([best_ref[g] for g in range(per_source)], axis=1)
    high = best.astype(jnp.bfloat16)
    rest = best - high.astype(jnp.float32)
    middle = rest.astype(jnp.bfloat16)
    low = (rest - middle.astype(jnp.float32)).astype(jnp.bfloat16)
    row = lax.broadcasted_iota(jnp.int32, (per_source * lanes, 128), 0)
    col = lax.broadcasted_iota(jnp.int32, (per_source * lanes, 128), 1)
    add = jnp.where(lax.shift_right_logical(row, q_bits) == col, 1.0, 0.0).astype(jnp.bfloat16)
    parts = jnp.dot(jnp.concatenate([high, middle, low], axis=0), add, preferred_element_type=jnp.float32)
    rows = best.shape[0]
    score = (parts[:rows] + parts[rows : 2 * rows] + parts[2 * rows :]) * (1.0 / q_tok)
    if first:
        out_ref[...] = score[:, :cap]
        return
    parts = ((earlier_ref[...], (*range(0, shards, 2), 1)), (score[:, :cap], distances))
    if out_ref.shape[0] == cap:
        wide_ref[...] = jnp.zeros_like(wide_ref)
        for scores, at in parts:
            for i, d in enumerate(at):
                wide_ref[pl.ds((jnp.bitwise_xor(me, d) * shards + me) * 2, 2), :cap] = scores[2 * i : 2 * i + 2]
        out_ref[...] = wide_ref[...].T[:cap]
        return
    for scores, at in parts:
        for i, d in enumerate(at):
            out_ref[pl.ds((shards - 1 - jnp.bitwise_xor(me, d)) * 2, 2), :] = scores[2 * i : 2 * i + 2]


def pick_kernel(sum_ref, out_ref, wide_ref):
    sources = out_ref.shape[1]
    wide_ref[...] = jnp.zeros_like(wide_ref)
    wide_ref[: sum_ref.shape[0], :] = sum_ref[...]
    wide_ref[...] = wide_ref[...].T
    start = pl.multiple_of(lax.axis_index("shard") * sources, 8)
    out_ref[0] = wide_ref[pl.ds(start, sources), : out_ref.shape[2]]


def order_kernel(back_ref, out_ref):
    shards = back_ref.shape[0] // 2
    for i in range(shards):
        out_ref[0, 2 * i : 2 * i + 2] = back_ref[2 * (shards - 1 - i) : 2 * (shards - i)]


def on_device(shards, queries, passages, passage_len, slot_query, slot_passage, slot_count):
    sources, _, cap = slot_query.shape
    q_dev, q_tok, width = queries.shape
    pack = 128 // q_tok
    per_source = -(-cap // pack)
    swap = [(0, 1), (1, 0)]
    vmem, hbm, anywhere = (pl.BlockSpec(memory_space=space) for space in (pltpu.VMEM, pltpu.HBM, pl.ANY))
    params = pltpu.CompilerParams(vmem_limit_bytes=12 * 1024 * 1024)
    row = jax.ShapeDtypeStruct((shards, 128), jnp.int32)

    def placed(space, *arrays):
        return [pltpu.with_memory_space_constraint(x, space) for x in arrays]

    def swapped(piece, d):
        return lax.ppermute(piece, "shard", [(i, i ^ d) for i in range(shards)])

    pieces = [queries] + [None] * (shards - 1)
    for d in reversed(range(2, shards, 2)):
        pieces[d] = swapped(queries, d)
    other_passages = lax.ppermute(passages, "sub", swap)

    mine, theirs, own_passages = pl.pallas_call(
        functools.partial(pack_kernel, shards),
        out_shape=[row, row, jax.ShapeDtypeStruct(passages.shape, passages.dtype)],
        in_specs=[hbm] * 5,
        out_specs=[vmem] * 3,
        scratch_shapes=[
            pltpu.VMEM((sources, cap), jnp.int32),
            pltpu.VMEM((sources, cap), jnp.int32),
            pltpu.VMEM((sources,), jnp.int32),
            pltpu.VMEM(passage_len.shape, jnp.int32),
            pltpu.SemaphoreType.DMA((4,)),
            pltpu.SemaphoreType.DMA((CHUNKS,)),
        ],
        compiler_params=params,
    )(*placed(pltpu.HBM, slot_query.reshape(sources, cap), slot_passage.reshape(sources, cap), slot_count.reshape(sources), passage_len, passages))
    for d in range(1, shards, 2):
        pieces[d] = swapped(pieces[d - 1], 1)
    theirs, _ = lax.optimization_barrier((theirs, pieces[1]))
    other = lax.ppermute(theirs, "sub", swap)

    summed = shards * sources == 128
    returns = (cap, 128) if summed else (sources, cap)

    def scored(distances, *earlier):
        n, first = len(distances), not earlier
        return pl.pallas_call(
            functools.partial(score_kernel, shards, distances, pack, cap, first),
            out_shape=jax.ShapeDtypeStruct((2 * n, cap) if first else returns, jnp.float32),
            in_specs=[anywhere] * (2 + n) + [vmem] * (2 + len(earlier)),
            out_specs=vmem,
            scratch_shapes=[
                pltpu.VMEM((n, *queries.shape), queries.dtype),
                pltpu.VMEM((per_source, 2 * n, 128), jnp.float32),
                pltpu.VMEM((128, 128), jnp.float32),
                pltpu.SMEM((2, shards, 128), jnp.int32),
                pltpu.SMEM((n * per_source + 2 * GROUPS,), jnp.int32),
                pltpu.SemaphoreType.DMA((2,)),
                pltpu.SemaphoreType.DMA((n,)),
            ],
            compiler_params=params,
            cost_estimate=pl.CostEstimate(flops=1_000_000_000, bytes_accessed=9_000_000, transcendentals=0),
        )(mine, other, *(pieces[d] for d in reversed(distances)), *placed(pltpu.VMEM, own_passages, other_passages), *earlier)

    pieces[0] = placed(pltpu.HBM, queries)[0]
    scores = scored((*range(0, shards, 2), 1))
    scores = scored(range(3, shards, 2), scores)
    if summed:
        returned = lax.psum(scores, "shard")
    else:
        order = [list(reversed(range(shards)))]
        returned = lax.all_to_all(scores, "shard", split_axis=0, concat_axis=0, axis_index_groups=order, tiled=True)
    return pl.pallas_call(
        pick_kernel if summed else order_kernel,
        out_shape=jax.ShapeDtypeStruct((1, sources, cap), jnp.float32),
        in_specs=[vmem],
        out_specs=vmem,
        scratch_shapes=[pltpu.VMEM((128, 128), jnp.float32)] * summed,
        compiler_params=params,
    )(returned)


def solution(mesh):
    return jax.shard_map(
        functools.partial(on_device, mesh.shape["shard"]),
        mesh=mesh,
        in_specs=(
            P(("groups", "shard", "sub"), None, None),
            P(("shard", "sub"), None, None),
            P(("shard", "sub")),
            P("groups", ("shard", "sub"), None),
            P("groups", ("shard", "sub"), None),
            P("groups", ("shard", "sub")),
        ),
        out_specs=P(("groups", "shard", "sub"), None, None),
        check_vma=False,
    )
```

```python
import functools

import jax
import jax.numpy as jnp
from jax import lax
from jax.experimental import pallas as pl
from jax.experimental.pallas import tpu as pltpu
from jax.sharding import PartitionSpec as P

GROUPS = 8
CHUNKS = 8
SHIFT = 8
QUERY, PASSAGE, LENGTH, COUNT = 0, 32, 64, 96


def pack_kernel(
    shards, query_hbm, passage_hbm, count_hbm, length_hbm, tokens_hbm, own_hbm,
    mine_ref, theirs_ref, tokens_ref, own_ref, query_ref, passage_ref, count_ref, length_ref, sems, own_sems,
):
    copies = [
        pltpu.make_async_copy(src, dst, sems.at[i])
        for i, (src, dst) in enumerate(
            (
                (query_hbm, query_ref),
                (passage_hbm, passage_ref),
                (count_hbm, count_ref),
                (length_hbm, length_ref),
                (tokens_hbm, tokens_ref),
            )
        )
    ]
    size = own_ref.shape[0] // CHUNKS
    own_copies = [
        pltpu.make_async_copy(own_hbm.at[pl.ds(i * size, size)], own_ref.at[pl.ds(i * size, size)], own_sems.at[i])
        for i in range(CHUNKS)
    ]
    for copy in copies + own_copies:
        copy.start()
    for copy in copies:
        copy.wait()
    cap = query_ref.shape[1]
    lengths = length_ref[...].reshape(1, -1)
    counts = jnp.broadcast_to(count_ref[...].reshape(1, -1), (2 * shards, 2 * shards))
    row = lax.broadcasted_iota(jnp.int32, counts.shape, 0)
    col = lax.broadcasted_iota(jnp.int32, counts.shape, 1)
    counts = jnp.sum(jnp.where(row == col, counts, 0), axis=1, keepdims=True)
    blank = jnp.zeros((2 * shards, 32 - cap), jnp.int32)
    passage = jnp.concatenate([passage_ref[...], blank], axis=1)
    passage = jnp.concatenate([passage] * 4, axis=1)
    length = jnp.take_along_axis(jnp.broadcast_to(lengths, passage.shape), passage, axis=1)
    query = jnp.concatenate([jnp.concatenate([query_ref[...], blank], axis=1)] * 4, axis=1)
    lane = lax.broadcasted_iota(jnp.int32, passage.shape, 1)
    packed = jnp.where(lane < PASSAGE, query, jnp.where(lane < LENGTH, passage, jnp.where(lane < COUNT, length, counts)))
    packed = packed.reshape(shards, 2, 128)
    first = lax.axis_index("sub") == 0
    mine_ref[...] = jnp.where(first, packed[:, 0], packed[:, 1])
    theirs_ref[...] = jnp.where(first, packed[:, 1], packed[:, 0])
    for copy in own_copies:
        copy.wait()


def score_kernel(shards, distances, pack, cap, first, *refs):
    n = len(distances)
    p = n if first else n - 1
    meta_hbm, pieces, passage_refs, refs = refs[:2], refs[2 : 2 + p], refs[2 + p : 4 + p], refs[4 + p :]
    earlier_ref = None if first else refs[0]
    out_ref, query_ref, best_ref, meta_ref, work_ref, meta_sems, piece_sems = refs[-7:]
    q_tok, width = query_ref.shape[2:]
    tok_slots = passage_refs[0].shape[1]
    per_source = best_ref.shape[0]
    lanes = pack * q_tok
    q_bits = q_tok.bit_length() - 1
    me, core = lax.axis_index("shard"), lax.axis_index("sub")
    copies = [pltpu.make_async_copy(meta_hbm[i], meta_ref.at[i], meta_sems.at[i]) for i in range(2)]
    for i, piece in enumerate(reversed(pieces)):
        at = query_ref.at[i] if first else query_ref.at[pl.ds(0, 2)] if i == 0 else query_ref.at[i + 1]
        copies.append(pltpu.make_async_copy(piece, at, piece_sems.at[i]))
    for copy in copies:
        copy.start()
    best_ref[...] = jnp.zeros_like(best_ref)
    token = lax.broadcasted_iota(jnp.int32, (tok_slots, 2 * q_tok), 0)
    left = lax.broadcasted_iota(jnp.int32, (1, 2 * q_tok), 1) < q_tok
    place = lax.shift_right_logical(lax.broadcasted_iota(jnp.int32, (1, lanes), 1), q_bits)
    blank = jnp.zeros((q_tok, width), query_ref.dtype)
    for copy in copies:
        copy.wait()

    for which, passages in enumerate(passage_refs):
        owner = core if which == 0 else 1 - core

        def shard_of(i):
            if first:
                return jnp.bitwise_xor(me, jnp.where(i == 1, 1, i * 2))
            return jnp.bitwise_xor(me, jnp.where(i == 0, 2, i * 2 + 1))

        def list_source(i, total):
            live = meta_ref[which, shard_of(i), COUNT]
            for g in range(per_source):
                work_ref[total + g] = (i << SHIFT) + g
            return total + lax.shift_right_logical(live + pack - 1, pack.bit_length() - 1)

        total = lax.fori_loop(0, n, list_source, 0)
        for g in range(GROUPS):
            work_ref[total + g] = 0

        def one_step(step, carry):
            for j in range(GROUPS):
                work = work_ref[step * GROUPS + j]
                i, g = lax.shift_right_logical(work, SHIFT), jnp.bitwise_and(work, (1 << SHIFT) - 1)
                shard = shard_of(i)
                best = []
                for a in range(0, pack, 2):
                    slots = [g * pack + a, g * pack + a + 1]
                    if cap % pack:
                        slots = [jnp.minimum(slot, cap - 1) for slot in slots]
                    query = [query_ref[i, meta_ref[which, shard, QUERY + slot]] for slot in slots]
                    passage = [meta_ref[which, shard, PASSAGE + slot] for slot in slots]
                    limit = [meta_ref[which, shard, LENGTH + slot] for slot in slots]
                    sims = lax.dot_general(
                        jnp.concatenate([passages[p] for p in passage], axis=1),
                        jnp.concatenate(
                            [jnp.concatenate([query[0], blank], axis=1), jnp.concatenate([blank, query[1]], axis=1)], axis=0
                        ),
                        (((1,), (1,)), ((), ())), preferred_element_type=jnp.float32,
                    )
                    live = token < jnp.where(left, limit[0], limit[1])
                    best.append(jnp.max(jnp.where(live, sims, -1e30), axis=0, keepdims=True))
                best = jnp.concatenate(best, axis=1)
                best = jnp.where(place + g * pack < meta_ref[which, shard, COUNT], best, 0.0)
                best_ref[g, pl.ds(i * 2 + owner, 1), :] = best
            return carry

        lax.fori_loop(0, lax.shift_right_logical(total + GROUPS - 1, GROUPS.bit_length() - 1), one_step, 0)

    best = jnp.concatenate([best_ref[g] for g in range(per_source)], axis=1)
    high = best.astype(jnp.bfloat16)
    rest = best - high.astype(jnp.float32)
    middle = rest.astype(jnp.bfloat16)
    low = (rest - middle.astype(jnp.float32)).astype(jnp.bfloat16)
    row = lax.broadcasted_iota(jnp.int32, (per_source * lanes, 128), 0)
    col = lax.broadcasted_iota(jnp.int32, (per_source * lanes, 128), 1)
    add = jnp.where(lax.shift_right_logical(row, q_bits) == col, 1.0, 0.0).astype(jnp.bfloat16)
    parts = jnp.dot(jnp.concatenate([high, middle, low], axis=0), add, preferred_element_type=jnp.float32)
    rows = best.shape[0]
    score = (parts[:rows] + parts[rows : 2 * rows] + parts[2 * rows :]) * (1.0 / q_tok)
    if first:
        out_ref[...] = score[:, :cap]
        return
    for scores, at in ((earlier_ref[...], (0, 1, *range(4, shards, 2))), (score[:, :cap], distances)):
        for i, d in enumerate(at):
            out_ref[pl.ds((shards - 1 - jnp.bitwise_xor(me, d)) * 2, 2), :] = scores[2 * i : 2 * i + 2]


def pair_kernel(one_ref, other_ref, out_ref):
    out_ref[0] = one_ref[...]
    out_ref[1] = other_ref[...]


def order_kernel(back_ref, out_ref):
    shards = back_ref.shape[0] // 2
    for i in range(shards):
        out_ref[0, 2 * i : 2 * i + 2] = back_ref[2 * (shards - 1 - i) : 2 * (shards - i)]


def on_device(shards, queries, passages, passage_len, slot_query, slot_passage, slot_count):
    sources, _, cap = slot_query.shape
    q_dev, q_tok, width = queries.shape
    pack = 128 // q_tok
    per_source = -(-cap // pack)
    swap = [(0, 1), (1, 0)]
    vmem, hbm, anywhere = (pl.BlockSpec(memory_space=space) for space in (pltpu.VMEM, pltpu.HBM, pl.ANY))
    params = pltpu.CompilerParams(vmem_limit_bytes=12 * 1024 * 1024)
    row = jax.ShapeDtypeStruct((shards, 128), jnp.int32)

    def placed(space, *arrays):
        return [pltpu.with_memory_space_constraint(x, space) for x in arrays]

    def swapped(piece, d):
        return lax.ppermute(piece, "shard", [(i, i ^ d) for i in range(shards)])

    pieces = [queries, swapped(queries, 1)] + [None] * (shards - 2)
    for d in range(4, shards, 2):
        pieces[d] = swapped(queries, d)
    other_passages = lax.ppermute(passages, "sub", swap)

    mine, theirs, own_queries, own_passages = pl.pallas_call(
        functools.partial(pack_kernel, shards),
        out_shape=[row, row, *(jax.ShapeDtypeStruct(x.shape, x.dtype) for x in (queries, passages))],
        in_specs=[hbm] * 6,
        out_specs=[vmem] * 4,
        scratch_shapes=[
            pltpu.VMEM((sources, cap), jnp.int32),
            pltpu.VMEM((sources, cap), jnp.int32),
            pltpu.VMEM((sources,), jnp.int32),
            pltpu.VMEM(passage_len.shape, jnp.int32),
            pltpu.SemaphoreType.DMA((5,)),
            pltpu.SemaphoreType.DMA((CHUNKS,)),
        ],
        compiler_params=params,
    )(*placed(pltpu.HBM, slot_query.reshape(sources, cap), slot_passage.reshape(sources, cap), slot_count.reshape(sources), passage_len, queries, passages))
    both = pl.pallas_call(
        pair_kernel,
        out_shape=jax.ShapeDtypeStruct((2, *queries.shape), queries.dtype),
        in_specs=[vmem] * 2,
        out_specs=vmem,
        compiler_params=params,
    )(own_queries, pieces[1])
    both = swapped(both, 2)
    for d in range(5, shards, 2):
        pieces[d] = swapped(pieces[d - 1], 1) if d == shards - 1 else swapped(pieces[1], d - 1)
    theirs, _ = lax.optimization_barrier((theirs, pieces[1]))
    other = lax.ppermute(theirs, "sub", swap)

    def scored(distances, *earlier):
        n, first = len(distances), not earlier
        parts = [pieces[d] for d in reversed(distances)] if first else [*(pieces[d] for d in reversed(distances[2:])), both]
        return pl.pallas_call(
            functools.partial(score_kernel, shards, distances, pack, cap, first),
            out_shape=jax.ShapeDtypeStruct((2 * n if first else sources, cap), jnp.float32),
            in_specs=[anywhere] * (2 + len(parts)) + [vmem] * (2 + len(earlier)),
            out_specs=vmem,
            scratch_shapes=[
                pltpu.VMEM((n, *queries.shape), queries.dtype),
                pltpu.VMEM((per_source, 2 * n, 128), jnp.float32),
                pltpu.SMEM((2, shards, 128), jnp.int32),
                pltpu.SMEM((n * per_source + 2 * GROUPS,), jnp.int32),
                pltpu.SemaphoreType.DMA((2,)),
                pltpu.SemaphoreType.DMA((n,)),
            ],
            compiler_params=params,
            cost_estimate=pl.CostEstimate(flops=1_000_000_000, bytes_accessed=9_000_000, transcendentals=0),
        )(mine, other, *parts, *placed(pltpu.VMEM, own_passages, other_passages), *earlier)

    pieces[0] = own_queries
    scores = scored((0, 1, *range(4, shards, 2)))
    scores = scored((2, *range(3, shards, 2)), scores)
    order = [list(reversed(range(shards)))]
    returned = lax.all_to_all(scores, "shard", split_axis=0, concat_axis=0, axis_index_groups=order, tiled=True)
    return pl.pallas_call(
        order_kernel,
        out_shape=jax.ShapeDtypeStruct((1, sources, cap), jnp.float32),
        in_specs=[vmem],
        out_specs=vmem,
        compiler_params=params,
    )(returned)


def solution(mesh):
    return jax.shard_map(
        functools.partial(on_device, mesh.shape["shard"]),
        mesh=mesh,
        in_specs=(
            P(("groups", "shard", "sub"), None, None),
            P(("shard", "sub"), None, None),
            P(("shard", "sub")),
            P("groups", ("shard", "sub"), None),
            P("groups", ("shard", "sub"), None),
            P("groups", ("shard", "sub")),
        ),
        out_specs=P(("groups", "shard", "sub"), None, None),
        check_vma=False,
    )
```

```python
import functools

import jax
import jax.numpy as jnp
from jax import lax
from jax.experimental import pallas as pl
from jax.experimental.pallas import tpu as pltpu
from jax.sharding import PartitionSpec as P

GROUPS = 4
CHUNKS = 8
SHIFT = 8
QUERY, PASSAGE, LENGTH, COUNT = 0, 32, 64, 96


def pack_kernel(
    shards, query_hbm, passage_hbm, count_hbm, length_hbm, tokens_hbm, own_hbm,
    mine_ref, theirs_ref, tokens_ref, own_ref, query_ref, passage_ref, count_ref, length_ref, sems, own_sems,
):
    copies = [
        pltpu.make_async_copy(src, dst, sems.at[i])
        for i, (src, dst) in enumerate(
            (
                (query_hbm, query_ref),
                (passage_hbm, passage_ref),
                (count_hbm, count_ref),
                (length_hbm, length_ref),
                (tokens_hbm, tokens_ref),
            )
        )
    ]
    size = own_ref.shape[0] // CHUNKS
    own_copies = [
        pltpu.make_async_copy(own_hbm.at[pl.ds(i * size, size)], own_ref.at[pl.ds(i * size, size)], own_sems.at[i])
        for i in range(CHUNKS)
    ]
    for copy in copies + own_copies:
        copy.start()
    for copy in copies:
        copy.wait()
    cap = query_ref.shape[1]
    lengths = length_ref[...].reshape(1, -1)
    counts = jnp.broadcast_to(count_ref[...].reshape(1, -1), (2 * shards, 2 * shards))
    row = lax.broadcasted_iota(jnp.int32, counts.shape, 0)
    col = lax.broadcasted_iota(jnp.int32, counts.shape, 1)
    counts = jnp.sum(jnp.where(row == col, counts, 0), axis=1, keepdims=True)
    blank = jnp.zeros((2 * shards, 32 - cap), jnp.int32)
    passage = jnp.concatenate([passage_ref[...], blank], axis=1)
    passage = jnp.concatenate([passage] * 4, axis=1)
    length = jnp.take_along_axis(jnp.broadcast_to(lengths, passage.shape), passage, axis=1)
    query = jnp.concatenate([jnp.concatenate([query_ref[...], blank], axis=1)] * 4, axis=1)
    lane = lax.broadcasted_iota(jnp.int32, passage.shape, 1)
    packed = jnp.where(lane < PASSAGE, query, jnp.where(lane < LENGTH, passage, jnp.where(lane < COUNT, length, counts)))
    packed = packed.reshape(shards, 2, 128)
    first = lax.axis_index("sub") == 0
    mine_ref[...] = jnp.where(first, packed[:, 0], packed[:, 1])
    theirs_ref[...] = jnp.where(first, packed[:, 1], packed[:, 0])
    for copy in own_copies:
        copy.wait()


def score_kernel(shards, distances, pack, cap, first, *refs):
    n = len(distances)
    p = n if first else n - 1
    meta_hbm, pieces, passage_refs, refs = refs[:2], refs[2 : 2 + p], refs[2 + p : 4 + p], refs[4 + p :]
    earlier_ref = None if first else refs[0]
    out_ref, query_ref, best_ref, meta_ref, work_ref, meta_sems, piece_sems = refs[-7:]
    q_tok, width = query_ref.shape[2:]
    tok_slots = passage_refs[0].shape[1]
    per_source = best_ref.shape[0]
    lanes = pack * q_tok
    q_bits = q_tok.bit_length() - 1
    me, core = lax.axis_index("shard"), lax.axis_index("sub")
    copies = [pltpu.make_async_copy(meta_hbm[i], meta_ref.at[i], meta_sems.at[i]) for i in range(2)]
    for i, piece in enumerate(reversed(pieces)):
        at = query_ref.at[i] if first else query_ref.at[pl.ds(0, 2)] if i == 0 else query_ref.at[i + 1]
        copies.append(pltpu.make_async_copy(piece, at, piece_sems.at[i]))
    for copy in copies:
        copy.start()
    best_ref[...] = jnp.zeros_like(best_ref)
    token = lax.broadcasted_iota(jnp.int32, (tok_slots, lanes), 0)
    place = lax.shift_right_logical(lax.broadcasted_iota(jnp.int32, (1, lanes), 1), q_bits)
    blank = jnp.zeros((q_tok, width), query_ref.dtype)
    for copy in copies:
        copy.wait()

    for which, passages in enumerate(passage_refs):
        owner = core if which == 0 else 1 - core

        def shard_of(i):
            if first:
                return jnp.bitwise_xor(me, jnp.where(i == 1, 1, i * 2))
            return jnp.bitwise_xor(me, jnp.where(i == 0, 2, i * 2 + 1))

        def list_source(i, total):
            live = meta_ref[which, shard_of(i), COUNT]
            for g in range(per_source):
                work_ref[total + g] = (i << SHIFT) + g
            return total + lax.shift_right_logical(live + pack - 1, pack.bit_length() - 1)

        total = lax.fori_loop(0, n, list_source, 0)
        for g in range(GROUPS):
            work_ref[total + g] = 0

        def one_step(step, carry):
            for j in range(GROUPS):
                work = work_ref[step * GROUPS + j]
                i, g = lax.shift_right_logical(work, SHIFT), jnp.bitwise_and(work, (1 << SHIFT) - 1)
                shard = shard_of(i)
                rows, cols, limit = [], [], jnp.zeros((1, lanes), jnp.int32)
                for a in range(pack):
                    slot = g * pack + a
                    query, passage = meta_ref[which, shard, QUERY + slot], meta_ref[which, shard, PASSAGE + slot]
                    rows.append(jnp.concatenate([blank] * a + [query_ref[i, query]] + [blank] * (pack - 1 - a), axis=1))
                    cols.append(passages[passage])
                    limit = jnp.where(place == a, meta_ref[which, shard, LENGTH + slot], limit)
                sims = lax.dot_general(
                    jnp.concatenate(cols, axis=1), jnp.concatenate(rows, axis=0),
                    (((1,), (1,)), ((), ())), preferred_element_type=jnp.float32,
                )
                best = jnp.max(jnp.where(token < limit, sims, -1e30), axis=0, keepdims=True)
                best = jnp.where(place + g * pack < meta_ref[which, shard, COUNT], best, 0.0)
                best_ref[g, pl.ds(i * 2 + owner, 1), :] = best
            return carry

        lax.fori_loop(0, lax.shift_right_logical(total + GROUPS - 1, GROUPS.bit_length() - 1), one_step, 0)

    best = jnp.concatenate([best_ref[g] for g in range(per_source)], axis=1)
    high = best.astype(jnp.bfloat16)
    rest = best - high.astype(jnp.float32)
    middle = rest.astype(jnp.bfloat16)
    low = (rest - middle.astype(jnp.float32)).astype(jnp.bfloat16)
    row = lax.broadcasted_iota(jnp.int32, (per_source * lanes, 128), 0)
    col = lax.broadcasted_iota(jnp.int32, (per_source * lanes, 128), 1)
    add = jnp.where(lax.shift_right_logical(row, q_bits) == col, 1.0, 0.0).astype(jnp.bfloat16)
    parts = jnp.dot(jnp.concatenate([high, middle, low], axis=0), add, preferred_element_type=jnp.float32)
    rows = best.shape[0]
    score = (parts[:rows] + parts[rows : 2 * rows] + parts[2 * rows :]) * (1.0 / q_tok)
    if first:
        out_ref[...] = score[:, :cap]
        return
    for scores, at in ((earlier_ref[...], (0, 1, *range(4, shards, 2))), (score[:, :cap], distances)):
        for i, d in enumerate(at):
            out_ref[pl.ds((shards - 1 - jnp.bitwise_xor(me, d)) * 2, 2), :] = scores[2 * i : 2 * i + 2]


def pair_kernel(one_ref, other_ref, out_ref):
    out_ref[0] = one_ref[...]
    out_ref[1] = other_ref[...]


def order_kernel(back_ref, out_ref):
    shards = back_ref.shape[0] // 2
    for i in range(shards):
        out_ref[0, 2 * i : 2 * i + 2] = back_ref[2 * (shards - 1 - i) : 2 * (shards - i)]


def on_device(shards, queries, passages, passage_len, slot_query, slot_passage, slot_count):
    sources, _, cap = slot_query.shape
    q_dev, q_tok, width = queries.shape
    pack = 128 // q_tok
    per_source = -(-cap // pack)
    swap = [(0, 1), (1, 0)]
    vmem, hbm, anywhere = (pl.BlockSpec(memory_space=space) for space in (pltpu.VMEM, pltpu.HBM, pl.ANY))
    params = pltpu.CompilerParams(vmem_limit_bytes=12 * 1024 * 1024)
    row = jax.ShapeDtypeStruct((shards, 128), jnp.int32)

    def placed(space, *arrays):
        return [pltpu.with_memory_space_constraint(x, space) for x in arrays]

    def swapped(piece, d):
        return lax.ppermute(piece, "shard", [(i, i ^ d) for i in range(shards)])

    pieces = [queries, swapped(queries, 1)] + [None] * (shards - 2)
    for d in range(4, shards, 2):
        pieces[d] = swapped(queries, d)
    other_passages = lax.ppermute(passages, "sub", swap)

    mine, theirs, own_queries, own_passages = pl.pallas_call(
        functools.partial(pack_kernel, shards),
        out_shape=[row, row, *(jax.ShapeDtypeStruct(x.shape, x.dtype) for x in (queries, passages))],
        in_specs=[hbm] * 6,
        out_specs=[vmem] * 4,
        scratch_shapes=[
            pltpu.VMEM((sources, cap), jnp.int32),
            pltpu.VMEM((sources, cap), jnp.int32),
            pltpu.VMEM((sources,), jnp.int32),
            pltpu.VMEM(passage_len.shape, jnp.int32),
            pltpu.SemaphoreType.DMA((5,)),
            pltpu.SemaphoreType.DMA((CHUNKS,)),
        ],
        compiler_params=params,
    )(*placed(pltpu.HBM, slot_query.reshape(sources, cap), slot_passage.reshape(sources, cap), slot_count.reshape(sources), passage_len, queries, passages))
    both = pl.pallas_call(
        pair_kernel,
        out_shape=jax.ShapeDtypeStruct((2, *queries.shape), queries.dtype),
        in_specs=[vmem] * 2,
        out_specs=vmem,
        compiler_params=params,
    )(own_queries, pieces[1])
    both = swapped(both, 2)
    for d in range(5, shards, 2):
        pieces[d] = swapped(pieces[d - 1], 1)
    theirs, _ = lax.optimization_barrier((theirs, pieces[1]))
    other = lax.ppermute(theirs, "sub", swap)

    def scored(distances, *earlier):
        n, first = len(distances), not earlier
        parts = [pieces[d] for d in reversed(distances)] if first else [*(pieces[d] for d in reversed(distances[2:])), both]
        return pl.pallas_call(
            functools.partial(score_kernel, shards, distances, pack, cap, first),
            out_shape=jax.ShapeDtypeStruct((2 * n if first else sources, cap), jnp.float32),
            in_specs=[anywhere] * (2 + len(parts)) + [vmem] * (2 + len(earlier)),
            out_specs=vmem,
            scratch_shapes=[
                pltpu.VMEM((n, *queries.shape), queries.dtype),
                pltpu.VMEM((per_source, 2 * n, 128), jnp.float32),
                pltpu.SMEM((2, shards, 128), jnp.int32),
                pltpu.SMEM((n * per_source + 2 * GROUPS,), jnp.int32),
                pltpu.SemaphoreType.DMA((2,)),
                pltpu.SemaphoreType.DMA((n,)),
            ],
            compiler_params=params,
            cost_estimate=pl.CostEstimate(flops=1_000_000_000, bytes_accessed=9_000_000, transcendentals=0),
        )(mine, other, *parts, *placed(pltpu.VMEM, own_passages, other_passages), *earlier)

    pieces[0] = own_queries
    scores = scored((0, 1, *range(4, shards, 2)))
    scores = scored((2, *range(3, shards, 2)), scores)
    order = [list(reversed(range(shards)))]
    returned = lax.all_to_all(scores, "shard", split_axis=0, concat_axis=0, axis_index_groups=order, tiled=True)
    return pl.pallas_call(
        order_kernel,
        out_shape=jax.ShapeDtypeStruct((1, sources, cap), jnp.float32),
        in_specs=[vmem],
        out_specs=vmem,
        compiler_params=params,
    )(returned)


def solution(mesh):
    return jax.shard_map(
        functools.partial(on_device, mesh.shape["shard"]),
        mesh=mesh,
        in_specs=(
            P(("groups", "shard", "sub"), None, None),
            P(("shard", "sub"), None, None),
            P(("shard", "sub")),
            P("groups", ("shard", "sub"), None),
            P("groups", ("shard", "sub"), None),
            P("groups", ("shard", "sub")),
        ),
        out_specs=P(("groups", "shard", "sub"), None, None),
        check_vma=False,
    )
```

```python
import functools

import jax
import jax.numpy as jnp
from jax import lax
from jax.experimental import pallas as pl
from jax.experimental.pallas import tpu as pltpu
from jax.sharding import PartitionSpec as P

GROUPS = 8
CHUNKS = 8
SHIFT = 8
QUERY, PASSAGE, LENGTH, COUNT = 0, 32, 64, 96


def pack_kernel(
    shards, query_hbm, passage_hbm, count_hbm, length_hbm, tokens_hbm, own_hbm,
    mine_ref, theirs_ref, tokens_ref, own_ref, query_ref, passage_ref, count_ref, length_ref, sems, own_sems,
):
    copies = [
        pltpu.make_async_copy(src, dst, sems.at[i])
        for i, (src, dst) in enumerate(
            (
                (query_hbm, query_ref),
                (passage_hbm, passage_ref),
                (count_hbm, count_ref),
                (length_hbm, length_ref),
                (tokens_hbm, tokens_ref),
            )
        )
    ]
    size = own_ref.shape[0] // CHUNKS
    own_copies = [
        pltpu.make_async_copy(own_hbm.at[pl.ds(i * size, size)], own_ref.at[pl.ds(i * size, size)], own_sems.at[i])
        for i in range(CHUNKS)
    ]
    for copy in copies + own_copies:
        copy.start()
    for copy in copies:
        copy.wait()
    cap = query_ref.shape[1]
    lengths = length_ref[...].reshape(1, -1)
    counts = jnp.broadcast_to(count_ref[...].reshape(1, -1), (2 * shards, 2 * shards))
    row = lax.broadcasted_iota(jnp.int32, counts.shape, 0)
    col = lax.broadcasted_iota(jnp.int32, counts.shape, 1)
    counts = jnp.sum(jnp.where(row == col, counts, 0), axis=1, keepdims=True)
    blank = jnp.zeros((2 * shards, 32 - cap), jnp.int32)
    passage = jnp.concatenate([passage_ref[...], blank], axis=1)
    passage = jnp.concatenate([passage] * 4, axis=1)
    length = jnp.take_along_axis(jnp.broadcast_to(lengths, passage.shape), passage, axis=1)
    query = jnp.concatenate([jnp.concatenate([query_ref[...], blank], axis=1)] * 4, axis=1)
    lane = lax.broadcasted_iota(jnp.int32, passage.shape, 1)
    packed = jnp.where(lane < PASSAGE, query, jnp.where(lane < LENGTH, passage, jnp.where(lane < COUNT, length, counts)))
    packed = packed.reshape(shards, 2, 128)
    first = lax.axis_index("sub") == 0
    mine_ref[...] = jnp.where(first, packed[:, 0], packed[:, 1])
    theirs_ref[...] = jnp.where(first, packed[:, 1], packed[:, 0])
    for copy in own_copies:
        copy.wait()


def score_kernel(shards, distances, pack, cap, first, *refs):
    n = len(distances)
    p = n if first else n - 1
    meta_hbm, pieces, passage_refs, refs = refs[:2], refs[2 : 2 + p], refs[2 + p : 4 + p], refs[4 + p :]
    earlier_ref = None if first else refs[0]
    out_ref, query_ref, best_ref, meta_ref, work_ref, meta_sems, piece_sems = refs[-7:]
    q_tok, width = query_ref.shape[2:]
    tok_slots = passage_refs[0].shape[1]
    per_source = best_ref.shape[0]
    lanes = pack * q_tok
    q_bits = q_tok.bit_length() - 1
    me, core = lax.axis_index("shard"), lax.axis_index("sub")
    copies = [pltpu.make_async_copy(meta_hbm[i], meta_ref.at[i], meta_sems.at[i]) for i in range(2)]
    for i, piece in enumerate(reversed(pieces)):
        at = query_ref.at[i] if first else query_ref.at[pl.ds(0, 2)] if i == 0 else query_ref.at[i + 1]
        copies.append(pltpu.make_async_copy(piece, at, piece_sems.at[i]))
    for copy in copies:
        copy.start()
    best_ref[...] = jnp.zeros_like(best_ref)
    token = lax.broadcasted_iota(jnp.int32, (tok_slots, lanes), 0)
    place = lax.shift_right_logical(lax.broadcasted_iota(jnp.int32, (1, lanes), 1), q_bits)
    blank = jnp.zeros((q_tok, width), query_ref.dtype)
    for copy in copies:
        copy.wait()

    for which, passages in enumerate(passage_refs):
        owner = core if which == 0 else 1 - core

        def shard_of(i):
            if first:
                return jnp.bitwise_xor(me, jnp.where(i == 1, 1, i * 2))
            return jnp.bitwise_xor(me, jnp.where(i == 0, 2, i * 2 + 1))

        def list_source(i, total):
            live = meta_ref[which, shard_of(i), COUNT]
            for g in range(per_source):
                work_ref[total + g] = (i << SHIFT) + g
            return total + lax.shift_right_logical(live + pack - 1, pack.bit_length() - 1)

        total = lax.fori_loop(0, n, list_source, 0)
        for g in range(GROUPS):
            work_ref[total + g] = 0

        def one_step(first_group, groups):
            for j in range(groups):
                work = work_ref[first_group + j]
                i, g = lax.shift_right_logical(work, SHIFT), jnp.bitwise_and(work, (1 << SHIFT) - 1)
                shard = shard_of(i)
                rows, cols, limit = [], [], jnp.zeros((1, lanes), jnp.int32)
                for a in range(pack):
                    slot = g * pack + a
                    query, passage = meta_ref[which, shard, QUERY + slot], meta_ref[which, shard, PASSAGE + slot]
                    rows.append(jnp.concatenate([blank] * a + [query_ref[i, query]] + [blank] * (pack - 1 - a), axis=1))
                    cols.append(passages[passage])
                    limit = jnp.where(place == a, meta_ref[which, shard, LENGTH + slot], limit)
                sims = lax.dot_general(
                    jnp.concatenate(cols, axis=1), jnp.concatenate(rows, axis=0),
                    (((1,), (1,)), ((), ())), preferred_element_type=jnp.float32,
                )
                best = jnp.max(jnp.where(token < limit, sims, -1e30), axis=0, keepdims=True)
                best = jnp.where(place + g * pack < meta_ref[which, shard, COUNT], best, 0.0)
                best_ref[g, pl.ds(i * 2 + owner, 1), :] = best

        half = GROUPS // 2
        steps = lax.shift_right_logical(total + half - 1, GROUPS.bit_length() - 1)

        @pl.loop(0, steps)
        def _(step):
            one_step(step * GROUPS, GROUPS)

        @pl.when(total > steps * GROUPS)
        def _():
            one_step(steps * GROUPS, half)

    best = jnp.concatenate([best_ref[g] for g in range(per_source)], axis=1)
    high = best.astype(jnp.bfloat16)
    rest = best - high.astype(jnp.float32)
    middle = rest.astype(jnp.bfloat16)
    low = (rest - middle.astype(jnp.float32)).astype(jnp.bfloat16)
    row = lax.broadcasted_iota(jnp.int32, (per_source * lanes, 128), 0)
    col = lax.broadcasted_iota(jnp.int32, (per_source * lanes, 128), 1)
    add = jnp.where(lax.shift_right_logical(row, q_bits) == col, 1.0, 0.0).astype(jnp.bfloat16)
    parts = jnp.dot(jnp.concatenate([high, middle, low], axis=0), add, preferred_element_type=jnp.float32)
    rows = best.shape[0]
    score = (parts[:rows] + parts[rows : 2 * rows] + parts[2 * rows :]) * (1.0 / q_tok)
    if first:
        out_ref[...] = score[:, :cap]
        return
    for scores, at in ((earlier_ref[...], (0, 1, *range(4, shards, 2))), (score[:, :cap], distances)):
        for i, d in enumerate(at):
            out_ref[pl.ds((shards - 1 - jnp.bitwise_xor(me, d)) * 2, 2), :] = scores[2 * i : 2 * i + 2]


def pair_kernel(one_ref, other_ref, out_ref):
    out_ref[0] = one_ref[...]
    out_ref[1] = other_ref[...]


def order_kernel(back_ref, out_ref):
    shards = back_ref.shape[0] // 2
    for i in range(shards):
        out_ref[0, 2 * i : 2 * i + 2] = back_ref[2 * (shards - 1 - i) : 2 * (shards - i)]


def on_device(shards, queries, passages, passage_len, slot_query, slot_passage, slot_count):
    sources, _, cap = slot_query.shape
    q_dev, q_tok, width = queries.shape
    pack = 128 // q_tok
    per_source = -(-cap // pack)
    swap = [(0, 1), (1, 0)]
    vmem, hbm, anywhere = (pl.BlockSpec(memory_space=space) for space in (pltpu.VMEM, pltpu.HBM, pl.ANY))
    params = pltpu.CompilerParams(vmem_limit_bytes=12 * 1024 * 1024)
    row = jax.ShapeDtypeStruct((shards, 128), jnp.int32)

    def placed(space, *arrays):
        return [pltpu.with_memory_space_constraint(x, space) for x in arrays]

    def swapped(piece, d):
        return lax.ppermute(piece, "shard", [(i, i ^ d) for i in range(shards)])

    pieces = [queries, swapped(queries, 1)] + [None] * (shards - 2)
    for d in range(4, shards, 2):
        pieces[d] = swapped(queries, d)
    other_passages = lax.ppermute(passages, "sub", swap)

    mine, theirs, own_queries, own_passages = pl.pallas_call(
        functools.partial(pack_kernel, shards),
        out_shape=[row, row, *(jax.ShapeDtypeStruct(x.shape, x.dtype) for x in (queries, passages))],
        in_specs=[hbm] * 6,
        out_specs=[vmem] * 4,
        scratch_shapes=[
            pltpu.VMEM((sources, cap), jnp.int32),
            pltpu.VMEM((sources, cap), jnp.int32),
            pltpu.VMEM((sources,), jnp.int32),
            pltpu.VMEM(passage_len.shape, jnp.int32),
            pltpu.SemaphoreType.DMA((5,)),
            pltpu.SemaphoreType.DMA((CHUNKS,)),
        ],
        compiler_params=params,
    )(*placed(pltpu.HBM, slot_query.reshape(sources, cap), slot_passage.reshape(sources, cap), slot_count.reshape(sources), passage_len, queries, passages))
    both = pl.pallas_call(
        pair_kernel,
        out_shape=jax.ShapeDtypeStruct((2, *queries.shape), queries.dtype),
        in_specs=[vmem] * 2,
        out_specs=vmem,
        compiler_params=params,
    )(own_queries, pieces[1])
    both = swapped(both, 2)
    for d in range(5, shards, 2):
        pieces[d] = swapped(pieces[d - 1], 1)
    theirs, _ = lax.optimization_barrier((theirs, pieces[1]))
    other = lax.ppermute(theirs, "sub", swap)

    def scored(distances, *earlier):
        n, first = len(distances), not earlier
        parts = [pieces[d] for d in reversed(distances)] if first else [*(pieces[d] for d in reversed(distances[2:])), both]
        return pl.pallas_call(
            functools.partial(score_kernel, shards, distances, pack, cap, first),
            out_shape=jax.ShapeDtypeStruct((2 * n if first else sources, cap), jnp.float32),
            in_specs=[anywhere] * (2 + len(parts)) + [vmem] * (2 + len(earlier)),
            out_specs=vmem,
            scratch_shapes=[
                pltpu.VMEM((n, *queries.shape), queries.dtype),
                pltpu.VMEM((per_source, 2 * n, 128), jnp.float32),
                pltpu.SMEM((2, shards, 128), jnp.int32),
                pltpu.SMEM((n * per_source + 2 * GROUPS,), jnp.int32),
                pltpu.SemaphoreType.DMA((2,)),
                pltpu.SemaphoreType.DMA((n,)),
            ],
            compiler_params=params,
            cost_estimate=pl.CostEstimate(flops=1_000_000_000, bytes_accessed=9_000_000, transcendentals=0),
        )(mine, other, *parts, *placed(pltpu.VMEM, own_passages, other_passages), *earlier)

    pieces[0] = own_queries
    scores = scored((0, 1, *range(4, shards, 2)))
    scores = scored((2, *range(3, shards, 2)), scores)
    order = [list(reversed(range(shards)))]
    returned = lax.all_to_all(scores, "shard", split_axis=0, concat_axis=0, axis_index_groups=order, tiled=True)
    return pl.pallas_call(
        order_kernel,
        out_shape=jax.ShapeDtypeStruct((1, sources, cap), jnp.float32),
        in_specs=[vmem],
        out_specs=vmem,
        compiler_params=params,
    )(returned)


def solution(mesh):
    return jax.shard_map(
        functools.partial(on_device, mesh.shape["shard"]),
        mesh=mesh,
        in_specs=(
            P(("groups", "shard", "sub"), None, None),
            P(("shard", "sub"), None, None),
            P(("shard", "sub")),
            P("groups", ("shard", "sub"), None),
            P("groups", ("shard", "sub"), None),
            P("groups", ("shard", "sub")),
        ),
        out_specs=P(("groups", "shard", "sub"), None, None),
        check_vma=False,
    )
```

```python
import functools

import jax
import jax.numpy as jnp
from jax import lax
from jax.experimental import pallas as pl
from jax.experimental.pallas import tpu as pltpu
from jax.sharding import PartitionSpec as P

GROUPS = 8
CHUNKS = 8
SHIFT = 8
QUERY, PASSAGE, LENGTH, COUNT = 0, 32, 64, 96


def pack_kernel(
    shards, query_hbm, passage_hbm, count_hbm, length_hbm, tokens_hbm, own_hbm,
    mine_ref, theirs_ref, tokens_ref, own_ref, query_ref, passage_ref, count_ref, length_ref, sems, own_sems,
):
    copies = [
        pltpu.make_async_copy(src, dst, sems.at[i])
        for i, (src, dst) in enumerate(
            (
                (query_hbm, query_ref),
                (passage_hbm, passage_ref),
                (count_hbm, count_ref),
                (length_hbm, length_ref),
                (tokens_hbm, tokens_ref),
            )
        )
    ]
    size = own_ref.shape[0] // CHUNKS
    own_copies = [
        pltpu.make_async_copy(own_hbm.at[pl.ds(i * size, size)], own_ref.at[pl.ds(i * size, size)], own_sems.at[i])
        for i in range(CHUNKS)
    ]
    for copy in copies + own_copies:
        copy.start()
    for copy in copies:
        copy.wait()
    cap = query_ref.shape[1]
    lengths = length_ref[...].reshape(1, -1)
    counts = jnp.broadcast_to(count_ref[...].reshape(1, -1), (2 * shards, 2 * shards))
    row = lax.broadcasted_iota(jnp.int32, counts.shape, 0)
    col = lax.broadcasted_iota(jnp.int32, counts.shape, 1)
    counts = jnp.sum(jnp.where(row == col, counts, 0), axis=1, keepdims=True)
    blank = jnp.zeros((2 * shards, 32 - cap), jnp.int32)
    passage = jnp.concatenate([passage_ref[...], blank], axis=1)
    passage = jnp.concatenate([passage] * 4, axis=1)
    length = jnp.take_along_axis(jnp.broadcast_to(lengths, passage.shape), passage, axis=1)
    query = jnp.concatenate([jnp.concatenate([query_ref[...], blank], axis=1)] * 4, axis=1)
    lane = lax.broadcasted_iota(jnp.int32, passage.shape, 1)
    packed = jnp.where(lane < PASSAGE, query, jnp.where(lane < LENGTH, passage, jnp.where(lane < COUNT, length, counts)))
    packed = packed.reshape(shards, 2, 128)
    first = lax.axis_index("sub") == 0
    mine_ref[...] = jnp.where(first, packed[:, 0], packed[:, 1])
    theirs_ref[...] = jnp.where(first, packed[:, 1], packed[:, 0])
    for copy in own_copies:
        copy.wait()


def score_kernel(shards, distances, pack, cap, first, *refs):
    n = len(distances)
    p = n if first else n - 1
    meta_hbm, pieces, passage_refs, refs = refs[:2], refs[2 : 2 + p], refs[2 + p : 4 + p], refs[4 + p :]
    earlier_ref = None if first else refs[0]
    out_ref, query_ref, best_ref, meta_ref, work_ref, meta_sems, piece_sems = refs[-7:]
    q_tok, width = query_ref.shape[2:]
    tok_slots = passage_refs[0].shape[1]
    per_source = best_ref.shape[0]
    lanes = pack * q_tok
    q_bits = q_tok.bit_length() - 1
    me, core = lax.axis_index("shard"), lax.axis_index("sub")
    copies = [pltpu.make_async_copy(meta_hbm[i], meta_ref.at[i], meta_sems.at[i]) for i in range(2)]
    for i, piece in enumerate(reversed(pieces)):
        at = query_ref.at[i] if first else query_ref.at[pl.ds(0, 2)] if i == 0 else query_ref.at[i + 1]
        copies.append(pltpu.make_async_copy(piece, at, piece_sems.at[i]))
    for copy in copies:
        copy.start()
    best_ref[...] = jnp.zeros_like(best_ref)
    token = lax.broadcasted_iota(jnp.int32, (tok_slots, lanes), 0)
    place = lax.shift_right_logical(lax.broadcasted_iota(jnp.int32, (1, lanes), 1), q_bits)
    blank = jnp.zeros((q_tok, width), query_ref.dtype)
    for copy in copies:
        copy.wait()

    for which, passages in enumerate(passage_refs):
        owner = core if which == 0 else 1 - core

        def shard_of(i):
            if first:
                return jnp.bitwise_xor(me, jnp.where(i == 1, 1, i * 2))
            return jnp.bitwise_xor(me, jnp.where(i == 0, 2, i * 2 + 1))

        def list_source(i, total):
            live = meta_ref[which, shard_of(i), COUNT]
            for g in range(per_source):
                work_ref[total + g] = (i << SHIFT) + g
            return total + lax.shift_right_logical(live + pack - 1, pack.bit_length() - 1)

        total = lax.fori_loop(0, n, list_source, 0)
        for g in range(GROUPS):
            work_ref[total + g] = 0

        def one_step(first_group, groups):
            for j in range(groups):
                work = work_ref[first_group + j]
                i, g = lax.shift_right_logical(work, SHIFT), jnp.bitwise_and(work, (1 << SHIFT) - 1)
                shard = shard_of(i)
                rows, cols, limit = [], [], jnp.zeros((1, lanes), jnp.int32)
                for a in range(pack):
                    slot = g * pack + a
                    query, passage = meta_ref[which, shard, QUERY + slot], meta_ref[which, shard, PASSAGE + slot]
                    rows.append(jnp.concatenate([blank] * a + [query_ref[i, query]] + [blank] * (pack - 1 - a), axis=1))
                    cols.append(passages[passage])
                    limit = jnp.where(place == a, meta_ref[which, shard, LENGTH + slot], limit)
                sims = lax.dot_general(
                    jnp.concatenate(cols, axis=1), jnp.concatenate(rows, axis=0),
                    (((1,), (1,)), ((), ())), preferred_element_type=jnp.float32,
                )
                best = jnp.max(jnp.where(token < limit, sims, -1e30), axis=0, keepdims=True)
                best = jnp.where(place + g * pack < meta_ref[which, shard, COUNT], best, 0.0)
                best_ref[g, pl.ds(i * 2 + owner, 1), :] = best

        half = GROUPS // 2
        steps = lax.shift_right_logical(total + half - 1, GROUPS.bit_length() - 1)

        @pl.loop(0, steps)
        def _(step):
            one_step(step * GROUPS, GROUPS)

        @pl.when(total > steps * GROUPS)
        def _():
            one_step(steps * GROUPS, half)

    best = jnp.concatenate([best_ref[g] for g in range(per_source)], axis=1)
    high = best.astype(jnp.bfloat16)
    rest = best - high.astype(jnp.float32)
    middle = rest.astype(jnp.bfloat16)
    low = (rest - middle.astype(jnp.float32)).astype(jnp.bfloat16)
    row = lax.broadcasted_iota(jnp.int32, (per_source * lanes, 128), 0)
    col = lax.broadcasted_iota(jnp.int32, (per_source * lanes, 128), 1)
    add = jnp.where(lax.shift_right_logical(row, q_bits) == col, 1.0, 0.0).astype(jnp.bfloat16)
    parts = jnp.dot(jnp.concatenate([high, middle, low], axis=0), add, preferred_element_type=jnp.float32)
    rows = best.shape[0]
    score = (parts[:rows] + parts[rows : 2 * rows] + parts[2 * rows :]) * (1.0 / q_tok)
    if first:
        out_ref[...] = score[:, :cap]
        return
    for scores, at in ((earlier_ref[...], (0, 1, *range(4, shards, 2))), (score[:, :cap], distances)):
        for i, d in enumerate(at):
            out_ref[pl.ds((shards - 1 - jnp.bitwise_xor(me, d)) * 2, 2), :] = scores[2 * i : 2 * i + 2]


def pair_kernel(one_ref, other_ref, earlier_ref, out_ref):
    out_ref[0] = one_ref[...]
    out_ref[1] = other_ref[...]


def order_kernel(back_ref, out_ref):
    shards = back_ref.shape[0] // 2
    for i in range(shards):
        out_ref[0, 2 * i : 2 * i + 2] = back_ref[2 * (shards - 1 - i) : 2 * (shards - i)]


def on_device(shards, queries, passages, passage_len, slot_query, slot_passage, slot_count):
    sources, _, cap = slot_query.shape
    q_dev, q_tok, width = queries.shape
    pack = 128 // q_tok
    per_source = -(-cap // pack)
    swap = [(0, 1), (1, 0)]
    vmem, hbm, anywhere = (pl.BlockSpec(memory_space=space) for space in (pltpu.VMEM, pltpu.HBM, pl.ANY))
    params = pltpu.CompilerParams(vmem_limit_bytes=12 * 1024 * 1024)
    row = jax.ShapeDtypeStruct((shards, 128), jnp.int32)

    def placed(space, *arrays):
        return [pltpu.with_memory_space_constraint(x, space) for x in arrays]

    def swapped(piece, d):
        return lax.ppermute(piece, "shard", [(i, i ^ d) for i in range(shards)])

    pieces = [queries, swapped(queries, 1)] + [None] * (shards - 2)
    for d in range(4, shards, 2):
        pieces[d] = swapped(queries, d)
    other_passages = lax.ppermute(passages, "sub", swap)

    mine, theirs, own_queries, own_passages = pl.pallas_call(
        functools.partial(pack_kernel, shards),
        out_shape=[row, row, *(jax.ShapeDtypeStruct(x.shape, x.dtype) for x in (queries, passages))],
        in_specs=[hbm] * 6,
        out_specs=[vmem] * 4,
        scratch_shapes=[
            pltpu.VMEM((sources, cap), jnp.int32),
            pltpu.VMEM((sources, cap), jnp.int32),
            pltpu.VMEM((sources,), jnp.int32),
            pltpu.VMEM(passage_len.shape, jnp.int32),
            pltpu.SemaphoreType.DMA((5,)),
            pltpu.SemaphoreType.DMA((CHUNKS,)),
        ],
        compiler_params=params,
    )(*placed(pltpu.HBM, slot_query.reshape(sources, cap), slot_passage.reshape(sources, cap), slot_count.reshape(sources), passage_len, queries, passages))
    both = pl.pallas_call(
        pair_kernel,
        out_shape=jax.ShapeDtypeStruct((2, *queries.shape), queries.dtype),
        in_specs=[vmem, vmem, anywhere],
        out_specs=vmem,
        compiler_params=params,
    )(own_queries, pieces[1], pieces[4])
    both = swapped(both, 2)
    for d in range(5, shards, 2):
        pieces[d] = swapped(pieces[d - 1], 1)
    theirs, _ = lax.optimization_barrier((theirs, pieces[4]))
    other = lax.ppermute(theirs, "sub", swap)

    def scored(distances, *earlier):
        n, first = len(distances), not earlier
        parts = [pieces[d] for d in reversed(distances)] if first else [*(pieces[d] for d in reversed(distances[2:])), both]
        return pl.pallas_call(
            functools.partial(score_kernel, shards, distances, pack, cap, first),
            out_shape=jax.ShapeDtypeStruct((2 * n if first else sources, cap), jnp.float32),
            in_specs=[anywhere] * (2 + len(parts)) + [vmem] * (2 + len(earlier)),
            out_specs=vmem,
            scratch_shapes=[
                pltpu.VMEM((n, *queries.shape), queries.dtype),
                pltpu.VMEM((per_source, 2 * n, 128), jnp.float32),
                pltpu.SMEM((2, shards, 128), jnp.int32),
                pltpu.SMEM((n * per_source + 2 * GROUPS,), jnp.int32),
                pltpu.SemaphoreType.DMA((2,)),
                pltpu.SemaphoreType.DMA((n,)),
            ],
            compiler_params=params,
            cost_estimate=pl.CostEstimate(flops=1_000_000_000, bytes_accessed=9_000_000, transcendentals=0),
        )(mine, other, *parts, *placed(pltpu.VMEM, own_passages, other_passages), *earlier)

    pieces[0] = own_queries
    scores = scored((0, 1, *range(4, shards, 2)))
    scores = scored((2, *range(3, shards, 2)), scores)
    order = [list(reversed(range(shards)))]
    returned = lax.all_to_all(scores, "shard", split_axis=0, concat_axis=0, axis_index_groups=order, tiled=True)
    return pl.pallas_call(
        order_kernel,
        out_shape=jax.ShapeDtypeStruct((1, sources, cap), jnp.float32),
        in_specs=[vmem],
        out_specs=vmem,
        compiler_params=params,
    )(returned)


def solution(mesh):
    return jax.shard_map(
        functools.partial(on_device, mesh.shape["shard"]),
        mesh=mesh,
        in_specs=(
            P(("groups", "shard", "sub"), None, None),
            P(("shard", "sub"), None, None),
            P(("shard", "sub")),
            P("groups", ("shard", "sub"), None),
            P("groups", ("shard", "sub"), None),
            P("groups", ("shard", "sub")),
        ),
        out_specs=P(("groups", "shard", "sub"), None, None),
        check_vma=False,
    )
```

```python
import functools

import jax
import jax.numpy as jnp
from jax import lax
from jax.experimental import pallas as pl
from jax.experimental.pallas import tpu as pltpu
from jax.sharding import PartitionSpec as P

GROUPS = 8
CHUNKS = 8
SHIFT = 8
QUERY, PASSAGE, LENGTH, COUNT = 0, 32, 64, 96


def pack_kernel(
    shards, query_hbm, passage_hbm, count_hbm, length_hbm, tokens_hbm, own_hbm,
    mine_ref, theirs_ref, tokens_ref, own_ref, query_ref, passage_ref, count_ref, length_ref, sems, own_sems,
):
    copies = [
        pltpu.make_async_copy(src, dst, sems.at[i])
        for i, (src, dst) in enumerate(
            (
                (query_hbm, query_ref),
                (passage_hbm, passage_ref),
                (count_hbm, count_ref),
                (length_hbm, length_ref),
                (tokens_hbm, tokens_ref),
            )
        )
    ]
    size = own_ref.shape[0] // CHUNKS
    own_copies = [
        pltpu.make_async_copy(own_hbm.at[pl.ds(i * size, size)], own_ref.at[pl.ds(i * size, size)], own_sems.at[i])
        for i in range(CHUNKS)
    ]
    for copy in copies + own_copies:
        copy.start()
    for copy in copies:
        copy.wait()
    cap = query_ref.shape[1]
    lengths = length_ref[...].reshape(1, -1)
    counts = jnp.broadcast_to(count_ref[...].reshape(1, -1), (2 * shards, 2 * shards))
    row = lax.broadcasted_iota(jnp.int32, counts.shape, 0)
    col = lax.broadcasted_iota(jnp.int32, counts.shape, 1)
    counts = jnp.sum(jnp.where(row == col, counts, 0), axis=1, keepdims=True)
    blank = jnp.zeros((2 * shards, 32 - cap), jnp.int32)
    passage = jnp.concatenate([passage_ref[...], blank], axis=1)
    passage = jnp.concatenate([passage] * 4, axis=1)
    length = jnp.take_along_axis(jnp.broadcast_to(lengths, passage.shape), passage, axis=1)
    query = jnp.concatenate([jnp.concatenate([query_ref[...], blank], axis=1)] * 4, axis=1)
    lane = lax.broadcasted_iota(jnp.int32, passage.shape, 1)
    packed = jnp.where(lane < PASSAGE, query, jnp.where(lane < LENGTH, passage, jnp.where(lane < COUNT, length, counts)))
    packed = packed.reshape(shards, 2, 128)
    first = lax.axis_index("sub") == 0
    mine_ref[...] = jnp.where(first, packed[:, 0], packed[:, 1])
    theirs_ref[...] = jnp.where(first, packed[:, 1], packed[:, 0])
    for copy in own_copies:
        copy.wait()


def score_kernel(shards, distances, call, pack, cap, *refs):
    n = len(distances)
    p = 1 if call == 1 else n
    meta_hbm, pieces, passage_refs, earlier = refs[:2], refs[2 : 2 + p], refs[2 + p : 4 + p], refs[4 + p : 4 + p + call]
    out_ref, query_ref, best_ref, add_ref, meta_ref, work_ref, meta_sems, piece_sems = refs[-8:]
    q_tok, width = query_ref.shape[2:]
    tok_slots = passage_refs[0].shape[1]
    per_source = best_ref.shape[0]
    lanes = pack * q_tok
    q_bits = q_tok.bit_length() - 1
    me, core = lax.axis_index("shard"), lax.axis_index("sub")
    copies = [pltpu.make_async_copy(meta_hbm[i], meta_ref.at[i], meta_sems.at[i]) for i in range(2)]
    for i, piece in enumerate(reversed(pieces)):
        copies.append(pltpu.make_async_copy(piece, query_ref if call == 1 else query_ref.at[i], piece_sems.at[i]))
    for copy in copies:
        copy.start()
    best_ref[...] = jnp.zeros_like(best_ref)
    row = lax.broadcasted_iota(jnp.int32, add_ref.shape, 0)
    col = lax.broadcasted_iota(jnp.int32, add_ref.shape, 1)
    add_ref[...] = jnp.where(lax.shift_right_logical(row, q_bits) == col, 1.0, 0.0).astype(add_ref.dtype)
    token = lax.broadcasted_iota(jnp.int32, (tok_slots, lanes), 0)
    place = lax.shift_right_logical(lax.broadcasted_iota(jnp.int32, (1, lanes), 1), q_bits)
    blank = jnp.zeros((q_tok, width), query_ref.dtype)

    def shard_of(i):
        return jnp.bitwise_xor(me, (jnp.where(i == 1, 1, i * 2), i + 2, i * 2 + 5)[call])

    for copy in copies[:2]:
        copy.wait()
    totals = []
    for which in range(2):

        def list_source(i, total):
            live = meta_ref[which, shard_of(i), COUNT]
            for g in range(per_source):
                work_ref[which, total + g] = (i << SHIFT) + g
            return total + lax.shift_right_logical(live + pack - 1, pack.bit_length() - 1)

        total = 0
        if n <= 8:
            for i in range(n):
                total = list_source(i, total)
        else:
            total = lax.fori_loop(0, n, list_source, 0)
        for g in range(GROUPS):
            work_ref[which, total + g] = 0
        totals.append(total)
    for copy in copies[2:]:
        copy.wait()

    for which, passages in enumerate(passage_refs):
        owner = core if which == 0 else 1 - core
        total = totals[which]

        def one_step(first_group, groups):
            for j in range(groups):
                work = work_ref[which, first_group + j]
                i, g = lax.shift_right_logical(work, SHIFT), jnp.bitwise_and(work, (1 << SHIFT) - 1)
                shard = shard_of(i)
                rows, cols, limit = [], [], jnp.zeros((1, lanes), jnp.int32)
                for a in range(pack):
                    slot = g * pack + a
                    query, passage = meta_ref[which, shard, QUERY + slot], meta_ref[which, shard, PASSAGE + slot]
                    rows.append(jnp.concatenate([blank] * a + [query_ref[i, query]] + [blank] * (pack - 1 - a), axis=1))
                    cols.append(passages[passage])
                    limit = jnp.where(place == a, meta_ref[which, shard, LENGTH + slot], limit)
                sims = lax.dot_general(
                    jnp.concatenate(cols, axis=1), jnp.concatenate(rows, axis=0),
                    (((1,), (1,)), ((), ())), preferred_element_type=jnp.float32,
                )
                best = jnp.max(jnp.where(token < limit, sims, -1e30), axis=0, keepdims=True)
                best = jnp.where(place + g * pack < meta_ref[which, shard, COUNT], best, 0.0)
                best_ref[g, pl.ds(i * 2 + owner, 1), :] = best

        half = GROUPS // 2
        steps = lax.shift_right_logical(total + half - 1, GROUPS.bit_length() - 1)

        @pl.loop(0, steps)
        def _(step):
            one_step(step * GROUPS, GROUPS)

        @pl.when(total > steps * GROUPS)
        def _():
            one_step(steps * GROUPS, half)

    best = jnp.concatenate([best_ref[g] for g in range(per_source)], axis=1)
    high = best.astype(jnp.bfloat16)
    rest = best - high.astype(jnp.float32)
    middle = rest.astype(jnp.bfloat16)
    low = (rest - middle.astype(jnp.float32)).astype(jnp.bfloat16)
    parts = jnp.dot(jnp.concatenate([high, middle, low], axis=0), add_ref[...], preferred_element_type=jnp.float32)
    rows = best.shape[0]
    score = (parts[:rows] + parts[rows : 2 * rows] + parts[2 * rows :]) * (1.0 / q_tok)
    if call < 2:
        out_ref[...] = score[:, :cap]
        return
    for scores, at in zip((*(ref[...] for ref in earlier), score[:, :cap]), ((0, 1, *range(4, shards, 2)), (2, 3), distances)):
        for i, d in enumerate(at):
            out_ref[pl.ds((shards - 1 - jnp.bitwise_xor(me, d)) * 2, 2), :] = scores[2 * i : 2 * i + 2]


def pair_kernel(one_ref, other_ref, out_ref):
    out_ref[0] = one_ref[...]
    out_ref[1] = other_ref[...]


def order_kernel(back_ref, out_ref):
    shards = back_ref.shape[0] // 2
    for i in range(shards):
        out_ref[0, 2 * i : 2 * i + 2] = back_ref[2 * (shards - 1 - i) : 2 * (shards - i)]


def on_device(shards, queries, passages, passage_len, slot_query, slot_passage, slot_count):
    sources, _, cap = slot_query.shape
    q_dev, q_tok, width = queries.shape
    pack = 128 // q_tok
    per_source = -(-cap // pack)
    swap = [(0, 1), (1, 0)]
    vmem, hbm, anywhere = (pl.BlockSpec(memory_space=space) for space in (pltpu.VMEM, pltpu.HBM, pl.ANY))
    params = pltpu.CompilerParams(vmem_limit_bytes=12 * 1024 * 1024)
    row = jax.ShapeDtypeStruct((shards, 128), jnp.int32)

    def placed(space, *arrays):
        return [pltpu.with_memory_space_constraint(x, space) for x in arrays]

    def swapped(piece, d):
        return lax.ppermute(piece, "shard", [(i, i ^ d) for i in range(shards)])

    pieces = [queries, swapped(queries, 1)] + [None] * (shards - 2)
    for d in range(4, shards, 2):
        pieces[d] = swapped(queries, d)
    other_passages = lax.ppermute(passages, "sub", swap)

    mine, theirs, own_queries, own_passages = pl.pallas_call(
        functools.partial(pack_kernel, shards),
        out_shape=[row, row, *(jax.ShapeDtypeStruct(x.shape, x.dtype) for x in (queries, passages))],
        in_specs=[hbm] * 6,
        out_specs=[vmem] * 4,
        scratch_shapes=[
            pltpu.VMEM((sources, cap), jnp.int32),
            pltpu.VMEM((sources, cap), jnp.int32),
            pltpu.VMEM((sources,), jnp.int32),
            pltpu.VMEM(passage_len.shape, jnp.int32),
            pltpu.SemaphoreType.DMA((5,)),
            pltpu.SemaphoreType.DMA((CHUNKS,)),
        ],
        compiler_params=params,
    )(*placed(pltpu.HBM, slot_query.reshape(sources, cap), slot_passage.reshape(sources, cap), slot_count.reshape(sources), passage_len, queries, passages))
    both = pl.pallas_call(
        pair_kernel,
        out_shape=jax.ShapeDtypeStruct((2, *queries.shape), queries.dtype),
        in_specs=[vmem] * 2,
        out_specs=vmem,
        compiler_params=params,
    )(own_queries, pieces[1])
    both = swapped(both, 2)
    for d in range(5, shards, 2):
        pieces[d] = swapped(pieces[d - 1], 1)
    theirs, _ = lax.optimization_barrier((theirs, pieces[1]))
    other = lax.ppermute(theirs, "sub", swap)

    def scored(distances, parts, *earlier):
        n, call = len(distances), len(earlier)
        return pl.pallas_call(
            functools.partial(score_kernel, shards, distances, call, pack, cap),
            out_shape=jax.ShapeDtypeStruct((2 * n if call < 2 else sources, cap), jnp.float32),
            in_specs=[anywhere] * (2 + len(parts)) + [vmem] * (2 + len(earlier)),
            out_specs=vmem,
            scratch_shapes=[
                pltpu.VMEM((n, *queries.shape), queries.dtype),
                pltpu.VMEM((per_source, 2 * n, 128), jnp.float32),
                pltpu.VMEM((per_source * 128, 128), jnp.bfloat16),
                pltpu.SMEM((2, shards, 128), jnp.int32),
                pltpu.SMEM((2, n * per_source + 2 * GROUPS), jnp.int32),
                pltpu.SemaphoreType.DMA((2,)),
                pltpu.SemaphoreType.DMA((n,)),
            ],
            compiler_params=params,
            cost_estimate=pl.CostEstimate(flops=1_000_000_000, bytes_accessed=9_000_000, transcendentals=0),
        )(mine, other, *parts, *placed(pltpu.VMEM, own_passages, other_passages), *earlier)

    pieces[0] = own_queries
    near, far = (0, 1, *range(4, shards, 2)), range(5, shards, 2)
    scores = [scored(near, [pieces[d] for d in reversed(near)])]
    scores.append(scored((2, 3), [both], *scores))
    scores = scored(far, [pieces[d] for d in reversed(far)], *scores)
    order = [list(reversed(range(shards)))]
    returned = lax.all_to_all(scores, "shard", split_axis=0, concat_axis=0, axis_index_groups=order, tiled=True)
    return pl.pallas_call(
        order_kernel,
        out_shape=jax.ShapeDtypeStruct((1, sources, cap), jnp.float32),
        in_specs=[vmem],
        out_specs=vmem,
        compiler_params=params,
    )(returned)


def solution(mesh):
    return jax.shard_map(
        functools.partial(on_device, mesh.shape["shard"]),
        mesh=mesh,
        in_specs=(
            P(("groups", "shard", "sub"), None, None),
            P(("shard", "sub"), None, None),
            P(("shard", "sub")),
            P("groups", ("shard", "sub"), None),
            P("groups", ("shard", "sub"), None),
            P("groups", ("shard", "sub")),
        ),
        out_specs=P(("groups", "shard", "sub"), None, None),
        check_vma=False,
    )
```

```python
import functools

import jax
import jax.numpy as jnp
from jax import lax
from jax.experimental import pallas as pl
from jax.experimental.pallas import tpu as pltpu
from jax.sharding import PartitionSpec as P

GROUPS = 8
CHUNKS = 8
SHIFT = 8
QUERY, PASSAGE, LENGTH, COUNT = 0, 32, 64, 96


def pack_kernel(
    shards, query_hbm, passage_hbm, count_hbm, length_hbm, tokens_hbm, own_hbm,
    mine_ref, theirs_ref, tokens_ref, own_ref, add_ref, query_ref, passage_ref, count_ref, length_ref, sems, own_sems,
):
    copies = [
        pltpu.make_async_copy(src, dst, sems.at[i])
        for i, (src, dst) in enumerate(
            (
                (query_hbm, query_ref),
                (passage_hbm, passage_ref),
                (count_hbm, count_ref),
                (length_hbm, length_ref),
                (tokens_hbm, tokens_ref),
            )
        )
    ]
    size = own_ref.shape[0] // CHUNKS
    own_copies = [
        pltpu.make_async_copy(own_hbm.at[pl.ds(i * size, size)], own_ref.at[pl.ds(i * size, size)], own_sems.at[i])
        for i in range(CHUNKS)
    ]
    for copy in copies + own_copies:
        copy.start()
    row = lax.broadcasted_iota(jnp.int32, add_ref.shape, 0)
    col = lax.broadcasted_iota(jnp.int32, add_ref.shape, 1)
    q_bits = tokens_ref.shape[1].bit_length() - 1
    add_ref[...] = jnp.where(lax.shift_right_logical(row, q_bits) == col, 1.0, 0.0).astype(add_ref.dtype)
    for copy in copies:
        copy.wait()
    cap = query_ref.shape[1]
    lengths = length_ref[...].reshape(1, -1)
    counts = jnp.broadcast_to(count_ref[...].reshape(1, -1), (2 * shards, 2 * shards))
    row = lax.broadcasted_iota(jnp.int32, counts.shape, 0)
    col = lax.broadcasted_iota(jnp.int32, counts.shape, 1)
    counts = jnp.sum(jnp.where(row == col, counts, 0), axis=1, keepdims=True)
    blank = jnp.zeros((2 * shards, 32 - cap), jnp.int32)
    passage = jnp.concatenate([passage_ref[...], blank], axis=1)
    passage = jnp.concatenate([passage] * 4, axis=1)
    length = jnp.take_along_axis(jnp.broadcast_to(lengths, passage.shape), passage, axis=1)
    query = jnp.concatenate([jnp.concatenate([query_ref[...], blank], axis=1)] * 4, axis=1)
    lane = lax.broadcasted_iota(jnp.int32, passage.shape, 1)
    packed = jnp.where(lane < PASSAGE, query, jnp.where(lane < LENGTH, passage, jnp.where(lane < COUNT, length, counts)))
    packed = packed.reshape(shards, 2, 128)
    first = lax.axis_index("sub") == 0
    mine_ref[...] = jnp.where(first, packed[:, 0], packed[:, 1])
    theirs_ref[...] = jnp.where(first, packed[:, 1], packed[:, 0])
    for copy in own_copies:
        copy.wait()


def distance(call, i):
    return (jnp.where(i == 1, 1, i * 2), i + 2, i * 2 + 5)[call]


def list_kernel(sizes, pack, per_source, mine, other, mine_ref, other_ref, total_ref, *refs):
    work_refs, sems = refs[:-1], refs[-1]
    me = lax.axis_index("shard")
    rows = (mine_ref, other_ref)
    copies = [pltpu.make_async_copy(src, dst, sems.at[i]) for i, (src, dst) in enumerate(zip((mine, other), rows))]
    for copy in copies:
        copy.start()
    for copy in copies:
        copy.wait()
    for call, n in enumerate(sizes):
        for which in range(2):

            def list_source(i, total):
                live = rows[which][jnp.bitwise_xor(me, distance(call, i)), COUNT]
                for g in range(per_source):
                    work_refs[call][which, total + g] = (i << SHIFT) + g
                return total + lax.shift_right_logical(live + pack - 1, pack.bit_length() - 1)

            total = 0
            if n <= 8:
                for i in range(n):
                    total = list_source(i, total)
            else:
                total = lax.fori_loop(0, n, list_source, 0)
            for g in range(GROUPS):
                work_refs[call][which, total + g] = 0
            total_ref[call, which] = total


def score_kernel(shards, distances, call, pack, cap, *refs):
    n = len(distances)
    p = 1 if call == 1 else n
    metas, total_ref, work_ref, pieces, refs = refs[:2], refs[2], refs[3], refs[4 : 4 + p], refs[4 + p :]
    passage_refs, add_ref, earlier, (out_ref, query_ref, best_ref) = refs[:2], refs[2], refs[3 : 3 + call], refs[-3:]
    q_tok, width = query_ref.shape[2:]
    tok_slots = passage_refs[0].shape[1]
    per_source = best_ref.shape[0]
    lanes = pack * q_tok
    q_bits = q_tok.bit_length() - 1
    me, core = lax.axis_index("shard"), lax.axis_index("sub")
    if call == 1:
        query_ref[...] = pieces[0][...]
    else:
        for i, piece in enumerate(reversed(pieces)):
            query_ref[i] = piece[...]
    best_ref[...] = jnp.zeros_like(best_ref)
    token = lax.broadcasted_iota(jnp.int32, (tok_slots, lanes), 0)
    place = lax.shift_right_logical(lax.broadcasted_iota(jnp.int32, (1, lanes), 1), q_bits)
    blank = jnp.zeros((q_tok, width), query_ref.dtype)

    for which, passages in enumerate(passage_refs):
        meta_ref = metas[which]
        owner = core if which == 0 else 1 - core
        total = total_ref[call, which]

        def one_step(first_group, groups):
            for j in range(groups):
                work = work_ref[which, first_group + j]
                i, g = lax.shift_right_logical(work, SHIFT), jnp.bitwise_and(work, (1 << SHIFT) - 1)
                shard = jnp.bitwise_xor(me, distance(call, i))
                rows, cols, limit = [], [], jnp.zeros((1, lanes), jnp.int32)
                for a in range(pack):
                    slot = g * pack + a
                    query, passage = meta_ref[shard, QUERY + slot], meta_ref[shard, PASSAGE + slot]
                    rows.append(jnp.concatenate([blank] * a + [query_ref[i, query]] + [blank] * (pack - 1 - a), axis=1))
                    cols.append(passages[passage])
                    limit = jnp.where(place == a, meta_ref[shard, LENGTH + slot], limit)
                sims = lax.dot_general(
                    jnp.concatenate(cols, axis=1), jnp.concatenate(rows, axis=0),
                    (((1,), (1,)), ((), ())), preferred_element_type=jnp.float32,
                )
                best = jnp.max(jnp.where(token < limit, sims, -1e30), axis=0, keepdims=True)
                best = jnp.where(place + g * pack < meta_ref[shard, COUNT], best, 0.0)
                best_ref[g, pl.ds(i * 2 + owner, 1), :] = best

        half = GROUPS // 2
        steps = lax.shift_right_logical(total + half - 1, GROUPS.bit_length() - 1)

        @pl.loop(0, steps)
        def _(step):
            one_step(step * GROUPS, GROUPS)

        @pl.when(total > steps * GROUPS)
        def _():
            one_step(steps * GROUPS, half)

    best = jnp.concatenate([best_ref[g] for g in range(per_source)], axis=1)
    high = best.astype(jnp.bfloat16)
    rest = best - high.astype(jnp.float32)
    middle = rest.astype(jnp.bfloat16)
    low = (rest - middle.astype(jnp.float32)).astype(jnp.bfloat16)
    parts = jnp.dot(jnp.concatenate([high, middle, low], axis=0), add_ref[...], preferred_element_type=jnp.float32)
    rows = best.shape[0]
    score = (parts[:rows] + parts[rows : 2 * rows] + parts[2 * rows :]) * (1.0 / q_tok)
    if call < 2:
        out_ref[...] = score[:, :cap]
        return
    for scores, at in zip((*(ref[...] for ref in earlier), score[:, :cap]), ((0, 1, *range(4, shards, 2)), (2, 3), distances)):
        for i, d in enumerate(at):
            out_ref[pl.ds((shards - 1 - jnp.bitwise_xor(me, d)) * 2, 2), :] = scores[2 * i : 2 * i + 2]


def pair_kernel(one_ref, other_ref, out_ref):
    out_ref[0] = one_ref[...]
    out_ref[1] = other_ref[...]


def order_kernel(back_ref, out_ref):
    shards = back_ref.shape[0] // 2
    for i in range(shards):
        out_ref[0, 2 * i : 2 * i + 2] = back_ref[2 * (shards - 1 - i) : 2 * (shards - i)]


def on_device(shards, queries, passages, passage_len, slot_query, slot_passage, slot_count):
    sources, _, cap = slot_query.shape
    q_dev, q_tok, width = queries.shape
    pack = 128 // q_tok
    per_source = -(-cap // pack)
    swap = [(0, 1), (1, 0)]
    vmem, hbm, smem, anywhere = (pl.BlockSpec(memory_space=space) for space in (pltpu.VMEM, pltpu.HBM, pltpu.SMEM, pl.ANY))
    params = pltpu.CompilerParams(vmem_limit_bytes=12 * 1024 * 1024)
    row = jax.ShapeDtypeStruct((shards, 128), jnp.int32)

    def placed(space, *arrays):
        return [pltpu.with_memory_space_constraint(x, space) for x in arrays]

    def swapped(piece, d):
        return lax.ppermute(piece, "shard", [(i, i ^ d) for i in range(shards)])

    pieces = [queries, swapped(queries, 1)] + [None] * (shards - 2)
    for d in range(4, shards, 2):
        pieces[d] = swapped(queries, d)
    other_passages = lax.ppermute(passages, "sub", swap)

    mine, theirs, own_queries, own_passages, add = pl.pallas_call(
        functools.partial(pack_kernel, shards),
        out_shape=[
            row, row, *(jax.ShapeDtypeStruct(x.shape, x.dtype) for x in (queries, passages)),
            jax.ShapeDtypeStruct((per_source * 128, 128), jnp.bfloat16),
        ],
        in_specs=[hbm] * 6,
        out_specs=[vmem] * 5,
        scratch_shapes=[
            pltpu.VMEM((sources, cap), jnp.int32),
            pltpu.VMEM((sources, cap), jnp.int32),
            pltpu.VMEM((sources,), jnp.int32),
            pltpu.VMEM(passage_len.shape, jnp.int32),
            pltpu.SemaphoreType.DMA((5,)),
            pltpu.SemaphoreType.DMA((CHUNKS,)),
        ],
        compiler_params=params,
    )(*placed(pltpu.HBM, slot_query.reshape(sources, cap), slot_passage.reshape(sources, cap), slot_count.reshape(sources), passage_len, queries, passages))
    both = pl.pallas_call(
        pair_kernel,
        out_shape=jax.ShapeDtypeStruct((2, *queries.shape), queries.dtype),
        in_specs=[vmem] * 2,
        out_specs=vmem,
        compiler_params=params,
    )(own_queries, pieces[1])
    both = swapped(both, 2)
    for d in range(5, shards, 2):
        pieces[d] = swapped(pieces[d - 1], 1)
    theirs, _ = lax.optimization_barrier((theirs, pieces[1]))
    other = lax.ppermute(theirs, "sub", swap)

    near, far = (0, 1, *range(4, shards, 2)), range(5, shards, 2)
    calls = (near, (2, 3), far)
    *rows, totals, work_near, work_next, work_far = pl.pallas_call(
        functools.partial(list_kernel, tuple(map(len, calls)), pack, per_source),
        out_shape=[
            *[pltpu.SMEM(row.shape, row.dtype)] * 2,
            pltpu.SMEM((len(calls), 2), jnp.int32),
            *(pltpu.SMEM((2, len(call) * per_source + 2 * GROUPS), jnp.int32) for call in calls),
        ],
        in_specs=[anywhere] * 2,
        out_specs=[smem] * (3 + len(calls)),
        scratch_shapes=[pltpu.SemaphoreType.DMA((2,))],
        compiler_params=params,
    )(mine, other)
    works = (work_near, work_next, work_far)

    def scored(parts, *earlier):
        call = len(earlier)
        distances = calls[call]
        n = len(distances)
        return pl.pallas_call(
            functools.partial(score_kernel, shards, distances, call, pack, cap),
            out_shape=jax.ShapeDtypeStruct((2 * n if call < 2 else sources, cap), jnp.float32),
            in_specs=[smem] * 4 + [vmem] * (len(parts) + 3 + len(earlier)),
            out_specs=vmem,
            scratch_shapes=[
                pltpu.VMEM((n, *queries.shape), queries.dtype),
                pltpu.VMEM((per_source, 2 * n, 128), jnp.float32),
            ],
            compiler_params=params,
            cost_estimate=pl.CostEstimate(flops=1_000_000_000, bytes_accessed=9_000_000, transcendentals=0),
        )(*placed(pltpu.SMEM, *rows, totals, works[call]), *parts, *placed(pltpu.VMEM, own_passages, other_passages), add, *earlier)

    pieces[0] = own_queries
    scores = [scored([pieces[d] for d in reversed(near)])]
    scores.append(scored([both], *scores))
    scores = scored([pieces[d] for d in reversed(far)], *scores)
    order = [list(reversed(range(shards)))]
    returned = lax.all_to_all(scores, "shard", split_axis=0, concat_axis=0, axis_index_groups=order, tiled=True)
    return pl.pallas_call(
        order_kernel,
        out_shape=jax.ShapeDtypeStruct((1, sources, cap), jnp.float32),
        in_specs=[vmem],
        out_specs=vmem,
        compiler_params=params,
    )(returned)


def solution(mesh):
    return jax.shard_map(
        functools.partial(on_device, mesh.shape["shard"]),
        mesh=mesh,
        in_specs=(
            P(("groups", "shard", "sub"), None, None),
            P(("shard", "sub"), None, None),
            P(("shard", "sub")),
            P("groups", ("shard", "sub"), None),
            P("groups", ("shard", "sub"), None),
            P("groups", ("shard", "sub")),
        ),
        out_specs=P(("groups", "shard", "sub"), None, None),
        check_vma=False,
    )
```

```python
import functools

import jax
import jax.numpy as jnp
from jax import lax
from jax.experimental import pallas as pl
from jax.experimental.pallas import tpu as pltpu
from jax.sharding import PartitionSpec as P

GROUPS = 8
CHUNKS = 8
SHIFT = 8
QUERY, PASSAGE, LENGTH, COUNT = 0, 32, 64, 96


def distance(call, i):
    return (jnp.where(i == 1, 1, i * 2), i + 2, i * 2 + 5)[call]


def list_groups(sizes, pack, per_source, row_ref, total_ref, work_refs):
    me = lax.axis_index("shard")
    for call, (n, work_ref) in enumerate(zip(sizes, work_refs)):

        def list_source(i, total):
            live = row_ref[jnp.bitwise_xor(me, distance(call, i)), COUNT]
            for g in range(per_source):
                work_ref[total + g] = (i << SHIFT) + g
            return total + lax.shift_right_logical(live + pack - 1, pack.bit_length() - 1)

        total = 0
        if n <= 8:
            for i in range(n):
                total = list_source(i, total)
        else:
            total = lax.fori_loop(0, n, list_source, 0)
        for g in range(GROUPS):
            work_ref[total + g] = 0
        total_ref[call] = total


def pack_kernel(shards, sizes, pack, per_source, *refs):
    query_hbm, passage_hbm, count_hbm, length_hbm, tokens_hbm, own_hbm, theirs_ref, tokens_ref, own_ref, add_ref = refs[:10]
    row_ref, total_ref, *work_refs = refs[10 : 12 + len(sizes)]
    mine_ref, query_ref, passage_ref, count_ref, length_ref, sems, own_sems, row_sem = refs[12 + len(sizes) :]
    copies = [
        pltpu.make_async_copy(src, dst, sems.at[i])
        for i, (src, dst) in enumerate(
            (
                (query_hbm, query_ref),
                (passage_hbm, passage_ref),
                (count_hbm, count_ref),
                (length_hbm, length_ref),
                (tokens_hbm, tokens_ref),
            )
        )
    ]
    size = own_ref.shape[0] // CHUNKS
    own_copies = [
        pltpu.make_async_copy(own_hbm.at[pl.ds(i * size, size)], own_ref.at[pl.ds(i * size, size)], own_sems.at[i])
        for i in range(CHUNKS)
    ]
    for copy in copies + own_copies:
        copy.start()
    row = lax.broadcasted_iota(jnp.int32, add_ref.shape, 0)
    col = lax.broadcasted_iota(jnp.int32, add_ref.shape, 1)
    q_bits = tokens_ref.shape[1].bit_length() - 1
    add_ref[...] = jnp.where(lax.shift_right_logical(row, q_bits) == col, 1.0, 0.0).astype(add_ref.dtype)
    for copy in copies:
        copy.wait()
    cap = query_ref.shape[1]
    lengths = length_ref[...].reshape(1, -1)
    counts = jnp.broadcast_to(count_ref[...].reshape(1, -1), (2 * shards, 2 * shards))
    row = lax.broadcasted_iota(jnp.int32, counts.shape, 0)
    col = lax.broadcasted_iota(jnp.int32, counts.shape, 1)
    counts = jnp.sum(jnp.where(row == col, counts, 0), axis=1, keepdims=True)
    blank = jnp.zeros((2 * shards, 32 - cap), jnp.int32)
    passage = jnp.concatenate([passage_ref[...], blank], axis=1)
    passage = jnp.concatenate([passage] * 4, axis=1)
    length = jnp.take_along_axis(jnp.broadcast_to(lengths, passage.shape), passage, axis=1)
    query = jnp.concatenate([jnp.concatenate([query_ref[...], blank], axis=1)] * 4, axis=1)
    lane = lax.broadcasted_iota(jnp.int32, passage.shape, 1)
    packed = jnp.where(lane < PASSAGE, query, jnp.where(lane < LENGTH, passage, jnp.where(lane < COUNT, length, counts)))
    packed = packed.reshape(shards, 2, 128)
    first = lax.axis_index("sub") == 0
    mine_ref[...] = jnp.where(first, packed[:, 0], packed[:, 1])
    theirs_ref[...] = jnp.where(first, packed[:, 1], packed[:, 0])
    copy = pltpu.make_async_copy(mine_ref, row_ref, row_sem)
    copy.start()
    copy.wait()
    list_groups(sizes, pack, per_source, row_ref, total_ref, work_refs)
    for copy in own_copies:
        copy.wait()


def score_kernel(shards, calls, call, pack, cap, *refs):
    distances = calls[call]
    n = len(distances)
    p = 1 if call == 1 else n
    lists, refs = [refs[:3]], refs[3:]
    if call == 0:
        other_rows, refs = refs[0], refs[1:]
        refs, (out_ref, *other_lists, query_ref, best_ref, row_sem) = refs[: p + 3], refs[p + 3 :]
        row_ref, total_ref, *work_refs = other_lists
        lists.append((row_ref, total_ref, work_refs[0]))
        copy = pltpu.make_async_copy(other_rows, row_ref, row_sem)
        copy.start()
    else:
        lists.append(refs[:3])
        refs, (out_ref, query_ref, best_ref) = refs[3:-3], refs[-3:]
    pieces, passage_refs, add_ref, earlier = refs[:p], refs[p : p + 2], refs[p + 2], refs[p + 3 :]
    q_tok, width = query_ref.shape[2:]
    tok_slots = passage_refs[0].shape[1]
    per_source = best_ref.shape[0]
    lanes = pack * q_tok
    q_bits = q_tok.bit_length() - 1
    me, core = lax.axis_index("shard"), lax.axis_index("sub")
    if call == 1:
        query_ref[...] = pieces[0][...]
    else:
        for i, piece in enumerate(reversed(pieces)):
            query_ref[i] = piece[...]
    best_ref[...] = jnp.zeros_like(best_ref)
    token = lax.broadcasted_iota(jnp.int32, (tok_slots, lanes), 0)
    place = lax.shift_right_logical(lax.broadcasted_iota(jnp.int32, (1, lanes), 1), q_bits)
    blank = jnp.zeros((q_tok, width), query_ref.dtype)

    for which, passages in enumerate(passage_refs):
        meta_ref, total_ref, work_ref = lists[which]
        owner = core if which == 0 else 1 - core
        if call == 0 and which == 1:
            copy.wait()
            list_groups(tuple(map(len, calls)), pack, per_source, row_ref, total_ref, work_refs)
        total = total_ref[call]

        def one_step(first_group, groups):
            for j in range(groups):
                work = work_ref[first_group + j]
                i, g = lax.shift_right_logical(work, SHIFT), jnp.bitwise_and(work, (1 << SHIFT) - 1)
                shard = jnp.bitwise_xor(me, distance(call, i))
                rows, cols, limit = [], [], jnp.zeros((1, lanes), jnp.int32)
                for a in range(pack):
                    slot = g * pack + a
                    query, passage = meta_ref[shard, QUERY + slot], meta_ref[shard, PASSAGE + slot]
                    rows.append(jnp.concatenate([blank] * a + [query_ref[i, query]] + [blank] * (pack - 1 - a), axis=1))
                    cols.append(passages[passage])
                    limit = jnp.where(place == a, meta_ref[shard, LENGTH + slot], limit)
                sims = lax.dot_general(
                    jnp.concatenate(cols, axis=1), jnp.concatenate(rows, axis=0),
                    (((1,), (1,)), ((), ())), preferred_element_type=jnp.float32,
                )
                best = jnp.max(jnp.where(token < limit, sims, -1e30), axis=0, keepdims=True)
                best = jnp.where(place + g * pack < meta_ref[shard, COUNT], best, 0.0)
                best_ref[g, pl.ds(i * 2 + owner, 1), :] = best

        half = GROUPS // 2
        steps = lax.shift_right_logical(total + half - 1, GROUPS.bit_length() - 1)

        @pl.loop(0, steps)
        def _(step):
            one_step(step * GROUPS, GROUPS)

        @pl.when(total > steps * GROUPS)
        def _():
            one_step(steps * GROUPS, half)

    best = jnp.concatenate([best_ref[g] for g in range(per_source)], axis=1)
    high = best.astype(jnp.bfloat16)
    rest = best - high.astype(jnp.float32)
    middle = rest.astype(jnp.bfloat16)
    low = (rest - middle.astype(jnp.float32)).astype(jnp.bfloat16)
    parts = jnp.dot(jnp.concatenate([high, middle, low], axis=0), add_ref[...], preferred_element_type=jnp.float32)
    rows = best.shape[0]
    score = (parts[:rows] + parts[rows : 2 * rows] + parts[2 * rows :]) * (1.0 / q_tok)
    if call < 2:
        out_ref[...] = score[:, :cap]
        return
    for scores, at in zip((*(ref[...] for ref in earlier), score[:, :cap]), ((0, 1, *range(4, shards, 2)), (2, 3), distances)):
        for i, d in enumerate(at):
            out_ref[pl.ds((shards - 1 - jnp.bitwise_xor(me, d)) * 2, 2), :] = scores[2 * i : 2 * i + 2]


def pair_kernel(one_ref, other_ref, out_ref):
    out_ref[0] = one_ref[...]
    out_ref[1] = other_ref[...]


def order_kernel(back_ref, out_ref):
    shards = back_ref.shape[0] // 2
    for i in range(shards):
        out_ref[0, 2 * i : 2 * i + 2] = back_ref[2 * (shards - 1 - i) : 2 * (shards - i)]


def on_device(shards, queries, passages, passage_len, slot_query, slot_passage, slot_count):
    sources, _, cap = slot_query.shape
    q_dev, q_tok, width = queries.shape
    pack = 128 // q_tok
    per_source = -(-cap // pack)
    swap = [(0, 1), (1, 0)]
    vmem, hbm, smem, anywhere = (pl.BlockSpec(memory_space=space) for space in (pltpu.VMEM, pltpu.HBM, pltpu.SMEM, pl.ANY))
    params = pltpu.CompilerParams(vmem_limit_bytes=12 * 1024 * 1024)
    row = jax.ShapeDtypeStruct((shards, 128), jnp.int32)

    def placed(space, *arrays):
        return [pltpu.with_memory_space_constraint(x, space) for x in arrays]

    def swapped(piece, d):
        return lax.ppermute(piece, "shard", [(i, i ^ d) for i in range(shards)])

    pieces = [queries, swapped(queries, 1)] + [None] * (shards - 2)
    for d in range(4, shards, 2):
        pieces[d] = swapped(queries, d)
    other_passages = lax.ppermute(passages, "sub", swap)

    calls = ((0, 1, *range(4, shards, 2)), (2, 3), range(5, shards, 2))
    sizes = tuple(map(len, calls))
    listed = [
        pltpu.SMEM(row.shape, row.dtype),
        pltpu.SMEM((len(calls),), jnp.int32),
        *(pltpu.SMEM((n * per_source + 2 * GROUPS,), jnp.int32) for n in sizes),
    ]
    theirs, own_queries, own_passages, add, *own_lists = pl.pallas_call(
        functools.partial(pack_kernel, shards, sizes, pack, per_source),
        out_shape=[
            row, *(jax.ShapeDtypeStruct(x.shape, x.dtype) for x in (queries, passages)),
            jax.ShapeDtypeStruct((per_source * 128, 128), jnp.bfloat16), *listed,
        ],
        in_specs=[hbm] * 6,
        out_specs=[vmem] * 4 + [smem] * len(listed),
        scratch_shapes=[
            pltpu.VMEM(row.shape, row.dtype),
            pltpu.VMEM((sources, cap), jnp.int32),
            pltpu.VMEM((sources, cap), jnp.int32),
            pltpu.VMEM((sources,), jnp.int32),
            pltpu.VMEM(passage_len.shape, jnp.int32),
            pltpu.SemaphoreType.DMA((5,)),
            pltpu.SemaphoreType.DMA((CHUNKS,)),
            pltpu.SemaphoreType.DMA,
        ],
        compiler_params=params,
    )(*placed(pltpu.HBM, slot_query.reshape(sources, cap), slot_passage.reshape(sources, cap), slot_count.reshape(sources), passage_len, queries, passages))
    both = pl.pallas_call(
        pair_kernel,
        out_shape=jax.ShapeDtypeStruct((2, *queries.shape), queries.dtype),
        in_specs=[vmem] * 2,
        out_specs=vmem,
        compiler_params=params,
    )(own_queries, pieces[1])
    both = swapped(both, 2)
    for d in range(5, shards, 2):
        pieces[d] = swapped(pieces[d - 1], 1)
    theirs, _ = lax.optimization_barrier((theirs, pieces[1]))
    other = lax.ppermute(theirs, "sub", swap)

    def scored(parts, lists, *earlier):
        call = len(earlier)
        n = sizes[call]
        scores = jax.ShapeDtypeStruct((2 * n if call < 2 else sources, cap), jnp.float32)
        own_rows, own_totals, *own_works = own_lists
        of_own = placed(pltpu.SMEM, own_rows, own_totals, own_works[call])
        if call:
            rows, totals, *works = lists
            of_other, others = placed(pltpu.SMEM, rows, totals, works[call]), [smem] * 3
        else:
            of_other, others = lists, [anywhere]
        return pl.pallas_call(
            functools.partial(score_kernel, shards, calls, call, pack, cap),
            out_shape=scores if call else [scores, *listed],
            in_specs=[smem] * 3 + others + [vmem] * (len(parts) + 3 + call),
            out_specs=vmem if call else [vmem] + [smem] * len(listed),
            scratch_shapes=[
                pltpu.VMEM((n, *queries.shape), queries.dtype),
                pltpu.VMEM((per_source, 2 * n, 128), jnp.float32),
                *([] if call else [pltpu.SemaphoreType.DMA]),
            ],
            compiler_params=params,
            cost_estimate=pl.CostEstimate(flops=1_000_000_000, bytes_accessed=9_000_000, transcendentals=0),
        )(*of_own, *of_other, *parts, *placed(pltpu.VMEM, own_passages, other_passages), add, *earlier)

    pieces[0] = own_queries
    near, _, far = calls
    first_scores, *lists = scored([pieces[d] for d in reversed(near)], [other])
    next_scores = scored([both], lists, first_scores)
    scores = scored([pieces[d] for d in reversed(far)], lists, first_scores, next_scores)
    order = [list(reversed(range(shards)))]
    returned = lax.all_to_all(scores, "shard", split_axis=0, concat_axis=0, axis_index_groups=order, tiled=True)
    return pl.pallas_call(
        order_kernel,
        out_shape=jax.ShapeDtypeStruct((1, sources, cap), jnp.float32),
        in_specs=[vmem],
        out_specs=vmem,
        compiler_params=params,
    )(returned)


def solution(mesh):
    return jax.shard_map(
        functools.partial(on_device, mesh.shape["shard"]),
        mesh=mesh,
        in_specs=(
            P(("groups", "shard", "sub"), None, None),
            P(("shard", "sub"), None, None),
            P(("shard", "sub")),
            P("groups", ("shard", "sub"), None),
            P("groups", ("shard", "sub"), None),
            P("groups", ("shard", "sub")),
        ),
        out_specs=P(("groups", "shard", "sub"), None, None),
        check_vma=False,
    )
```

```python
import functools

import jax
import jax.numpy as jnp
from jax import lax
from jax.experimental import pallas as pl
from jax.experimental.pallas import tpu as pltpu
from jax.sharding import PartitionSpec as P

GROUPS = 8
CHUNKS = 8
SHIFT = 8
QUERY, PASSAGE, LENGTH, COUNT = 0, 32, 64, 96


def distance(call, i):
    return (jnp.where(i == 1, 1, i * 2), i + 2, i * 2 + 5)[call]


def list_groups(sizes, pack, per_source, row_ref, total_ref, work_refs):
    me = lax.axis_index("shard")
    for call, (n, work_ref) in enumerate(zip(sizes, work_refs)):

        def list_source(i, total):
            live = row_ref[jnp.bitwise_xor(me, distance(call, i)), COUNT]
            for g in range(per_source):
                work_ref[total + g] = (i << SHIFT) + g
            return total + lax.shift_right_logical(live + pack - 1, pack.bit_length() - 1)

        total = 0
        if n <= 8:
            for i in range(n):
                total = list_source(i, total)
        else:
            total = lax.fori_loop(0, n, list_source, 0)
        for g in range(GROUPS):
            work_ref[total + g] = 0
        total_ref[call] = total


def pack_kernel(shards, sizes, pack, per_source, *refs):
    query_hbm, passage_hbm, count_hbm, length_hbm, tokens_hbm, own_hbm, theirs_ref, tokens_ref, own_ref, add_ref = refs[:10]
    row_ref, total_ref, *work_refs = refs[10 : 12 + len(sizes)]
    mine_ref, query_ref, passage_ref, count_ref, length_ref, sems, own_sems, row_sem = refs[12 + len(sizes) :]
    copies = [
        pltpu.make_async_copy(src, dst, sems.at[i])
        for i, (src, dst) in enumerate(
            (
                (query_hbm, query_ref),
                (passage_hbm, passage_ref),
                (count_hbm, count_ref),
                (length_hbm, length_ref),
                (tokens_hbm, tokens_ref),
            )
        )
    ]
    size = own_ref.shape[0] // CHUNKS
    own_copies = [
        pltpu.make_async_copy(own_hbm.at[pl.ds(i * size, size)], own_ref.at[pl.ds(i * size, size)], own_sems.at[i])
        for i in range(CHUNKS)
    ]
    for copy in copies + own_copies:
        copy.start()
    row = lax.broadcasted_iota(jnp.int32, add_ref.shape, 0)
    col = lax.broadcasted_iota(jnp.int32, add_ref.shape, 1)
    q_bits = tokens_ref.shape[1].bit_length() - 1
    add_ref[...] = jnp.where(lax.shift_right_logical(row, q_bits) == col, 1.0, 0.0).astype(add_ref.dtype)
    for copy in copies:
        copy.wait()
    cap = query_ref.shape[1]
    lengths = length_ref[...].reshape(1, -1)
    counts = jnp.broadcast_to(count_ref[...].reshape(1, -1), (2 * shards, 2 * shards))
    row = lax.broadcasted_iota(jnp.int32, counts.shape, 0)
    col = lax.broadcasted_iota(jnp.int32, counts.shape, 1)
    counts = jnp.sum(jnp.where(row == col, counts, 0), axis=1, keepdims=True)
    blank = jnp.zeros((2 * shards, 32 - cap), jnp.int32)
    passage = jnp.concatenate([passage_ref[...], blank], axis=1)
    passage = jnp.concatenate([passage] * 4, axis=1)
    length = jnp.take_along_axis(jnp.broadcast_to(lengths, passage.shape), passage, axis=1)
    query = jnp.concatenate([jnp.concatenate([query_ref[...], blank], axis=1)] * 4, axis=1)
    lane = lax.broadcasted_iota(jnp.int32, passage.shape, 1)
    packed = jnp.where(lane < PASSAGE, query, jnp.where(lane < LENGTH, passage, jnp.where(lane < COUNT, length, counts)))
    packed = packed.reshape(shards, 2, 128)
    first = lax.axis_index("sub") == 0
    mine_ref[...] = jnp.where(first, packed[:, 0], packed[:, 1])
    theirs_ref[...] = jnp.where(first, packed[:, 1], packed[:, 0])
    copy = pltpu.make_async_copy(mine_ref, row_ref, row_sem)
    copy.start()
    copy.wait()
    list_groups(sizes, pack, per_source, row_ref, total_ref, work_refs)
    for copy in own_copies:
        copy.wait()


def score_kernel(shards, calls, call, pack, cap, *refs):
    distances = calls[call]
    n = len(distances)
    p = 1 if call == 1 else n
    lists, refs = [refs[:3]], refs[3:]
    if call == 0:
        other_rows, refs = refs[0], refs[1:]
        refs, (out_ref, *other_lists, query_ref, best_ref, row_sem) = refs[: p + 3], refs[p + 3 :]
        row_ref, total_ref, *work_refs = other_lists
        lists.append((row_ref, total_ref, work_refs[0]))
        copy = pltpu.make_async_copy(other_rows, row_ref, row_sem)
        copy.start()
    else:
        lists.append(refs[:3])
        refs, (out_ref, query_ref, best_ref) = refs[3:-3], refs[-3:]
    pieces, passage_refs, add_ref, earlier = refs[:p], refs[p : p + 2], refs[p + 2], refs[p + 3 :]
    q_tok, width = query_ref.shape[2:]
    tok_slots = passage_refs[0].shape[1]
    per_source = best_ref.shape[0]
    lanes = pack * q_tok
    q_bits = q_tok.bit_length() - 1
    me, core = lax.axis_index("shard"), lax.axis_index("sub")
    if call == 1:
        query_ref[...] = pieces[0][...]
    else:
        for i, piece in enumerate(reversed(pieces)):
            query_ref[i] = piece[...]
    best_ref[...] = jnp.zeros_like(best_ref)
    token = lax.broadcasted_iota(jnp.int32, (tok_slots, lanes), 0)
    place = lax.shift_right_logical(lax.broadcasted_iota(jnp.int32, (1, lanes), 1), q_bits)
    blank = jnp.zeros((q_tok, width), query_ref.dtype)

    for which, passages in enumerate(passage_refs):
        meta_ref, total_ref, work_ref = lists[which]
        owner = core if which == 0 else 1 - core
        if call == 0 and which == 1:
            copy.wait()
            list_groups(tuple(map(len, calls)), pack, per_source, row_ref, total_ref, work_refs)
        total = total_ref[call]

        def one_step(first_group, groups):
            for j in range(groups):
                work = work_ref[first_group + j]
                i, g = lax.shift_right_logical(work, SHIFT), jnp.bitwise_and(work, (1 << SHIFT) - 1)
                shard = jnp.bitwise_xor(me, distance(call, i))
                rows, cols, limit = [], [], jnp.zeros((1, lanes), jnp.int32)
                for a in range(pack):
                    slot = g * pack + a
                    query, passage = meta_ref[shard, QUERY + slot], meta_ref[shard, PASSAGE + slot]
                    rows.append(jnp.concatenate([blank] * a + [query_ref[i, query]] + [blank] * (pack - 1 - a), axis=1))
                    cols.append(passages[passage])
                    limit = jnp.where(place == a, meta_ref[shard, LENGTH + slot], limit)
                sims = lax.dot_general(
                    jnp.concatenate(cols, axis=1), jnp.concatenate(rows, axis=0),
                    (((1,), (1,)), ((), ())), preferred_element_type=jnp.float32,
                )
                best = jnp.max(jnp.where(token < limit, sims, -1e30), axis=0, keepdims=True)
                best = jnp.where(place + g * pack < meta_ref[shard, COUNT], best, 0.0)
                best_ref[g, pl.ds(i * 2 + owner, 1), :] = best

        half = GROUPS // 2
        steps = lax.shift_right_logical(total + half - 1, GROUPS.bit_length() - 1)

        @pl.loop(0, steps)
        def _(step):
            one_step(step * GROUPS, GROUPS)

        @pl.when(total > steps * GROUPS)
        def _():
            one_step(steps * GROUPS, half)

    best = jnp.concatenate([best_ref[g] for g in range(per_source)], axis=1)
    high = best.astype(jnp.bfloat16)
    rest = best - high.astype(jnp.float32)
    middle = rest.astype(jnp.bfloat16)
    low = (rest - middle.astype(jnp.float32)).astype(jnp.bfloat16)
    parts = jnp.dot(jnp.concatenate([high, middle, low], axis=0), add_ref[...], preferred_element_type=jnp.float32)
    rows = best.shape[0]
    score = (parts[:rows] + parts[rows : 2 * rows] + parts[2 * rows :]) * (1.0 / q_tok)
    if call < 2:
        out_ref[...] = score[:, :cap]
        return
    for scores, at in zip((*(ref[...] for ref in earlier), score[:, :cap]), ((0, 1, *range(4, shards, 2)), (2, 3), distances)):
        for i, d in enumerate(at):
            out_ref[pl.ds((shards - 1 - jnp.bitwise_xor(me, d)) * 2, 2), :] = scores[2 * i : 2 * i + 2]


def pair_kernel(one_ref, other_ref, out_ref):
    out_ref[0] = one_ref[...]
    out_ref[1] = other_ref[...]


def order_kernel(back_ref, out_ref):
    shards = back_ref.shape[0] // 2
    for i in range(shards):
        out_ref[0, 2 * i : 2 * i + 2] = back_ref[2 * (shards - 1 - i) : 2 * (shards - i)]


def on_device(shards, queries, passages, passage_len, slot_query, slot_passage, slot_count):
    sources, _, cap = slot_query.shape
    q_dev, q_tok, width = queries.shape
    pack = 128 // q_tok
    per_source = -(-cap // pack)
    swap = [(0, 1), (1, 0)]
    vmem, hbm, smem, anywhere = (pl.BlockSpec(memory_space=space) for space in (pltpu.VMEM, pltpu.HBM, pltpu.SMEM, pl.ANY))
    params = pltpu.CompilerParams(vmem_limit_bytes=12 * 1024 * 1024)
    row = jax.ShapeDtypeStruct((shards, 128), jnp.int32)

    def placed(space, *arrays):
        return [pltpu.with_memory_space_constraint(x, space) for x in arrays]

    def swapped(piece, d):
        return lax.ppermute(piece, "shard", [(i, i ^ d) for i in range(shards)])

    pieces = [queries, swapped(queries, 1)] + [None] * (shards - 2)
    for d in range(4, shards, 2):
        pieces[d] = swapped(queries, d)
    other_passages = lax.ppermute(passages, "sub", swap)

    calls = ((0, 1, *range(4, shards, 2)), (2, 3), range(5, shards, 2))
    sizes = tuple(map(len, calls))
    listed = [
        pltpu.SMEM(row.shape, row.dtype),
        pltpu.SMEM((len(calls),), jnp.int32),
        *(pltpu.SMEM((n * per_source + 2 * GROUPS,), jnp.int32) for n in sizes),
    ]
    theirs, own_queries, own_passages, add, *own_lists = pl.pallas_call(
        functools.partial(pack_kernel, shards, sizes, pack, per_source),
        out_shape=[
            row, *(jax.ShapeDtypeStruct(x.shape, x.dtype) for x in (queries, passages)),
            jax.ShapeDtypeStruct((per_source * 128, 128), jnp.bfloat16), *listed,
        ],
        in_specs=[hbm] * 6,
        out_specs=[vmem] * 4 + [smem] * len(listed),
        scratch_shapes=[
            pltpu.VMEM(row.shape, row.dtype),
            pltpu.VMEM((sources, cap), jnp.int32),
            pltpu.VMEM((sources, cap), jnp.int32),
            pltpu.VMEM((sources,), jnp.int32),
            pltpu.VMEM(passage_len.shape, jnp.int32),
            pltpu.SemaphoreType.DMA((5,)),
            pltpu.SemaphoreType.DMA((CHUNKS,)),
            pltpu.SemaphoreType.DMA,
        ],
        compiler_params=params,
    )(*placed(pltpu.HBM, slot_query.reshape(sources, cap), slot_passage.reshape(sources, cap), slot_count.reshape(sources), passage_len, queries, passages))
    both = pl.pallas_call(
        pair_kernel,
        out_shape=jax.ShapeDtypeStruct((2, *queries.shape), queries.dtype),
        in_specs=[vmem] * 2,
        out_specs=vmem,
        compiler_params=params,
    )(own_queries, pieces[1])
    both = swapped(both, 2)
    for d in range(5, shards, 2):
        pieces[d] = swapped(pieces[1], d - 1) if d == shards - 1 else swapped(pieces[d - 1], 1)
    theirs, _ = lax.optimization_barrier((theirs, other_passages))
    other = lax.ppermute(theirs, "sub", swap)

    def scored(parts, lists, *earlier):
        call = len(earlier)
        n = sizes[call]
        scores = jax.ShapeDtypeStruct((2 * n if call < 2 else sources, cap), jnp.float32)
        own_rows, own_totals, *own_works = own_lists
        of_own = placed(pltpu.SMEM, own_rows, own_totals, own_works[call])
        if call:
            rows, totals, *works = lists
            of_other, others = placed(pltpu.SMEM, rows, totals, works[call]), [smem] * 3
        else:
            of_other, others = lists, [anywhere]
        return pl.pallas_call(
            functools.partial(score_kernel, shards, calls, call, pack, cap),
            out_shape=scores if call else [scores, *listed],
            in_specs=[smem] * 3 + others + [vmem] * (len(parts) + 3 + call),
            out_specs=vmem if call else [vmem] + [smem] * len(listed),
            scratch_shapes=[
                pltpu.VMEM((n, *queries.shape), queries.dtype),
                pltpu.VMEM((per_source, 2 * n, 128), jnp.float32),
                *([] if call else [pltpu.SemaphoreType.DMA]),
            ],
            compiler_params=params,
            cost_estimate=pl.CostEstimate(flops=1_000_000_000, bytes_accessed=9_000_000, transcendentals=0),
        )(*of_own, *of_other, *parts, *placed(pltpu.VMEM, own_passages, other_passages), add, *earlier)

    pieces[0] = own_queries
    near, _, far = calls
    first_scores, *lists = scored([pieces[d] for d in reversed(near)], [other])
    next_scores = scored([both], lists, first_scores)
    scores = scored([pieces[d] for d in reversed(far)], lists, first_scores, next_scores)
    order = [list(reversed(range(shards)))]
    returned = lax.all_to_all(scores, "shard", split_axis=0, concat_axis=0, axis_index_groups=order, tiled=True)
    return pl.pallas_call(
        order_kernel,
        out_shape=jax.ShapeDtypeStruct((1, sources, cap), jnp.float32),
        in_specs=[vmem],
        out_specs=vmem,
        compiler_params=params,
    )(returned)


def solution(mesh):
    return jax.shard_map(
        functools.partial(on_device, mesh.shape["shard"]),
        mesh=mesh,
        in_specs=(
            P(("groups", "shard", "sub"), None, None),
            P(("shard", "sub"), None, None),
            P(("shard", "sub")),
            P("groups", ("shard", "sub"), None),
            P("groups", ("shard", "sub"), None),
            P("groups", ("shard", "sub")),
        ),
        out_specs=P(("groups", "shard", "sub"), None, None),
        check_vma=False,
    )
```

```python
import functools

import jax
import jax.numpy as jnp
from jax import lax
from jax.experimental import pallas as pl
from jax.experimental.pallas import tpu as pltpu
from jax.sharding import PartitionSpec as P

GROUPS = 8
CHUNKS = 8
SHIFT = 8
QUERY, PASSAGE, LENGTH, COUNT = 0, 32, 64, 96


def distance(call, i):
    return (jnp.where(i == 1, 1, i * 2), i + 2, i * 2 + 5)[call]


def list_groups(sizes, pack, per_source, row_ref, total_ref, work_refs):
    me = lax.axis_index("shard")
    for call, (n, work_ref) in enumerate(zip(sizes, work_refs)):

        def list_source(i, total):
            live = row_ref[jnp.bitwise_xor(me, distance(call, i)), COUNT]
            for g in range(per_source):
                work_ref[total + g] = (i << SHIFT) + g
            return total + lax.shift_right_logical(live + pack - 1, pack.bit_length() - 1)

        total = 0
        if n <= 8:
            for i in range(n):
                total = list_source(i, total)
        else:
            total = lax.fori_loop(0, n, list_source, 0)
        for g in range(GROUPS):
            work_ref[total + g] = 0
        total_ref[call] = total


def pack_kernel(shards, sizes, pack, per_source, *refs):
    query_hbm, passage_hbm, count_hbm, length_hbm, tokens_hbm, own_hbm, theirs_ref, tokens_ref, own_ref, add_ref = refs[:10]
    row_ref, total_ref, *work_refs = refs[10 : 12 + len(sizes)]
    mine_ref, query_ref, passage_ref, count_ref, length_ref, sems, own_sems, row_sem = refs[12 + len(sizes) :]
    copies = [
        pltpu.make_async_copy(src, dst, sems.at[i])
        for i, (src, dst) in enumerate(
            (
                (query_hbm, query_ref),
                (passage_hbm, passage_ref),
                (count_hbm, count_ref),
                (length_hbm, length_ref),
                (tokens_hbm, tokens_ref),
            )
        )
    ]
    size = own_ref.shape[0] // CHUNKS
    own_copies = [
        pltpu.make_async_copy(own_hbm.at[pl.ds(i * size, size)], own_ref.at[pl.ds(i * size, size)], own_sems.at[i])
        for i in range(CHUNKS)
    ]
    for copy in copies + own_copies[: CHUNKS // 4]:
        copy.start()
    row = lax.broadcasted_iota(jnp.int32, add_ref.shape, 0)
    col = lax.broadcasted_iota(jnp.int32, add_ref.shape, 1)
    q_bits = tokens_ref.shape[1].bit_length() - 1
    add_ref[...] = jnp.where(lax.shift_right_logical(row, q_bits) == col, 1.0, 0.0).astype(add_ref.dtype)
    for copy in copies:
        copy.wait()
    cap = query_ref.shape[1]
    lengths = length_ref[...].reshape(1, -1)
    counts = jnp.broadcast_to(count_ref[...].reshape(1, -1), (2 * shards, 2 * shards))
    row = lax.broadcasted_iota(jnp.int32, counts.shape, 0)
    col = lax.broadcasted_iota(jnp.int32, counts.shape, 1)
    counts = jnp.sum(jnp.where(row == col, counts, 0), axis=1, keepdims=True)
    blank = jnp.zeros((2 * shards, 32 - cap), jnp.int32)
    passage = jnp.concatenate([passage_ref[...], blank], axis=1)
    passage = jnp.concatenate([passage] * 4, axis=1)
    length = jnp.take_along_axis(jnp.broadcast_to(lengths, passage.shape), passage, axis=1)
    query = jnp.concatenate([jnp.concatenate([query_ref[...], blank], axis=1)] * 4, axis=1)
    lane = lax.broadcasted_iota(jnp.int32, passage.shape, 1)
    packed = jnp.where(lane < PASSAGE, query, jnp.where(lane < LENGTH, passage, jnp.where(lane < COUNT, length, counts)))
    packed = packed.reshape(shards, 2, 128)
    first = lax.axis_index("sub") == 0
    mine_ref[...] = jnp.where(first, packed[:, 0], packed[:, 1])
    theirs_ref[...] = jnp.where(first, packed[:, 1], packed[:, 0])
    copy = pltpu.make_async_copy(mine_ref, row_ref, row_sem)
    copy.start()
    for own_copy in own_copies[CHUNKS // 4 :]:
        own_copy.start()
    copy.wait()
    list_groups(sizes, pack, per_source, row_ref, total_ref, work_refs)
    for copy in own_copies:
        copy.wait()


def score_kernel(shards, calls, call, pack, cap, *refs):
    distances = calls[call]
    n = len(distances)
    p = 1 if call == 1 else n
    lists, refs = [refs[:3]], refs[3:]
    if call == 0:
        other_rows, refs = refs[0], refs[1:]
        refs, (out_ref, *other_lists, query_ref, best_ref, row_sem) = refs[: p + 3], refs[p + 3 :]
        row_ref, total_ref, *work_refs = other_lists
        lists.append((row_ref, total_ref, work_refs[0]))
        copy = pltpu.make_async_copy(other_rows, row_ref, row_sem)
        copy.start()
    else:
        lists.append(refs[:3])
        refs, (out_ref, query_ref, best_ref) = refs[3:-3], refs[-3:]
    pieces, passage_refs, add_ref, earlier = refs[:p], refs[p : p + 2], refs[p + 2], refs[p + 3 :]
    q_tok, width = query_ref.shape[2:]
    tok_slots = passage_refs[0].shape[1]
    per_source = best_ref.shape[0]
    lanes = pack * q_tok
    q_bits = q_tok.bit_length() - 1
    me, core = lax.axis_index("shard"), lax.axis_index("sub")
    if call == 1:
        query_ref[...] = pieces[0][...]
    else:
        for i, piece in enumerate(reversed(pieces)):
            query_ref[i] = piece[...]
    best_ref[...] = jnp.zeros_like(best_ref)
    token = lax.broadcasted_iota(jnp.int32, (tok_slots, lanes), 0)
    place = lax.shift_right_logical(lax.broadcasted_iota(jnp.int32, (1, lanes), 1), q_bits)
    blank = jnp.zeros((q_tok, width), query_ref.dtype)

    for which, passages in enumerate(passage_refs):
        meta_ref, total_ref, work_ref = lists[which]
        owner = core if which == 0 else 1 - core
        if call == 0 and which == 1:
            copy.wait()
            list_groups(tuple(map(len, calls)), pack, per_source, row_ref, total_ref, work_refs)
        total = total_ref[call]

        def one_step(first_group, groups):
            for j in range(groups):
                work = work_ref[first_group + j]
                i, g = lax.shift_right_logical(work, SHIFT), jnp.bitwise_and(work, (1 << SHIFT) - 1)
                shard = jnp.bitwise_xor(me, distance(call, i))
                rows, cols, limit = [], [], jnp.zeros((1, lanes), jnp.int32)
                for a in range(pack):
                    slot = g * pack + a
                    query, passage = meta_ref[shard, QUERY + slot], meta_ref[shard, PASSAGE + slot]
                    rows.append(jnp.concatenate([blank] * a + [query_ref[i, query]] + [blank] * (pack - 1 - a), axis=1))
                    cols.append(passages[passage])
                    limit = jnp.where(place == a, meta_ref[shard, LENGTH + slot], limit)
                sims = lax.dot_general(
                    jnp.concatenate(cols, axis=1), jnp.concatenate(rows, axis=0),
                    (((1,), (1,)), ((), ())), preferred_element_type=jnp.float32,
                )
                best = jnp.max(jnp.where(token < limit, sims, -1e30), axis=0, keepdims=True)
                best = jnp.where(place + g * pack < meta_ref[shard, COUNT], best, 0.0)
                best_ref[g, pl.ds(i * 2 + owner, 1), :] = best

        half = GROUPS // 2
        steps = lax.shift_right_logical(total + half - 1, GROUPS.bit_length() - 1)

        @pl.loop(0, steps)
        def _(step):
            one_step(step * GROUPS, GROUPS)

        @pl.when(total > steps * GROUPS)
        def _():
            one_step(steps * GROUPS, half)

    best = jnp.concatenate([best_ref[g] for g in range(per_source)], axis=1)
    high = best.astype(jnp.bfloat16)
    rest = best - high.astype(jnp.float32)
    middle = rest.astype(jnp.bfloat16)
    low = (rest - middle.astype(jnp.float32)).astype(jnp.bfloat16)
    parts = jnp.dot(jnp.concatenate([high, middle, low], axis=0), add_ref[...], preferred_element_type=jnp.float32)
    rows = best.shape[0]
    score = (parts[:rows] + parts[rows : 2 * rows] + parts[2 * rows :]) * (1.0 / q_tok)
    if call < 2:
        out_ref[...] = score[:, :cap]
        return
    for scores, at in zip((*(ref[...] for ref in earlier), score[:, :cap]), ((0, 1, *range(4, shards, 2)), (2, 3), distances)):
        for i, d in enumerate(at):
            out_ref[pl.ds((shards - 1 - jnp.bitwise_xor(me, d)) * 2, 2), :] = scores[2 * i : 2 * i + 2]


def pair_kernel(one_ref, other_ref, out_ref):
    out_ref[0] = one_ref[...]
    out_ref[1] = other_ref[...]


def order_kernel(back_ref, out_ref):
    shards = back_ref.shape[0] // 2
    for i in range(shards):
        out_ref[0, 2 * i : 2 * i + 2] = back_ref[2 * (shards - 1 - i) : 2 * (shards - i)]


def on_device(shards, queries, passages, passage_len, slot_query, slot_passage, slot_count):
    sources, _, cap = slot_query.shape
    q_dev, q_tok, width = queries.shape
    pack = 128 // q_tok
    per_source = -(-cap // pack)
    swap = [(0, 1), (1, 0)]
    vmem, hbm, smem, anywhere = (pl.BlockSpec(memory_space=space) for space in (pltpu.VMEM, pltpu.HBM, pltpu.SMEM, pl.ANY))
    params = pltpu.CompilerParams(vmem_limit_bytes=12 * 1024 * 1024)
    row = jax.ShapeDtypeStruct((shards, 128), jnp.int32)

    def placed(space, *arrays):
        return [pltpu.with_memory_space_constraint(x, space) for x in arrays]

    def swapped(piece, d):
        return lax.ppermute(piece, "shard", [(i, i ^ d) for i in range(shards)])

    pieces = [queries, swapped(queries, 1)] + [None] * (shards - 2)
    for d in range(4, shards, 2):
        pieces[d] = swapped(queries, d)
    other_passages = lax.ppermute(passages, "sub", swap)

    calls = ((0, 1, *range(4, shards, 2)), (2, 3), range(5, shards, 2))
    sizes = tuple(map(len, calls))
    listed = [
        pltpu.SMEM(row.shape, row.dtype),
        pltpu.SMEM((len(calls),), jnp.int32),
        *(pltpu.SMEM((n * per_source + 2 * GROUPS,), jnp.int32) for n in sizes),
    ]
    theirs, own_queries, own_passages, add, *own_lists = pl.pallas_call(
        functools.partial(pack_kernel, shards, sizes, pack, per_source),
        out_shape=[
            row, *(jax.ShapeDtypeStruct(x.shape, x.dtype) for x in (queries, passages)),
            jax.ShapeDtypeStruct((per_source * 128, 128), jnp.bfloat16), *listed,
        ],
        in_specs=[hbm] * 6,
        out_specs=[vmem] * 4 + [smem] * len(listed),
        scratch_shapes=[
            pltpu.VMEM(row.shape, row.dtype),
            pltpu.VMEM((sources, cap), jnp.int32),
            pltpu.VMEM((sources, cap), jnp.int32),
            pltpu.VMEM((sources,), jnp.int32),
            pltpu.VMEM(passage_len.shape, jnp.int32),
            pltpu.SemaphoreType.DMA((5,)),
            pltpu.SemaphoreType.DMA((CHUNKS,)),
            pltpu.SemaphoreType.DMA,
        ],
        compiler_params=params,
    )(*placed(pltpu.HBM, slot_query.reshape(sources, cap), slot_passage.reshape(sources, cap), slot_count.reshape(sources), passage_len, queries, passages))
    both = pl.pallas_call(
        pair_kernel,
        out_shape=jax.ShapeDtypeStruct((2, *queries.shape), queries.dtype),
        in_specs=[vmem] * 2,
        out_specs=vmem,
        compiler_params=params,
    )(own_queries, pieces[1])
    both = swapped(both, 2)
    for d in range(5, shards, 2):
        pieces[d] = swapped(pieces[1], d - 1) if d == shards - 1 else swapped(pieces[d - 1], 1)
    theirs, _ = lax.optimization_barrier((theirs, other_passages))
    other = lax.ppermute(theirs, "sub", swap)

    def scored(parts, lists, *earlier):
        call = len(earlier)
        n = sizes[call]
        scores = jax.ShapeDtypeStruct((2 * n if call < 2 else sources, cap), jnp.float32)
        own_rows, own_totals, *own_works = own_lists
        of_own = placed(pltpu.SMEM, own_rows, own_totals, own_works[call])
        if call:
            rows, totals, *works = lists
            of_other, others = placed(pltpu.SMEM, rows, totals, works[call]), [smem] * 3
        else:
            of_other, others = lists, [anywhere]
        return pl.pallas_call(
            functools.partial(score_kernel, shards, calls, call, pack, cap),
            out_shape=scores if call else [scores, *listed],
            in_specs=[smem] * 3 + others + [vmem] * (len(parts) + 3 + call),
            out_specs=vmem if call else [vmem] + [smem] * len(listed),
            scratch_shapes=[
                pltpu.VMEM((n, *queries.shape), queries.dtype),
                pltpu.VMEM((per_source, 2 * n, 128), jnp.float32),
                *([] if call else [pltpu.SemaphoreType.DMA]),
            ],
            compiler_params=params,
            cost_estimate=pl.CostEstimate(flops=1_000_000_000, bytes_accessed=9_000_000, transcendentals=0),
        )(*of_own, *of_other, *parts, *placed(pltpu.VMEM, own_passages, other_passages), add, *earlier)

    pieces[0] = own_queries
    near, _, far = calls
    first_scores, *lists = scored([pieces[d] for d in reversed(near)], [other])
    next_scores = scored([both], lists, first_scores)
    scores = scored([pieces[d] for d in reversed(far)], lists, first_scores, next_scores)
    order = [list(reversed(range(shards)))]
    returned = lax.all_to_all(scores, "shard", split_axis=0, concat_axis=0, axis_index_groups=order, tiled=True)
    return pl.pallas_call(
        order_kernel,
        out_shape=jax.ShapeDtypeStruct((1, sources, cap), jnp.float32),
        in_specs=[vmem],
        out_specs=vmem,
        compiler_params=params,
    )(returned)


def solution(mesh):
    return jax.shard_map(
        functools.partial(on_device, mesh.shape["shard"]),
        mesh=mesh,
        in_specs=(
            P(("groups", "shard", "sub"), None, None),
            P(("shard", "sub"), None, None),
            P(("shard", "sub")),
            P("groups", ("shard", "sub"), None),
            P("groups", ("shard", "sub"), None),
            P("groups", ("shard", "sub")),
        ),
        out_specs=P(("groups", "shard", "sub"), None, None),
        check_vma=False,
    )
```

```python
import functools

import jax
import jax.numpy as jnp
from jax import lax
from jax.experimental import pallas as pl
from jax.experimental.pallas import tpu as pltpu
from jax.sharding import PartitionSpec as P

GROUPS = 8
CHUNKS = 8
EARLY = 5
SHIFT = 8
QUERY, PASSAGE, LENGTH, COUNT = 0, 32, 64, 96


def distance(call, i):
    return (jnp.where(i == 1, 1, i * 2), i + 2, i * 2 + 5)[call]


def list_groups(sizes, pack, per_source, row_ref, total_ref, work_refs):
    me = lax.axis_index("shard")
    for call, (n, work_ref) in enumerate(zip(sizes, work_refs)):

        def list_source(i, total):
            live = row_ref[jnp.bitwise_xor(me, distance(call, i)), COUNT]
            for g in range(per_source):
                work_ref[total + g] = (i << SHIFT) + g
            return total + lax.shift_right_logical(live + pack - 1, pack.bit_length() - 1)

        total = 0
        if n <= 8:
            for i in range(n):
                total = list_source(i, total)
        else:
            total = lax.fori_loop(0, n, list_source, 0)
        for g in range(GROUPS):
            work_ref[total + g] = 0
        total_ref[call] = total


def pack_kernel(shards, sizes, pack, per_source, *refs):
    query_hbm, passage_hbm, count_hbm, length_hbm, tokens_hbm, own_hbm, theirs_ref, tokens_ref, own_ref, add_ref = refs[:10]
    row_ref, total_ref, *work_refs = refs[10 : 12 + len(sizes)]
    mine_ref, query_ref, passage_ref, count_ref, length_ref, sems, own_sems, row_sem = refs[12 + len(sizes) :]
    copies = [
        pltpu.make_async_copy(src, dst, sems.at[i])
        for i, (src, dst) in enumerate(
            (
                (query_hbm, query_ref),
                (passage_hbm, passage_ref),
                (count_hbm, count_ref),
                (length_hbm, length_ref),
                (tokens_hbm, tokens_ref),
            )
        )
    ]
    size = own_ref.shape[0] // CHUNKS
    own_copies = [
        pltpu.make_async_copy(own_hbm.at[pl.ds(i * size, size)], own_ref.at[pl.ds(i * size, size)], own_sems.at[i])
        for i in range(CHUNKS)
    ]
    for copy in copies + own_copies[: EARLY]:
        copy.start()
    row = lax.broadcasted_iota(jnp.int32, add_ref.shape, 0)
    col = lax.broadcasted_iota(jnp.int32, add_ref.shape, 1)
    q_bits = tokens_ref.shape[1].bit_length() - 1
    add_ref[...] = jnp.where(lax.shift_right_logical(row, q_bits) == col, 1.0, 0.0).astype(add_ref.dtype)
    for copy in copies:
        copy.wait()
    cap = query_ref.shape[1]
    lengths = length_ref[...].reshape(1, -1)
    counts = jnp.broadcast_to(count_ref[...].reshape(1, -1), (2 * shards, 2 * shards))
    row = lax.broadcasted_iota(jnp.int32, counts.shape, 0)
    col = lax.broadcasted_iota(jnp.int32, counts.shape, 1)
    counts = jnp.sum(jnp.where(row == col, counts, 0), axis=1, keepdims=True)
    blank = jnp.zeros((2 * shards, 32 - cap), jnp.int32)
    passage = jnp.concatenate([passage_ref[...], blank], axis=1)
    passage = jnp.concatenate([passage] * 4, axis=1)
    length = jnp.take_along_axis(jnp.broadcast_to(lengths, passage.shape), passage, axis=1)
    query = jnp.concatenate([jnp.concatenate([query_ref[...], blank], axis=1)] * 4, axis=1)
    lane = lax.broadcasted_iota(jnp.int32, passage.shape, 1)
    packed = jnp.where(lane < PASSAGE, query, jnp.where(lane < LENGTH, passage, jnp.where(lane < COUNT, length, counts)))
    packed = packed.reshape(shards, 2, 128)
    first = lax.axis_index("sub") == 0
    mine_ref[...] = jnp.where(first, packed[:, 0], packed[:, 1])
    theirs_ref[...] = jnp.where(first, packed[:, 1], packed[:, 0])
    copy = pltpu.make_async_copy(mine_ref, row_ref, row_sem)
    copy.start()
    for own_copy in own_copies[EARLY :]:
        own_copy.start()
    copy.wait()
    list_groups(sizes, pack, per_source, row_ref, total_ref, work_refs)
    for copy in own_copies:
        copy.wait()


def score_kernel(shards, calls, call, pack, cap, *refs):
    distances = calls[call]
    n = len(distances)
    p = 1 if call == 1 else n
    lists, refs = [refs[:3]], refs[3:]
    if call == 0:
        other_rows, refs = refs[0], refs[1:]
        refs, (out_ref, *other_lists, query_ref, best_ref, row_sem) = refs[: p + 3], refs[p + 3 :]
        row_ref, total_ref, *work_refs = other_lists
        lists.append((row_ref, total_ref, work_refs[0]))
        copy = pltpu.make_async_copy(other_rows, row_ref, row_sem)
        copy.start()
    else:
        lists.append(refs[:3])
        refs, (out_ref, query_ref, best_ref) = refs[3:-3], refs[-3:]
    pieces, passage_refs, add_ref, earlier = refs[:p], refs[p : p + 2], refs[p + 2], refs[p + 3 :]
    q_tok, width = query_ref.shape[2:]
    tok_slots = passage_refs[0].shape[1]
    per_source = best_ref.shape[0]
    lanes = pack * q_tok
    q_bits = q_tok.bit_length() - 1
    me, core = lax.axis_index("shard"), lax.axis_index("sub")
    if call == 1:
        query_ref[...] = pieces[0][...]
    else:
        for i, piece in enumerate(reversed(pieces)):
            query_ref[i] = piece[...]
    best_ref[...] = jnp.zeros_like(best_ref)
    token = lax.broadcasted_iota(jnp.int32, (tok_slots, lanes), 0)
    place = lax.shift_right_logical(lax.broadcasted_iota(jnp.int32, (1, lanes), 1), q_bits)
    blank = jnp.zeros((q_tok, width), query_ref.dtype)

    for which, passages in enumerate(passage_refs):
        meta_ref, total_ref, work_ref = lists[which]
        owner = core if which == 0 else 1 - core
        if call == 0 and which == 1:
            copy.wait()
            list_groups(tuple(map(len, calls)), pack, per_source, row_ref, total_ref, work_refs)
        total = total_ref[call]

        def one_step(first_group, groups):
            for j in range(groups):
                work = work_ref[first_group + j]
                i, g = lax.shift_right_logical(work, SHIFT), jnp.bitwise_and(work, (1 << SHIFT) - 1)
                shard = jnp.bitwise_xor(me, distance(call, i))
                rows, cols, limit = [], [], jnp.zeros((1, lanes), jnp.int32)
                for a in range(pack):
                    slot = g * pack + a
                    query, passage = meta_ref[shard, QUERY + slot], meta_ref[shard, PASSAGE + slot]
                    rows.append(jnp.concatenate([blank] * a + [query_ref[i, query]] + [blank] * (pack - 1 - a), axis=1))
                    cols.append(passages[passage])
                    limit = jnp.where(place == a, meta_ref[shard, LENGTH + slot], limit)
                sims = lax.dot_general(
                    jnp.concatenate(cols, axis=1), jnp.concatenate(rows, axis=0),
                    (((1,), (1,)), ((), ())), preferred_element_type=jnp.float32,
                )
                best = jnp.max(jnp.where(token < limit, sims, -1e30), axis=0, keepdims=True)
                best = jnp.where(place + g * pack < meta_ref[shard, COUNT], best, 0.0)
                best_ref[g, pl.ds(i * 2 + owner, 1), :] = best

        half = GROUPS // 2
        steps = lax.shift_right_logical(total + half - 1, GROUPS.bit_length() - 1)

        @pl.loop(0, steps)
        def _(step):
            one_step(step * GROUPS, GROUPS)

        @pl.when(total > steps * GROUPS)
        def _():
            one_step(steps * GROUPS, half)

    best = jnp.concatenate([best_ref[g] for g in range(per_source)], axis=1)
    high = best.astype(jnp.bfloat16)
    rest = best - high.astype(jnp.float32)
    middle = rest.astype(jnp.bfloat16)
    low = (rest - middle.astype(jnp.float32)).astype(jnp.bfloat16)
    parts = jnp.dot(jnp.concatenate([high, middle, low], axis=0), add_ref[...], preferred_element_type=jnp.float32)
    rows = best.shape[0]
    score = (parts[:rows] + parts[rows : 2 * rows] + parts[2 * rows :]) * (1.0 / q_tok)
    if call < 2:
        out_ref[...] = score[:, :cap]
        return
    for scores, at in zip((*(ref[...] for ref in earlier), score[:, :cap]), ((0, 1, *range(4, shards, 2)), (2, 3), distances)):
        for i, d in enumerate(at):
            out_ref[pl.ds((shards - 1 - jnp.bitwise_xor(me, d)) * 2, 2), :] = scores[2 * i : 2 * i + 2]


def pair_kernel(one_ref, other_ref, out_ref):
    out_ref[0] = one_ref[...]
    out_ref[1] = other_ref[...]


def order_kernel(back_ref, out_ref):
    shards = back_ref.shape[0] // 2
    for i in range(shards):
        out_ref[0, 2 * i : 2 * i + 2] = back_ref[2 * (shards - 1 - i) : 2 * (shards - i)]


def on_device(shards, queries, passages, passage_len, slot_query, slot_passage, slot_count):
    sources, _, cap = slot_query.shape
    q_dev, q_tok, width = queries.shape
    pack = 128 // q_tok
    per_source = -(-cap // pack)
    swap = [(0, 1), (1, 0)]
    vmem, hbm, smem, anywhere = (pl.BlockSpec(memory_space=space) for space in (pltpu.VMEM, pltpu.HBM, pltpu.SMEM, pl.ANY))
    params = pltpu.CompilerParams(vmem_limit_bytes=12 * 1024 * 1024)
    row = jax.ShapeDtypeStruct((shards, 128), jnp.int32)

    def placed(space, *arrays):
        return [pltpu.with_memory_space_constraint(x, space) for x in arrays]

    def swapped(piece, d):
        return lax.ppermute(piece, "shard", [(i, i ^ d) for i in range(shards)])

    pieces = [queries, swapped(queries, 1)] + [None] * (shards - 2)
    for d in range(4, shards, 2):
        pieces[d] = swapped(queries, d)
    other_passages = lax.ppermute(passages, "sub", swap)

    calls = ((0, 1, *range(4, shards, 2)), (2, 3), range(5, shards, 2))
    sizes = tuple(map(len, calls))
    listed = [
        pltpu.SMEM(row.shape, row.dtype),
        pltpu.SMEM((len(calls),), jnp.int32),
        *(pltpu.SMEM((n * per_source + 2 * GROUPS,), jnp.int32) for n in sizes),
    ]
    theirs, own_queries, own_passages, add, *own_lists = pl.pallas_call(
        functools.partial(pack_kernel, shards, sizes, pack, per_source),
        out_shape=[
            row, *(jax.ShapeDtypeStruct(x.shape, x.dtype) for x in (queries, passages)),
            jax.ShapeDtypeStruct((per_source * 128, 128), jnp.bfloat16), *listed,
        ],
        in_specs=[hbm] * 6,
        out_specs=[vmem] * 4 + [smem] * len(listed),
        scratch_shapes=[
            pltpu.VMEM(row.shape, row.dtype),
            pltpu.VMEM((sources, cap), jnp.int32),
            pltpu.VMEM((sources, cap), jnp.int32),
            pltpu.VMEM((sources,), jnp.int32),
            pltpu.VMEM(passage_len.shape, jnp.int32),
            pltpu.SemaphoreType.DMA((5,)),
            pltpu.SemaphoreType.DMA((CHUNKS,)),
            pltpu.SemaphoreType.DMA,
        ],
        compiler_params=params,
    )(*placed(pltpu.HBM, slot_query.reshape(sources, cap), slot_passage.reshape(sources, cap), slot_count.reshape(sources), passage_len, queries, passages))
    both = pl.pallas_call(
        pair_kernel,
        out_shape=jax.ShapeDtypeStruct((2, *queries.shape), queries.dtype),
        in_specs=[vmem] * 2,
        out_specs=vmem,
        compiler_params=params,
    )(own_queries, pieces[1])
    both = swapped(both, 2)
    for d in range(5, shards, 2):
        pieces[d] = swapped(pieces[1], d - 1) if d == shards - 1 else swapped(pieces[d - 1], 1)
    theirs, _ = lax.optimization_barrier((theirs, other_passages))
    other = lax.ppermute(theirs, "sub", swap)

    def scored(parts, lists, *earlier):
        call = len(earlier)
        n = sizes[call]
        scores = jax.ShapeDtypeStruct((2 * n if call < 2 else sources, cap), jnp.float32)
        own_rows, own_totals, *own_works = own_lists
        of_own = placed(pltpu.SMEM, own_rows, own_totals, own_works[call])
        if call:
            rows, totals, *works = lists
            of_other, others = placed(pltpu.SMEM, rows, totals, works[call]), [smem] * 3
        else:
            of_other, others = lists, [anywhere]
        return pl.pallas_call(
            functools.partial(score_kernel, shards, calls, call, pack, cap),
            out_shape=scores if call else [scores, *listed],
            in_specs=[smem] * 3 + others + [vmem] * (len(parts) + 3 + call),
            out_specs=vmem if call else [vmem] + [smem] * len(listed),
            scratch_shapes=[
                pltpu.VMEM((n, *queries.shape), queries.dtype),
                pltpu.VMEM((per_source, 2 * n, 128), jnp.float32),
                *([] if call else [pltpu.SemaphoreType.DMA]),
            ],
            compiler_params=params,
            cost_estimate=pl.CostEstimate(flops=1_000_000_000, bytes_accessed=9_000_000, transcendentals=0),
        )(*of_own, *of_other, *parts, *placed(pltpu.VMEM, own_passages, other_passages), add, *earlier)

    pieces[0] = own_queries
    near, _, far = calls
    first_scores, *lists = scored([pieces[d] for d in reversed(near)], [other])
    next_scores = scored([both], lists, first_scores)
    scores = scored([pieces[d] for d in reversed(far)], lists, first_scores, next_scores)
    order = [list(reversed(range(shards)))]
    returned = lax.all_to_all(scores, "shard", split_axis=0, concat_axis=0, axis_index_groups=order, tiled=True)
    return pl.pallas_call(
        order_kernel,
        out_shape=jax.ShapeDtypeStruct((1, sources, cap), jnp.float32),
        in_specs=[vmem],
        out_specs=vmem,
        compiler_params=params,
    )(returned)


def solution(mesh):
    return jax.shard_map(
        functools.partial(on_device, mesh.shape["shard"]),
        mesh=mesh,
        in_specs=(
            P(("groups", "shard", "sub"), None, None),
            P(("shard", "sub"), None, None),
            P(("shard", "sub")),
            P("groups", ("shard", "sub"), None),
            P("groups", ("shard", "sub"), None),
            P("groups", ("shard", "sub")),
        ),
        out_specs=P(("groups", "shard", "sub"), None, None),
        check_vma=False,
    )
```

```python
import functools

import jax
import jax.numpy as jnp
from jax import lax
from jax.experimental import pallas as pl
from jax.experimental.pallas import tpu as pltpu
from jax.sharding import PartitionSpec as P

GROUPS = 8
CHUNKS = 8
SHIFT = 8
QUERY, PASSAGE, LENGTH, COUNT = 0, 32, 64, 96


def distance(call, i):
    return (jnp.where(i == 1, 1, i * 2), i + 2, i * 2 + 5)[call]


def list_groups(sizes, pack, per_source, row_ref, total_ref, work_refs):
    me = lax.axis_index("shard")
    for call, (n, work_ref) in enumerate(zip(sizes, work_refs)):

        def list_source(i, total):
            live = row_ref[jnp.bitwise_xor(me, distance(call, i)), COUNT]
            for g in range(per_source):
                work_ref[total + g] = (i << SHIFT) + g
            return total + lax.shift_right_logical(live + pack - 1, pack.bit_length() - 1)

        total = 0
        if n <= 8:
            for i in range(n):
                total = list_source(i, total)
        else:
            total = lax.fori_loop(0, n, list_source, 0)
        for g in range(GROUPS):
            work_ref[total + g] = 0
        total_ref[call] = total


def pack_kernel(shards, *refs):
    query_hbm, passage_hbm, count_hbm, length_hbm, tokens_hbm, own_hbm, mine_ref, theirs_ref, tokens_ref, own_ref, add_ref = refs[:11]
    query_ref, passage_ref, count_ref, length_ref, sems, own_sems = refs[11:]
    copies = [
        pltpu.make_async_copy(src, dst, sems.at[i])
        for i, (src, dst) in enumerate(
            (
                (query_hbm, query_ref),
                (passage_hbm, passage_ref),
                (count_hbm, count_ref),
                (length_hbm, length_ref),
                (tokens_hbm, tokens_ref),
            )
        )
    ]
    size = own_ref.shape[0] // CHUNKS
    own_copies = [
        pltpu.make_async_copy(own_hbm.at[pl.ds(i * size, size)], own_ref.at[pl.ds(i * size, size)], own_sems.at[i])
        for i in range(CHUNKS)
    ]
    for copy in copies + own_copies:
        copy.start()
    row = lax.broadcasted_iota(jnp.int32, add_ref.shape, 0)
    col = lax.broadcasted_iota(jnp.int32, add_ref.shape, 1)
    q_bits = tokens_ref.shape[1].bit_length() - 1
    add_ref[...] = jnp.where(lax.shift_right_logical(row, q_bits) == col, 1.0, 0.0).astype(add_ref.dtype)
    for copy in copies:
        copy.wait()
    cap = query_ref.shape[1]
    lengths = length_ref[...].reshape(1, -1)
    counts = jnp.broadcast_to(count_ref[...].reshape(1, -1), (2 * shards, 2 * shards))
    row = lax.broadcasted_iota(jnp.int32, counts.shape, 0)
    col = lax.broadcasted_iota(jnp.int32, counts.shape, 1)
    counts = jnp.sum(jnp.where(row == col, counts, 0), axis=1, keepdims=True)
    blank = jnp.zeros((2 * shards, 32 - cap), jnp.int32)
    passage = jnp.concatenate([passage_ref[...], blank], axis=1)
    passage = jnp.concatenate([passage] * 4, axis=1)
    length = jnp.take_along_axis(jnp.broadcast_to(lengths, passage.shape), passage, axis=1)
    query = jnp.concatenate([jnp.concatenate([query_ref[...], blank], axis=1)] * 4, axis=1)
    lane = lax.broadcasted_iota(jnp.int32, passage.shape, 1)
    packed = jnp.where(lane < PASSAGE, query, jnp.where(lane < LENGTH, passage, jnp.where(lane < COUNT, length, counts)))
    packed = packed.reshape(shards, 2, 128)
    first = lax.axis_index("sub") == 0
    mine_ref[...] = jnp.where(first, packed[:, 0], packed[:, 1])
    theirs_ref[...] = jnp.where(first, packed[:, 1], packed[:, 0])
    for copy in own_copies:
        copy.wait()


def score_kernel(shards, calls, call, pack, cap, *refs):
    distances = calls[call]
    n = len(distances)
    p = 1 if call == 1 else n
    if call == 0:
        rows, refs = refs[:2], refs[2:]
        refs, (out_ref, *outs, query_ref, best_ref, row_sems) = refs[: p + 3], refs[p + 3 :]
        made = outs[: len(outs) // 2], outs[len(outs) // 2 :]
        lists = [(row_ref, total_ref, work_ref) for row_ref, total_ref, work_ref, *_ in made]
        copies = [pltpu.make_async_copy(row, each[0], row_sems.at[i]) for i, (row, each) in enumerate(zip(rows, made))]
        for copy in copies:
            copy.start()
    else:
        lists = [refs[:3], refs[3:6]]
        refs, (out_ref, query_ref, best_ref) = refs[6:-3], refs[-3:]
    pieces, passage_refs, add_ref, earlier = refs[:p], refs[p : p + 2], refs[p + 2], refs[p + 3 :]
    q_tok, width = query_ref.shape[2:]
    tok_slots = passage_refs[0].shape[1]
    per_source = best_ref.shape[0]
    lanes = pack * q_tok
    q_bits = q_tok.bit_length() - 1
    me, core = lax.axis_index("shard"), lax.axis_index("sub")
    if call == 1:
        query_ref[...] = pieces[0][...]
    else:
        for i, piece in enumerate(reversed(pieces)):
            query_ref[i] = piece[...]
    best_ref[...] = jnp.zeros_like(best_ref)
    token = lax.broadcasted_iota(jnp.int32, (tok_slots, lanes), 0)
    place = lax.shift_right_logical(lax.broadcasted_iota(jnp.int32, (1, lanes), 1), q_bits)
    blank = jnp.zeros((q_tok, width), query_ref.dtype)

    for which, passages in enumerate(passage_refs):
        meta_ref, total_ref, work_ref = lists[which]
        owner = core if which == 0 else 1 - core
        if call == 0:
            copies[which].wait()
            list_groups(tuple(map(len, calls)), pack, per_source, *made[which][:2], made[which][2:])
        total = total_ref[call]

        def one_step(first_group, groups):
            for j in range(groups):
                work = work_ref[first_group + j]
                i, g = lax.shift_right_logical(work, SHIFT), jnp.bitwise_and(work, (1 << SHIFT) - 1)
                shard = jnp.bitwise_xor(me, distance(call, i))
                rows, cols, limit = [], [], jnp.zeros((1, lanes), jnp.int32)
                for a in range(pack):
                    slot = g * pack + a
                    query, passage = meta_ref[shard, QUERY + slot], meta_ref[shard, PASSAGE + slot]
                    rows.append(jnp.concatenate([blank] * a + [query_ref[i, query]] + [blank] * (pack - 1 - a), axis=1))
                    cols.append(passages[passage])
                    limit = jnp.where(place == a, meta_ref[shard, LENGTH + slot], limit)
                sims = lax.dot_general(
                    jnp.concatenate(cols, axis=1), jnp.concatenate(rows, axis=0),
                    (((1,), (1,)), ((), ())), preferred_element_type=jnp.float32,
                )
                best = jnp.max(jnp.where(token < limit, sims, -1e30), axis=0, keepdims=True)
                best = jnp.where(place + g * pack < meta_ref[shard, COUNT], best, 0.0)
                best_ref[g, pl.ds(i * 2 + owner, 1), :] = best

        half = GROUPS // 2
        steps = lax.shift_right_logical(total + half - 1, GROUPS.bit_length() - 1)

        @pl.loop(0, steps)
        def _(step):
            one_step(step * GROUPS, GROUPS)

        @pl.when(total > steps * GROUPS)
        def _():
            one_step(steps * GROUPS, half)

    best = jnp.concatenate([best_ref[g] for g in range(per_source)], axis=1)
    high = best.astype(jnp.bfloat16)
    rest = best - high.astype(jnp.float32)
    middle = rest.astype(jnp.bfloat16)
    low = (rest - middle.astype(jnp.float32)).astype(jnp.bfloat16)
    parts = jnp.dot(jnp.concatenate([high, middle, low], axis=0), add_ref[...], preferred_element_type=jnp.float32)
    rows = best.shape[0]
    score = (parts[:rows] + parts[rows : 2 * rows] + parts[2 * rows :]) * (1.0 / q_tok)
    if call < 2:
        out_ref[...] = score[:, :cap]
        return
    for scores, at in zip((*(ref[...] for ref in earlier), score[:, :cap]), ((0, 1, *range(4, shards, 2)), (2, 3), distances)):
        for i, d in enumerate(at):
            out_ref[pl.ds((shards - 1 - jnp.bitwise_xor(me, d)) * 2, 2), :] = scores[2 * i : 2 * i + 2]


def pair_kernel(one_ref, other_ref, out_ref):
    out_ref[0] = one_ref[...]
    out_ref[1] = other_ref[...]


def order_kernel(back_ref, out_ref):
    shards = back_ref.shape[0] // 2
    for i in range(shards):
        out_ref[0, 2 * i : 2 * i + 2] = back_ref[2 * (shards - 1 - i) : 2 * (shards - i)]


def on_device(shards, queries, passages, passage_len, slot_query, slot_passage, slot_count):
    sources, _, cap = slot_query.shape
    q_dev, q_tok, width = queries.shape
    pack = 128 // q_tok
    per_source = -(-cap // pack)
    swap = [(0, 1), (1, 0)]
    vmem, hbm, smem, anywhere = (pl.BlockSpec(memory_space=space) for space in (pltpu.VMEM, pltpu.HBM, pltpu.SMEM, pl.ANY))
    params = pltpu.CompilerParams(vmem_limit_bytes=12 * 1024 * 1024)
    row = jax.ShapeDtypeStruct((shards, 128), jnp.int32)

    def placed(space, *arrays):
        return [pltpu.with_memory_space_constraint(x, space) for x in arrays]

    def swapped(piece, d):
        return lax.ppermute(piece, "shard", [(i, i ^ d) for i in range(shards)])

    pieces = [queries, swapped(queries, 1)] + [None] * (shards - 2)
    for d in range(4, shards, 2):
        pieces[d] = swapped(queries, d)
    other_passages = lax.ppermute(passages, "sub", swap)

    calls = ((0, 1, *range(4, shards, 2)), (2, 3), range(5, shards, 2))
    sizes = tuple(map(len, calls))
    listed = [
        pltpu.SMEM(row.shape, row.dtype),
        pltpu.SMEM((len(calls),), jnp.int32),
        *(pltpu.SMEM((n * per_source + 2 * GROUPS,), jnp.int32) for n in sizes),
    ]
    mine, theirs, own_queries, own_passages, add = pl.pallas_call(
        functools.partial(pack_kernel, shards),
        out_shape=[
            row, row, *(jax.ShapeDtypeStruct(x.shape, x.dtype) for x in (queries, passages)),
            jax.ShapeDtypeStruct((per_source * 128, 128), jnp.bfloat16),
        ],
        in_specs=[hbm] * 6,
        out_specs=[vmem] * 5,
        scratch_shapes=[
            pltpu.VMEM((sources, cap), jnp.int32),
            pltpu.VMEM((sources, cap), jnp.int32),
            pltpu.VMEM((sources,), jnp.int32),
            pltpu.VMEM(passage_len.shape, jnp.int32),
            pltpu.SemaphoreType.DMA((5,)),
            pltpu.SemaphoreType.DMA((CHUNKS,)),
        ],
        compiler_params=params,
    )(*placed(pltpu.HBM, slot_query.reshape(sources, cap), slot_passage.reshape(sources, cap), slot_count.reshape(sources), passage_len, queries, passages))
    both = pl.pallas_call(
        pair_kernel,
        out_shape=jax.ShapeDtypeStruct((2, *queries.shape), queries.dtype),
        in_specs=[vmem] * 2,
        out_specs=vmem,
        compiler_params=params,
    )(own_queries, pieces[1])
    both = swapped(both, 2)
    for d in range(5, shards, 2):
        pieces[d] = swapped(pieces[1], d - 1) if d == shards - 1 else swapped(pieces[d - 1], 1)
    theirs, _ = lax.optimization_barrier((theirs, other_passages))
    other = lax.ppermute(theirs, "sub", swap)

    def scored(parts, lists, *earlier):
        call = len(earlier)
        n = sizes[call]
        scores = jax.ShapeDtypeStruct((2 * n if call < 2 else sources, cap), jnp.float32)
        if call:
            given = [x for rows, totals, *works in lists for x in placed(pltpu.SMEM, rows, totals, works[call])]
        else:
            given = lists
        return pl.pallas_call(
            functools.partial(score_kernel, shards, calls, call, pack, cap),
            out_shape=scores if call else [scores, *listed, *listed],
            in_specs=([smem] * 6 if call else [anywhere] * 2) + [vmem] * (len(parts) + 3 + call),
            out_specs=vmem if call else [vmem] + [smem] * (2 * len(listed)),
            scratch_shapes=[
                pltpu.VMEM((n, *queries.shape), queries.dtype),
                pltpu.VMEM((per_source, 2 * n, 128), jnp.float32),
                *([] if call else [pltpu.SemaphoreType.DMA((2,))]),
            ],
            compiler_params=params,
            cost_estimate=pl.CostEstimate(flops=1_000_000_000, bytes_accessed=9_000_000, transcendentals=0),
        )(*given, *parts, *placed(pltpu.VMEM, own_passages, other_passages), add, *earlier)

    pieces[0] = own_queries
    near, _, far = calls
    first_scores, *made = scored([pieces[d] for d in reversed(near)], [mine, other])
    lists = made[: len(listed)], made[len(listed) :]
    next_scores = scored([both], lists, first_scores)
    scores = scored([pieces[d] for d in reversed(far)], lists, first_scores, next_scores)
    order = [list(reversed(range(shards)))]
    returned = lax.all_to_all(scores, "shard", split_axis=0, concat_axis=0, axis_index_groups=order, tiled=True)
    return pl.pallas_call(
        order_kernel,
        out_shape=jax.ShapeDtypeStruct((1, sources, cap), jnp.float32),
        in_specs=[vmem],
        out_specs=vmem,
        compiler_params=params,
    )(returned)


def solution(mesh):
    return jax.shard_map(
        functools.partial(on_device, mesh.shape["shard"]),
        mesh=mesh,
        in_specs=(
            P(("groups", "shard", "sub"), None, None),
            P(("shard", "sub"), None, None),
            P(("shard", "sub")),
            P("groups", ("shard", "sub"), None),
            P("groups", ("shard", "sub"), None),
            P("groups", ("shard", "sub")),
        ),
        out_specs=P(("groups", "shard", "sub"), None, None),
        check_vma=False,
    )
```

```python
import functools

import jax
import jax.numpy as jnp
from jax import lax
from jax.experimental import pallas as pl
from jax.experimental.pallas import tpu as pltpu
from jax.sharding import PartitionSpec as P

GROUPS = 12
REST = 8
CHUNKS = 8
SHIFT = 8
QUERY, PASSAGE, LENGTH, COUNT = 0, 32, 64, 96


def distance(call, i):
    return (jnp.where(i == 1, 1, i * 2), i + 2, i * 2 + 5)[call]


def list_groups(sizes, pack, per_source, row_ref, total_ref, work_refs):
    me = lax.axis_index("shard")
    for call, (n, work_ref) in enumerate(zip(sizes, work_refs)):

        def list_source(i, total):
            live = row_ref[jnp.bitwise_xor(me, distance(call, i)), COUNT]
            for g in range(per_source):
                work_ref[total + g] = (i << SHIFT) + g
            return total + lax.shift_right_logical(live + pack - 1, pack.bit_length() - 1)

        total = 0
        if n <= 8:
            for i in range(n):
                total = list_source(i, total)
        else:
            total = lax.fori_loop(0, n, list_source, 0)
        for g in range(REST // 2 - 1):
            work_ref[total + g] = 0
        total_ref[call] = total


def pack_kernel(shards, *refs):
    query_hbm, passage_hbm, count_hbm, length_hbm, tokens_hbm, own_hbm, mine_ref, theirs_ref, tokens_ref, own_ref, add_ref = refs[:11]
    query_ref, passage_ref, count_ref, length_ref, sems, own_sems = refs[11:]
    copies = [
        pltpu.make_async_copy(src, dst, sems.at[i])
        for i, (src, dst) in enumerate(
            (
                (query_hbm, query_ref),
                (passage_hbm, passage_ref),
                (count_hbm, count_ref),
                (length_hbm, length_ref),
                (tokens_hbm, tokens_ref),
            )
        )
    ]
    size = own_ref.shape[0] // CHUNKS
    own_copies = [
        pltpu.make_async_copy(own_hbm.at[pl.ds(i * size, size)], own_ref.at[pl.ds(i * size, size)], own_sems.at[i])
        for i in range(CHUNKS)
    ]
    for copy in copies + own_copies:
        copy.start()
    row = lax.broadcasted_iota(jnp.int32, add_ref.shape, 0)
    col = lax.broadcasted_iota(jnp.int32, add_ref.shape, 1)
    q_bits = tokens_ref.shape[1].bit_length() - 1
    add_ref[...] = jnp.where(lax.shift_right_logical(row, q_bits) == col, 1.0, 0.0).astype(add_ref.dtype)
    for copy in copies:
        copy.wait()
    cap = query_ref.shape[1]
    lengths = length_ref[...].reshape(1, -1)
    counts = jnp.broadcast_to(count_ref[...].reshape(1, -1), (2 * shards, 2 * shards))
    row = lax.broadcasted_iota(jnp.int32, counts.shape, 0)
    col = lax.broadcasted_iota(jnp.int32, counts.shape, 1)
    counts = jnp.sum(jnp.where(row == col, counts, 0), axis=1, keepdims=True)
    blank = jnp.zeros((2 * shards, 32 - cap), jnp.int32)
    passage = jnp.concatenate([passage_ref[...], blank], axis=1)
    passage = jnp.concatenate([passage] * 4, axis=1)
    length = jnp.take_along_axis(jnp.broadcast_to(lengths, passage.shape), passage, axis=1)
    query = jnp.concatenate([jnp.concatenate([query_ref[...], blank], axis=1)] * 4, axis=1)
    lane = lax.broadcasted_iota(jnp.int32, passage.shape, 1)
    packed = jnp.where(lane < PASSAGE, query, jnp.where(lane < LENGTH, passage, jnp.where(lane < COUNT, length, counts)))
    packed = packed.reshape(shards, 2, 128)
    first = lax.axis_index("sub") == 0
    mine_ref[...] = jnp.where(first, packed[:, 0], packed[:, 1])
    theirs_ref[...] = jnp.where(first, packed[:, 1], packed[:, 0])
    for copy in own_copies:
        copy.wait()


def score_kernel(shards, calls, call, pack, cap, *refs):
    distances = calls[call]
    n = len(distances)
    p = 1 if call == 1 else n
    if call == 0:
        rows, refs = refs[:2], refs[2:]
        refs, (out_ref, *outs, query_ref, best_ref, row_sems) = refs[: p + 3], refs[p + 3 :]
        made = outs[: len(outs) // 2], outs[len(outs) // 2 :]
        lists = [(row_ref, total_ref, work_ref) for row_ref, total_ref, work_ref, *_ in made]
        copies = [pltpu.make_async_copy(row, each[0], row_sems.at[i]) for i, (row, each) in enumerate(zip(rows, made))]
        for copy in copies:
            copy.start()
    else:
        lists = [refs[:3], refs[3:6]]
        refs, (out_ref, query_ref, best_ref) = refs[6:-3], refs[-3:]
    pieces, passage_refs, add_ref, earlier = refs[:p], refs[p : p + 2], refs[p + 2], refs[p + 3 :]
    q_tok, width = query_ref.shape[2:]
    tok_slots = passage_refs[0].shape[1]
    per_source = best_ref.shape[0]
    lanes = pack * q_tok
    q_bits = q_tok.bit_length() - 1
    me, core = lax.axis_index("shard"), lax.axis_index("sub")
    if call == 1:
        query_ref[...] = pieces[0][...]
    else:
        for i, piece in enumerate(reversed(pieces)):
            query_ref[i] = piece[...]
    best_ref[...] = jnp.zeros_like(best_ref)
    token = lax.broadcasted_iota(jnp.int32, (tok_slots, lanes), 0)
    place = lax.shift_right_logical(lax.broadcasted_iota(jnp.int32, (1, lanes), 1), q_bits)
    blank = jnp.zeros((q_tok, width), query_ref.dtype)

    for which, passages in enumerate(passage_refs):
        meta_ref, total_ref, work_ref = lists[which]
        owner = core if which == 0 else 1 - core
        if call == 0:
            copies[which].wait()
            list_groups(tuple(map(len, calls)), pack, per_source, *made[which][:2], made[which][2:])
        total = total_ref[call]

        def one_step(first_group, groups):
            for j in range(groups):
                work = work_ref[first_group + j]
                i, g = lax.shift_right_logical(work, SHIFT), jnp.bitwise_and(work, (1 << SHIFT) - 1)
                shard = jnp.bitwise_xor(me, distance(call, i))
                rows, cols, limit = [], [], jnp.zeros((1, lanes), jnp.int32)
                for a in range(pack):
                    slot = g * pack + a
                    query, passage = meta_ref[shard, QUERY + slot], meta_ref[shard, PASSAGE + slot]
                    rows.append(jnp.concatenate([blank] * a + [query_ref[i, query]] + [blank] * (pack - 1 - a), axis=1))
                    cols.append(passages[passage])
                    limit = jnp.where(place == a, meta_ref[shard, LENGTH + slot], limit)
                sims = lax.dot_general(
                    jnp.concatenate(cols, axis=1), jnp.concatenate(rows, axis=0),
                    (((1,), (1,)), ((), ())), preferred_element_type=jnp.float32,
                )
                best = jnp.max(jnp.where(token < limit, sims, -1e30), axis=0, keepdims=True)
                best = jnp.where(place + g * pack < meta_ref[shard, COUNT], best, 0.0)
                best_ref[g, pl.ds(i * 2 + owner, 1), :] = best

        steps = lax.div(total + GROUPS - REST - 1, GROUPS)
        rest = total - steps * GROUPS

        @pl.loop(0, steps)
        def _(step):
            one_step(step * GROUPS, GROUPS)

        @pl.when(rest > REST // 2)
        def _():
            one_step(steps * GROUPS, REST)

        @pl.when((rest > 0) & (rest <= REST // 2))
        def _():
            one_step(steps * GROUPS, REST // 2)

    best = jnp.concatenate([best_ref[g] for g in range(per_source)], axis=1)
    high = best.astype(jnp.bfloat16)
    rest = best - high.astype(jnp.float32)
    middle = rest.astype(jnp.bfloat16)
    low = (rest - middle.astype(jnp.float32)).astype(jnp.bfloat16)
    parts = jnp.dot(jnp.concatenate([high, middle, low], axis=0), add_ref[...], preferred_element_type=jnp.float32)
    rows = best.shape[0]
    score = (parts[:rows] + parts[rows : 2 * rows] + parts[2 * rows :]) * (1.0 / q_tok)
    if call < 2:
        out_ref[...] = score[:, :cap]
        return
    for scores, at in zip((*(ref[...] for ref in earlier), score[:, :cap]), ((0, 1, *range(4, shards, 2)), (2, 3), distances)):
        for i, d in enumerate(at):
            out_ref[pl.ds((shards - 1 - jnp.bitwise_xor(me, d)) * 2, 2), :] = scores[2 * i : 2 * i + 2]


def pair_kernel(one_ref, other_ref, out_ref):
    out_ref[0] = one_ref[...]
    out_ref[1] = other_ref[...]


def order_kernel(back_ref, out_ref):
    shards = back_ref.shape[0] // 2
    for i in range(shards):
        out_ref[0, 2 * i : 2 * i + 2] = back_ref[2 * (shards - 1 - i) : 2 * (shards - i)]


def on_device(shards, queries, passages, passage_len, slot_query, slot_passage, slot_count):
    sources, _, cap = slot_query.shape
    q_dev, q_tok, width = queries.shape
    pack = 128 // q_tok
    per_source = -(-cap // pack)
    swap = [(0, 1), (1, 0)]
    vmem, hbm, smem, anywhere = (pl.BlockSpec(memory_space=space) for space in (pltpu.VMEM, pltpu.HBM, pltpu.SMEM, pl.ANY))
    params = pltpu.CompilerParams(vmem_limit_bytes=12 * 1024 * 1024)
    row = jax.ShapeDtypeStruct((shards, 128), jnp.int32)

    def placed(space, *arrays):
        return [pltpu.with_memory_space_constraint(x, space) for x in arrays]

    def swapped(piece, d):
        return lax.ppermute(piece, "shard", [(i, i ^ d) for i in range(shards)])

    pieces = [queries, swapped(queries, 1)] + [None] * (shards - 2)
    for d in range(4, shards, 2):
        pieces[d] = swapped(queries, d)
    other_passages = lax.ppermute(passages, "sub", swap)

    calls = ((0, 1, *range(4, shards, 2)), (2, 3), range(5, shards, 2))
    sizes = tuple(map(len, calls))
    listed = [
        pltpu.SMEM(row.shape, row.dtype),
        pltpu.SMEM((len(calls),), jnp.int32),
        *(pltpu.SMEM((n * per_source + 2 * GROUPS,), jnp.int32) for n in sizes),
    ]
    mine, theirs, own_queries, own_passages, add = pl.pallas_call(
        functools.partial(pack_kernel, shards),
        out_shape=[
            row, row, *(jax.ShapeDtypeStruct(x.shape, x.dtype) for x in (queries, passages)),
            jax.ShapeDtypeStruct((per_source * 128, 128), jnp.bfloat16),
        ],
        in_specs=[hbm] * 6,
        out_specs=[vmem] * 5,
        scratch_shapes=[
            pltpu.VMEM((sources, cap), jnp.int32),
            pltpu.VMEM((sources, cap), jnp.int32),
            pltpu.VMEM((sources,), jnp.int32),
            pltpu.VMEM(passage_len.shape, jnp.int32),
            pltpu.SemaphoreType.DMA((5,)),
            pltpu.SemaphoreType.DMA((CHUNKS,)),
        ],
        compiler_params=params,
    )(*placed(pltpu.HBM, slot_query.reshape(sources, cap), slot_passage.reshape(sources, cap), slot_count.reshape(sources), passage_len, queries, passages))
    both = pl.pallas_call(
        pair_kernel,
        out_shape=jax.ShapeDtypeStruct((2, *queries.shape), queries.dtype),
        in_specs=[vmem] * 2,
        out_specs=vmem,
        compiler_params=params,
    )(own_queries, pieces[1])
    both = swapped(both, 2)
    for d in range(5, shards, 2):
        pieces[d] = swapped(pieces[1], d - 1) if d == shards - 1 else swapped(pieces[d - 1], 1)
    theirs, _ = lax.optimization_barrier((theirs, other_passages))
    other = lax.ppermute(theirs, "sub", swap)

    def scored(parts, lists, *earlier):
        call = len(earlier)
        n = sizes[call]
        scores = jax.ShapeDtypeStruct((2 * n if call < 2 else sources, cap), jnp.float32)
        if call:
            given = [x for rows, totals, *works in lists for x in placed(pltpu.SMEM, rows, totals, works[call])]
        else:
            given = lists
        return pl.pallas_call(
            functools.partial(score_kernel, shards, calls, call, pack, cap),
            out_shape=scores if call else [scores, *listed, *listed],
            in_specs=([smem] * 6 if call else [anywhere] * 2) + [vmem] * (len(parts) + 3 + call),
            out_specs=vmem if call else [vmem] + [smem] * (2 * len(listed)),
            scratch_shapes=[
                pltpu.VMEM((n, *queries.shape), queries.dtype),
                pltpu.VMEM((per_source, 2 * n, 128), jnp.float32),
                *([] if call else [pltpu.SemaphoreType.DMA((2,))]),
            ],
            compiler_params=params,
            cost_estimate=pl.CostEstimate(flops=1_000_000_000, bytes_accessed=9_000_000, transcendentals=0),
        )(*given, *parts, *placed(pltpu.VMEM, own_passages, other_passages), add, *earlier)

    pieces[0] = own_queries
    near, _, far = calls
    first_scores, *made = scored([pieces[d] for d in reversed(near)], [mine, other])
    lists = made[: len(listed)], made[len(listed) :]
    next_scores = scored([both], lists, first_scores)
    scores = scored([pieces[d] for d in reversed(far)], lists, first_scores, next_scores)
    order = [list(reversed(range(shards)))]
    returned = lax.all_to_all(scores, "shard", split_axis=0, concat_axis=0, axis_index_groups=order, tiled=True)
    return pl.pallas_call(
        order_kernel,
        out_shape=jax.ShapeDtypeStruct((1, sources, cap), jnp.float32),
        in_specs=[vmem],
        out_specs=vmem,
        compiler_params=params,
    )(returned)


def solution(mesh):
    return jax.shard_map(
        functools.partial(on_device, mesh.shape["shard"]),
        mesh=mesh,
        in_specs=(
            P(("groups", "shard", "sub"), None, None),
            P(("shard", "sub"), None, None),
            P(("shard", "sub")),
            P("groups", ("shard", "sub"), None),
            P("groups", ("shard", "sub"), None),
            P("groups", ("shard", "sub")),
        ),
        out_specs=P(("groups", "shard", "sub"), None, None),
        check_vma=False,
    )
```

```python
import functools

import jax
import jax.numpy as jnp
from jax import lax
from jax.experimental import pallas as pl
from jax.experimental.pallas import tpu as pltpu
from jax.sharding import PartitionSpec as P

GROUPS = 12
REST = 8
CHUNKS = 8
SHIFT = 8
QUERY, PASSAGE, LENGTH, COUNT = 0, 32, 64, 96


def distance(call, i):
    return (jnp.where(i == 1, 1, i * 2), i + 2, i * 2 + 5)[call]


def list_groups(sizes, pack, per_source, row_ref, total_ref, work_refs):
    me = lax.axis_index("shard")
    for call, (n, work_ref) in enumerate(zip(sizes, work_refs)):

        def list_source(i, total):
            live = row_ref[jnp.bitwise_xor(me, distance(call, i)), COUNT]
            for g in range(per_source):
                work_ref[total + g] = (i << SHIFT) + g
            return total + lax.shift_right_logical(live + pack - 1, pack.bit_length() - 1)

        total = 0
        if n <= 8:
            for i in range(n):
                total = list_source(i, total)
        else:
            total = lax.fori_loop(0, n, list_source, 0)
        for g in range(REST // 2 - 1):
            work_ref[total + g] = 0
        total_ref[call] = total


def pack_kernel(shards, *refs):
    query_hbm, passage_hbm, count_hbm, length_hbm, tokens_hbm, own_hbm, row_ref, theirs_ref, tokens_ref, own_ref, add_ref = refs[:11]
    mine_ref, query_ref, passage_ref, count_ref, length_ref, sems, own_sems, row_sem = refs[11:]
    copies = [
        pltpu.make_async_copy(src, dst, sems.at[i])
        for i, (src, dst) in enumerate(
            (
                (query_hbm, query_ref),
                (passage_hbm, passage_ref),
                (count_hbm, count_ref),
                (length_hbm, length_ref),
                (tokens_hbm, tokens_ref),
            )
        )
    ]
    size = own_ref.shape[0] // CHUNKS
    own_copies = [
        pltpu.make_async_copy(own_hbm.at[pl.ds(i * size, size)], own_ref.at[pl.ds(i * size, size)], own_sems.at[i])
        for i in range(CHUNKS)
    ]
    for copy in copies + own_copies:
        copy.start()
    row = lax.broadcasted_iota(jnp.int32, add_ref.shape, 0)
    col = lax.broadcasted_iota(jnp.int32, add_ref.shape, 1)
    q_bits = tokens_ref.shape[1].bit_length() - 1
    add_ref[...] = jnp.where(lax.shift_right_logical(row, q_bits) == col, 1.0, 0.0).astype(add_ref.dtype)
    for copy in copies:
        copy.wait()
    cap = query_ref.shape[1]
    lengths = length_ref[...].reshape(1, -1)
    counts = jnp.broadcast_to(count_ref[...].reshape(1, -1), (2 * shards, 2 * shards))
    row = lax.broadcasted_iota(jnp.int32, counts.shape, 0)
    col = lax.broadcasted_iota(jnp.int32, counts.shape, 1)
    counts = jnp.sum(jnp.where(row == col, counts, 0), axis=1, keepdims=True)
    blank = jnp.zeros((2 * shards, 32 - cap), jnp.int32)
    passage = jnp.concatenate([passage_ref[...], blank], axis=1)
    passage = jnp.concatenate([passage] * 4, axis=1)
    length = jnp.take_along_axis(jnp.broadcast_to(lengths, passage.shape), passage, axis=1)
    query = jnp.concatenate([jnp.concatenate([query_ref[...], blank], axis=1)] * 4, axis=1)
    lane = lax.broadcasted_iota(jnp.int32, passage.shape, 1)
    packed = jnp.where(lane < PASSAGE, query, jnp.where(lane < LENGTH, passage, jnp.where(lane < COUNT, length, counts)))
    packed = packed.reshape(shards, 2, 128)
    first = lax.axis_index("sub") == 0
    mine_ref[...] = jnp.where(first, packed[:, 0], packed[:, 1])
    theirs_ref[...] = jnp.where(first, packed[:, 1], packed[:, 0])
    row_copy = pltpu.make_async_copy(mine_ref, row_ref, row_sem)
    row_copy.start()
    for copy in own_copies:
        copy.wait()
    row_copy.wait()


def score_kernel(shards, calls, call, pack, cap, *refs):
    distances = calls[call]
    n = len(distances)
    p = 1 if call == 1 else n
    if call == 0:
        (own_rows, rows), refs = refs[:2], refs[2:]
        refs, (out_ref, *outs, query_ref, best_ref, row_sem) = refs[: p + 3], refs[p + 3 :]
        made = (own_rows, *outs[: len(calls) + 1]), outs[len(calls) + 1 :]
        lists = [(row_ref, total_ref, work_ref) for row_ref, total_ref, work_ref, *_ in made]
        copy = pltpu.make_async_copy(rows, made[1][0], row_sem)
        copy.start()
    else:
        lists = [refs[:3], refs[3:6]]
        refs, (out_ref, query_ref, best_ref) = refs[6:-3], refs[-3:]
    pieces, passage_refs, add_ref, earlier = refs[:p], refs[p : p + 2], refs[p + 2], refs[p + 3 :]
    q_tok, width = query_ref.shape[2:]
    tok_slots = passage_refs[0].shape[1]
    per_source = best_ref.shape[0]
    lanes = pack * q_tok
    q_bits = q_tok.bit_length() - 1
    me, core = lax.axis_index("shard"), lax.axis_index("sub")
    if call == 1:
        query_ref[...] = pieces[0][...]
    else:
        for i, piece in enumerate(reversed(pieces)):
            query_ref[i] = piece[...]
    best_ref[...] = jnp.zeros_like(best_ref)
    token = lax.broadcasted_iota(jnp.int32, (tok_slots, lanes), 0)
    place = lax.shift_right_logical(lax.broadcasted_iota(jnp.int32, (1, lanes), 1), q_bits)
    blank = jnp.zeros((q_tok, width), query_ref.dtype)

    for which, passages in enumerate(passage_refs):
        meta_ref, total_ref, work_ref = lists[which]
        owner = core if which == 0 else 1 - core
        if call == 0:
            if which == 1:
                copy.wait()
            list_groups(tuple(map(len, calls)), pack, per_source, *made[which][:2], made[which][2:])
        total = total_ref[call]

        def one_step(first_group, groups):
            for j in range(groups):
                work = work_ref[first_group + j]
                i, g = lax.shift_right_logical(work, SHIFT), jnp.bitwise_and(work, (1 << SHIFT) - 1)
                shard = jnp.bitwise_xor(me, distance(call, i))
                rows, cols, limit = [], [], jnp.zeros((1, lanes), jnp.int32)
                for a in range(pack):
                    slot = g * pack + a
                    query, passage = meta_ref[shard, QUERY + slot], meta_ref[shard, PASSAGE + slot]
                    rows.append(jnp.concatenate([blank] * a + [query_ref[i, query]] + [blank] * (pack - 1 - a), axis=1))
                    cols.append(passages[passage])
                    limit = jnp.where(place == a, meta_ref[shard, LENGTH + slot], limit)
                sims = lax.dot_general(
                    jnp.concatenate(cols, axis=1), jnp.concatenate(rows, axis=0),
                    (((1,), (1,)), ((), ())), preferred_element_type=jnp.float32,
                )
                best = jnp.max(jnp.where(token < limit, sims, -1e30), axis=0, keepdims=True)
                best = jnp.where(place + g * pack < meta_ref[shard, COUNT], best, 0.0)
                best_ref[g, pl.ds(i * 2 + owner, 1), :] = best

        steps = lax.div(total + GROUPS - REST - 1, GROUPS)
        rest = total - steps * GROUPS

        @pl.loop(0, steps)
        def _(step):
            one_step(step * GROUPS, GROUPS)

        @pl.when(rest > REST // 2)
        def _():
            one_step(steps * GROUPS, REST)

        @pl.when((rest > 0) & (rest <= REST // 2))
        def _():
            one_step(steps * GROUPS, REST // 2)

    best = jnp.concatenate([best_ref[g] for g in range(per_source)], axis=1)
    high = best.astype(jnp.bfloat16)
    rest = best - high.astype(jnp.float32)
    middle = rest.astype(jnp.bfloat16)
    low = (rest - middle.astype(jnp.float32)).astype(jnp.bfloat16)
    parts = jnp.dot(jnp.concatenate([high, middle, low], axis=0), add_ref[...], preferred_element_type=jnp.float32)
    rows = best.shape[0]
    score = (parts[:rows] + parts[rows : 2 * rows] + parts[2 * rows :]) * (1.0 / q_tok)
    if call < 2:
        out_ref[...] = score[:, :cap]
        return
    for scores, at in zip((*(ref[...] for ref in earlier), score[:, :cap]), ((0, 1, *range(4, shards, 2)), (2, 3), distances)):
        for i, d in enumerate(at):
            out_ref[pl.ds((shards - 1 - jnp.bitwise_xor(me, d)) * 2, 2), :] = scores[2 * i : 2 * i + 2]


def pair_kernel(one_ref, other_ref, out_ref):
    out_ref[0] = one_ref[...]
    out_ref[1] = other_ref[...]


def order_kernel(back_ref, out_ref):
    shards = back_ref.shape[0] // 2
    for i in range(shards):
        out_ref[0, 2 * i : 2 * i + 2] = back_ref[2 * (shards - 1 - i) : 2 * (shards - i)]


def on_device(shards, queries, passages, passage_len, slot_query, slot_passage, slot_count):
    sources, _, cap = slot_query.shape
    q_dev, q_tok, width = queries.shape
    pack = 128 // q_tok
    per_source = -(-cap // pack)
    swap = [(0, 1), (1, 0)]
    vmem, hbm, smem, anywhere = (pl.BlockSpec(memory_space=space) for space in (pltpu.VMEM, pltpu.HBM, pltpu.SMEM, pl.ANY))
    params = pltpu.CompilerParams(vmem_limit_bytes=12 * 1024 * 1024)
    row = jax.ShapeDtypeStruct((shards, 128), jnp.int32)

    def placed(space, *arrays):
        return [pltpu.with_memory_space_constraint(x, space) for x in arrays]

    def swapped(piece, d):
        return lax.ppermute(piece, "shard", [(i, i ^ d) for i in range(shards)])

    pieces = [queries, swapped(queries, 1)] + [None] * (shards - 2)
    for d in range(4, shards, 2):
        pieces[d] = swapped(queries, d)
    other_passages = lax.ppermute(passages, "sub", swap)

    calls = ((0, 1, *range(4, shards, 2)), (2, 3), range(5, shards, 2))
    sizes = tuple(map(len, calls))
    listed = [
        pltpu.SMEM(row.shape, row.dtype),
        pltpu.SMEM((len(calls),), jnp.int32),
        *(pltpu.SMEM((n * per_source + 2 * GROUPS,), jnp.int32) for n in sizes),
    ]
    mine, theirs, own_queries, own_passages, add = pl.pallas_call(
        functools.partial(pack_kernel, shards),
        out_shape=[
            pltpu.SMEM(row.shape, row.dtype), row, *(jax.ShapeDtypeStruct(x.shape, x.dtype) for x in (queries, passages)),
            jax.ShapeDtypeStruct((per_source * 128, 128), jnp.bfloat16),
        ],
        in_specs=[hbm] * 6,
        out_specs=[smem] + [vmem] * 4,
        scratch_shapes=[
            pltpu.VMEM(row.shape, row.dtype),
            pltpu.VMEM((sources, cap), jnp.int32),
            pltpu.VMEM((sources, cap), jnp.int32),
            pltpu.VMEM((sources,), jnp.int32),
            pltpu.VMEM(passage_len.shape, jnp.int32),
            pltpu.SemaphoreType.DMA((5,)),
            pltpu.SemaphoreType.DMA((CHUNKS,)),
            pltpu.SemaphoreType.DMA,
        ],
        compiler_params=params,
    )(*placed(pltpu.HBM, slot_query.reshape(sources, cap), slot_passage.reshape(sources, cap), slot_count.reshape(sources), passage_len, queries, passages))
    both = pl.pallas_call(
        pair_kernel,
        out_shape=jax.ShapeDtypeStruct((2, *queries.shape), queries.dtype),
        in_specs=[vmem] * 2,
        out_specs=vmem,
        compiler_params=params,
    )(own_queries, pieces[1])
    both = swapped(both, 2)
    for d in range(5, shards, 2):
        pieces[d] = swapped(pieces[1], d - 1) if d == shards - 1 else swapped(pieces[d - 1], 1)
    theirs, _ = lax.optimization_barrier((theirs, other_passages))
    other = lax.ppermute(theirs, "sub", swap)

    def scored(parts, lists, *earlier):
        call = len(earlier)
        n = sizes[call]
        scores = jax.ShapeDtypeStruct((2 * n if call < 2 else sources, cap), jnp.float32)
        if call:
            given = [x for rows, totals, *works in lists for x in placed(pltpu.SMEM, rows, totals, works[call])]
        else:
            given = [*placed(pltpu.SMEM, lists[0]), lists[1]]
        return pl.pallas_call(
            functools.partial(score_kernel, shards, calls, call, pack, cap),
            out_shape=scores if call else [scores, *listed[1:], *listed],
            in_specs=([smem] * 6 if call else [smem, anywhere]) + [vmem] * (len(parts) + 3 + call),
            out_specs=vmem if call else [vmem] + [smem] * (2 * len(listed) - 1),
            scratch_shapes=[
                pltpu.VMEM((n, *queries.shape), queries.dtype),
                pltpu.VMEM((per_source, 2 * n, 128), jnp.float32),
                *([] if call else [pltpu.SemaphoreType.DMA]),
            ],
            compiler_params=params,
            cost_estimate=pl.CostEstimate(flops=1_000_000_000, bytes_accessed=9_000_000, transcendentals=0),
        )(*given, *parts, *placed(pltpu.VMEM, own_passages, other_passages), add, *earlier)

    pieces[0] = own_queries
    near, _, far = calls
    first_scores, *made = scored([pieces[d] for d in reversed(near)], [mine, other])
    lists = [mine, *made[: len(calls) + 1]], made[len(calls) + 1 :]
    next_scores = scored([both], lists, first_scores)
    scores = scored([pieces[d] for d in reversed(far)], lists, first_scores, next_scores)
    order = [list(reversed(range(shards)))]
    returned = lax.all_to_all(scores, "shard", split_axis=0, concat_axis=0, axis_index_groups=order, tiled=True)
    return pl.pallas_call(
        order_kernel,
        out_shape=jax.ShapeDtypeStruct((1, sources, cap), jnp.float32),
        in_specs=[vmem],
        out_specs=vmem,
        compiler_params=params,
    )(returned)


def solution(mesh):
    return jax.shard_map(
        functools.partial(on_device, mesh.shape["shard"]),
        mesh=mesh,
        in_specs=(
            P(("groups", "shard", "sub"), None, None),
            P(("shard", "sub"), None, None),
            P(("shard", "sub")),
            P("groups", ("shard", "sub"), None),
            P("groups", ("shard", "sub"), None),
            P("groups", ("shard", "sub")),
        ),
        out_specs=P(("groups", "shard", "sub"), None, None),
        check_vma=False,
    )
```

```python
import functools

import jax
import jax.numpy as jnp
from jax import lax
from jax.experimental import pallas as pl
from jax.experimental.pallas import tpu as pltpu
from jax.sharding import PartitionSpec as P

GROUPS = 12
REST = 8
CHUNKS = 8
SHIFT = 8
QUERY, PASSAGE, LENGTH, COUNT = 0, 32, 64, 96


def distance(call, i):
    return (jnp.where(i == 1, 1, i * 2), i + 2, i * 2 + 5)[call]


def list_groups(sizes, pack, per_source, row_ref, total_ref, work_refs):
    me = lax.axis_index("shard")
    for call, (n, work_ref) in enumerate(zip(sizes, work_refs)):

        def list_source(i, total):
            live = row_ref[jnp.bitwise_xor(me, distance(call, i)), COUNT]
            for g in range(per_source):
                work_ref[total + g] = (i << SHIFT) + g
            return total + lax.shift_right_logical(live + pack - 1, pack.bit_length() - 1)

        total = 0
        if n <= 8:
            for i in range(n):
                total = list_source(i, total)
        else:
            total = lax.fori_loop(0, n, list_source, 0)
        for g in range(REST // 2 - 1):
            work_ref[total + g] = 0
        total_ref[call] = total


def pack_kernel(shards, *refs):
    query_hbm, passage_hbm, count_hbm, length_hbm, tokens_hbm, own_hbm, row_ref, theirs_ref, tokens_ref, own_ref, add_ref = refs[:11]
    mine_ref, query_ref, passage_ref, count_ref, length_ref, sems, own_sems, row_sem = refs[11:]
    copies = [
        pltpu.make_async_copy(src, dst, sems.at[i])
        for i, (src, dst) in enumerate(
            (
                (query_hbm, query_ref),
                (passage_hbm, passage_ref),
                (count_hbm, count_ref),
                (length_hbm, length_ref),
                (tokens_hbm, tokens_ref),
            )
        )
    ]
    size = own_ref.shape[0] // CHUNKS
    own_copies = [
        pltpu.make_async_copy(own_hbm.at[pl.ds(i * size, size)], own_ref.at[pl.ds(i * size, size)], own_sems.at[i])
        for i in range(CHUNKS)
    ]
    for copy in copies + own_copies:
        copy.start()
    row = lax.broadcasted_iota(jnp.int32, add_ref.shape, 0)
    col = lax.broadcasted_iota(jnp.int32, add_ref.shape, 1)
    q_bits = tokens_ref.shape[1].bit_length() - 1
    add_ref[...] = jnp.where(lax.shift_right_logical(row, q_bits) == col, 1.0, 0.0).astype(add_ref.dtype)
    for copy in copies:
        copy.wait()
    cap = query_ref.shape[1]
    lengths = length_ref[...].reshape(1, -1)
    counts = jnp.broadcast_to(count_ref[...].reshape(1, -1), (2 * shards, 2 * shards))
    row = lax.broadcasted_iota(jnp.int32, counts.shape, 0)
    col = lax.broadcasted_iota(jnp.int32, counts.shape, 1)
    counts = jnp.sum(jnp.where(row == col, counts, 0), axis=1, keepdims=True)
    blank = jnp.zeros((2 * shards, 32 - cap), jnp.int32)
    passage = jnp.concatenate([passage_ref[...], blank], axis=1)
    passage = jnp.concatenate([passage] * 4, axis=1)
    length = jnp.take_along_axis(jnp.broadcast_to(lengths, passage.shape), passage, axis=1)
    query = jnp.concatenate([jnp.concatenate([query_ref[...], blank], axis=1)] * 4, axis=1)
    lane = lax.broadcasted_iota(jnp.int32, passage.shape, 1)
    packed = jnp.where(lane < PASSAGE, query, jnp.where(lane < LENGTH, passage, jnp.where(lane < COUNT, length, counts)))
    packed = packed.reshape(shards, 2, 128)
    first = lax.axis_index("sub") == 0
    mine_ref[...] = jnp.where(first, packed[:, 0], packed[:, 1])
    theirs_ref[...] = jnp.where(first, packed[:, 1], packed[:, 0])
    row_copy = pltpu.make_async_copy(mine_ref, row_ref, row_sem)
    row_copy.start(priority=1)
    for copy in own_copies:
        copy.wait()
    row_copy.wait()


def score_kernel(shards, calls, call, pack, cap, *refs):
    distances = calls[call]
    n = len(distances)
    p = 1 if call == 1 else n
    if call == 0:
        (own_rows, rows), refs = refs[:2], refs[2:]
        refs, (out_ref, *outs, query_ref, best_ref, row_sem) = refs[: p + 3], refs[p + 3 :]
        made = (own_rows, *outs[: len(calls) + 1]), outs[len(calls) + 1 :]
        lists = [(row_ref, total_ref, work_ref) for row_ref, total_ref, work_ref, *_ in made]
        copy = pltpu.make_async_copy(rows, made[1][0], row_sem)
        copy.start()
    else:
        lists = [refs[:3], refs[3:6]]
        refs, (out_ref, query_ref, best_ref) = refs[6:-3], refs[-3:]
    pieces, passage_refs, add_ref, earlier = refs[:p], refs[p : p + 2], refs[p + 2], refs[p + 3 :]
    q_tok, width = query_ref.shape[2:]
    tok_slots = passage_refs[0].shape[1]
    per_source = best_ref.shape[0]
    lanes = pack * q_tok
    q_bits = q_tok.bit_length() - 1
    me, core = lax.axis_index("shard"), lax.axis_index("sub")
    if call == 1:
        query_ref[...] = pieces[0][...]
    else:
        for i, piece in enumerate(reversed(pieces)):
            query_ref[i] = piece[...]
    best_ref[...] = jnp.zeros_like(best_ref)
    token = lax.broadcasted_iota(jnp.int32, (tok_slots, lanes), 0)
    place = lax.shift_right_logical(lax.broadcasted_iota(jnp.int32, (1, lanes), 1), q_bits)
    blank = jnp.zeros((q_tok, width), query_ref.dtype)

    for which, passages in enumerate(passage_refs):
        meta_ref, total_ref, work_ref = lists[which]
        owner = core if which == 0 else 1 - core
        if call == 0:
            if which == 1:
                copy.wait()
            list_groups(tuple(map(len, calls)), pack, per_source, *made[which][:2], made[which][2:])
        total = total_ref[call]

        def one_step(first_group, groups):
            for j in range(groups):
                work = work_ref[first_group + j]
                i, g = lax.shift_right_logical(work, SHIFT), jnp.bitwise_and(work, (1 << SHIFT) - 1)
                shard = jnp.bitwise_xor(me, distance(call, i))
                rows, cols, limit = [], [], jnp.zeros((1, lanes), jnp.int32)
                for a in range(pack):
                    slot = g * pack + a
                    query, passage = meta_ref[shard, QUERY + slot], meta_ref[shard, PASSAGE + slot]
                    rows.append(jnp.concatenate([blank] * a + [query_ref[i, query]] + [blank] * (pack - 1 - a), axis=1))
                    cols.append(passages[passage])
                    limit = jnp.where(place == a, meta_ref[shard, LENGTH + slot], limit)
                sims = lax.dot_general(
                    jnp.concatenate(cols, axis=1), jnp.concatenate(rows, axis=0),
                    (((1,), (1,)), ((), ())), preferred_element_type=jnp.float32,
                )
                best = jnp.max(jnp.where(token < limit, sims, -1e30), axis=0, keepdims=True)
                best = jnp.where(place + g * pack < meta_ref[shard, COUNT], best, 0.0)
                best_ref[g, pl.ds(i * 2 + owner, 1), :] = best

        steps = lax.div(total + GROUPS - REST - 1, GROUPS)
        rest = total - steps * GROUPS

        @pl.loop(0, steps)
        def _(step):
            one_step(step * GROUPS, GROUPS)

        @pl.when(rest > REST // 2)
        def _():
            one_step(steps * GROUPS, REST)

        @pl.when((rest > 0) & (rest <= REST // 2))
        def _():
            one_step(steps * GROUPS, REST // 2)

    best = jnp.concatenate([best_ref[g] for g in range(per_source)], axis=1)
    high = best.astype(jnp.bfloat16)
    rest = best - high.astype(jnp.float32)
    middle = rest.astype(jnp.bfloat16)
    low = (rest - middle.astype(jnp.float32)).astype(jnp.bfloat16)
    parts = jnp.dot(jnp.concatenate([high, middle, low], axis=0), add_ref[...], preferred_element_type=jnp.float32)
    rows = best.shape[0]
    score = (parts[:rows] + parts[rows : 2 * rows] + parts[2 * rows :]) * (1.0 / q_tok)
    if call < 2:
        out_ref[...] = score[:, :cap]
        return
    for scores, at in zip((*(ref[...] for ref in earlier), score[:, :cap]), ((0, 1, *range(4, shards, 2)), (2, 3), distances)):
        for i, d in enumerate(at):
            out_ref[pl.ds((shards - 1 - jnp.bitwise_xor(me, d)) * 2, 2), :] = scores[2 * i : 2 * i + 2]


def pair_kernel(one_ref, other_ref, out_ref):
    out_ref[0] = one_ref[...]
    out_ref[1] = other_ref[...]


def order_kernel(back_ref, out_ref):
    shards = back_ref.shape[0] // 2
    for i in range(shards):
        out_ref[0, 2 * i : 2 * i + 2] = back_ref[2 * (shards - 1 - i) : 2 * (shards - i)]


def on_device(shards, queries, passages, passage_len, slot_query, slot_passage, slot_count):
    sources, _, cap = slot_query.shape
    q_dev, q_tok, width = queries.shape
    pack = 128 // q_tok
    per_source = -(-cap // pack)
    swap = [(0, 1), (1, 0)]
    vmem, hbm, smem, anywhere = (pl.BlockSpec(memory_space=space) for space in (pltpu.VMEM, pltpu.HBM, pltpu.SMEM, pl.ANY))
    params = pltpu.CompilerParams(vmem_limit_bytes=12 * 1024 * 1024)
    row = jax.ShapeDtypeStruct((shards, 128), jnp.int32)

    def placed(space, *arrays):
        return [pltpu.with_memory_space_constraint(x, space) for x in arrays]

    def swapped(piece, d):
        return lax.ppermute(piece, "shard", [(i, i ^ d) for i in range(shards)])

    pieces = [queries, swapped(queries, 1)] + [None] * (shards - 2)
    for d in range(4, shards, 2):
        pieces[d] = swapped(queries, d)
    other_passages = lax.ppermute(passages, "sub", swap)

    calls = ((0, 1, *range(4, shards, 2)), (2, 3), range(5, shards, 2))
    sizes = tuple(map(len, calls))
    listed = [
        pltpu.SMEM(row.shape, row.dtype),
        pltpu.SMEM((len(calls),), jnp.int32),
        *(pltpu.SMEM((n * per_source + 2 * GROUPS,), jnp.int32) for n in sizes),
    ]
    mine, theirs, own_queries, own_passages, add = pl.pallas_call(
        functools.partial(pack_kernel, shards),
        out_shape=[
            pltpu.SMEM(row.shape, row.dtype), row, *(jax.ShapeDtypeStruct(x.shape, x.dtype) for x in (queries, passages)),
            jax.ShapeDtypeStruct((per_source * 128, 128), jnp.bfloat16),
        ],
        in_specs=[hbm] * 6,
        out_specs=[smem] + [vmem] * 4,
        scratch_shapes=[
            pltpu.VMEM(row.shape, row.dtype),
            pltpu.VMEM((sources, cap), jnp.int32),
            pltpu.VMEM((sources, cap), jnp.int32),
            pltpu.VMEM((sources,), jnp.int32),
            pltpu.VMEM(passage_len.shape, jnp.int32),
            pltpu.SemaphoreType.DMA((5,)),
            pltpu.SemaphoreType.DMA((CHUNKS,)),
            pltpu.SemaphoreType.DMA,
        ],
        compiler_params=params,
    )(*placed(pltpu.HBM, slot_query.reshape(sources, cap), slot_passage.reshape(sources, cap), slot_count.reshape(sources), passage_len, queries, passages))
    both = pl.pallas_call(
        pair_kernel,
        out_shape=jax.ShapeDtypeStruct((2, *queries.shape), queries.dtype),
        in_specs=[vmem] * 2,
        out_specs=vmem,
        compiler_params=params,
    )(own_queries, pieces[1])
    both = swapped(both, 2)
    for d in range(5, shards, 2):
        pieces[d] = swapped(pieces[1], d - 1) if d == shards - 1 else swapped(pieces[d - 1], 1)
    theirs, _ = lax.optimization_barrier((theirs, other_passages))
    other = lax.ppermute(theirs, "sub", swap)

    def scored(parts, lists, *earlier):
        call = len(earlier)
        n = sizes[call]
        scores = jax.ShapeDtypeStruct((2 * n if call < 2 else sources, cap), jnp.float32)
        if call:
            given = [x for rows, totals, *works in lists for x in placed(pltpu.SMEM, rows, totals, works[call])]
        else:
            given = [*placed(pltpu.SMEM, lists[0]), lists[1]]
        return pl.pallas_call(
            functools.partial(score_kernel, shards, calls, call, pack, cap),
            out_shape=scores if call else [scores, *listed[1:], *listed],
            in_specs=([smem] * 6 if call else [smem, anywhere]) + [vmem] * (len(parts) + 3 + call),
            out_specs=vmem if call else [vmem] + [smem] * (2 * len(listed) - 1),
            scratch_shapes=[
                pltpu.VMEM((n, *queries.shape), queries.dtype),
                pltpu.VMEM((per_source, 2 * n, 128), jnp.float32),
                *([] if call else [pltpu.SemaphoreType.DMA]),
            ],
            compiler_params=params,
            cost_estimate=pl.CostEstimate(flops=1_000_000_000, bytes_accessed=9_000_000, transcendentals=0),
        )(*given, *parts, *placed(pltpu.VMEM, own_passages, other_passages), add, *earlier)

    pieces[0] = own_queries
    near, _, far = calls
    first_scores, *made = scored([pieces[d] for d in reversed(near)], [mine, other])
    lists = [mine, *made[: len(calls) + 1]], made[len(calls) + 1 :]
    next_scores = scored([both], lists, first_scores)
    scores = scored([pieces[d] for d in reversed(far)], lists, first_scores, next_scores)
    order = [list(reversed(range(shards)))]
    returned = lax.all_to_all(scores, "shard", split_axis=0, concat_axis=0, axis_index_groups=order, tiled=True)
    return pl.pallas_call(
        order_kernel,
        out_shape=jax.ShapeDtypeStruct((1, sources, cap), jnp.float32),
        in_specs=[vmem],
        out_specs=vmem,
        compiler_params=params,
    )(returned)


def solution(mesh):
    return jax.shard_map(
        functools.partial(on_device, mesh.shape["shard"]),
        mesh=mesh,
        in_specs=(
            P(("groups", "shard", "sub"), None, None),
            P(("shard", "sub"), None, None),
            P(("shard", "sub")),
            P("groups", ("shard", "sub"), None),
            P("groups", ("shard", "sub"), None),
            P("groups", ("shard", "sub")),
        ),
        out_specs=P(("groups", "shard", "sub"), None, None),
        check_vma=False,
    )
```

```python
import functools

import jax
import jax.numpy as jnp
from jax import lax
from jax.experimental import pallas as pl
from jax.experimental.pallas import tpu as pltpu
from jax.sharding import PartitionSpec as P

GROUPS = 12
REST = 8
CHUNKS = 8
SHIFT = 8
QUERY, PASSAGE, LENGTH, COUNT = 0, 32, 64, 96


def distance(call, i):
    return (jnp.where(i == 1, 1, i * 2), i + 2, i * 2 + 5)[call]


def list_groups(sizes, pack, per_source, row_ref, total_ref, work_refs):
    me = lax.axis_index("shard")
    for call, (n, work_ref) in enumerate(zip(sizes, work_refs)):

        def list_source(i, total):
            live = row_ref[jnp.bitwise_xor(me, distance(call, i)), COUNT]
            for g in range(per_source):
                work_ref[total + g] = (i << SHIFT) + g
            return total + lax.shift_right_logical(live + pack - 1, pack.bit_length() - 1)

        total = 0
        if n <= 8:
            for i in range(n):
                total = list_source(i, total)
        else:
            total = lax.fori_loop(0, n, list_source, 0)
        for g in range(REST // 2 - 1):
            work_ref[total + g] = 0
        total_ref[call] = total


def pack_kernel(shards, *refs):
    query_hbm, passage_hbm, count_hbm, length_hbm, tokens_hbm, own_hbm, mine_ref, theirs_ref, tokens_ref, own_ref, add_ref = refs[:11]
    query_ref, passage_ref, count_ref, length_ref, sems, own_sems = refs[11:]
    copies = [
        pltpu.make_async_copy(src, dst, sems.at[i])
        for i, (src, dst) in enumerate(
            (
                (query_hbm, query_ref),
                (passage_hbm, passage_ref),
                (count_hbm, count_ref),
                (length_hbm, length_ref),
                (tokens_hbm, tokens_ref),
            )
        )
    ]
    size = own_ref.shape[0] // CHUNKS
    own_copies = [
        pltpu.make_async_copy(own_hbm.at[pl.ds(i * size, size)], own_ref.at[pl.ds(i * size, size)], own_sems.at[i])
        for i in range(CHUNKS)
    ]
    for copy in copies:
        copy.start()
    for i, copy in enumerate(own_copies):
        copy.start(priority=i % 2)
    row = lax.broadcasted_iota(jnp.int32, add_ref.shape, 0)
    col = lax.broadcasted_iota(jnp.int32, add_ref.shape, 1)
    q_bits = tokens_ref.shape[1].bit_length() - 1
    add_ref[...] = jnp.where(lax.shift_right_logical(row, q_bits) == col, 1.0, 0.0).astype(add_ref.dtype)
    for copy in copies:
        copy.wait()
    cap = query_ref.shape[1]
    lengths = length_ref[...].reshape(1, -1)
    counts = jnp.broadcast_to(count_ref[...].reshape(1, -1), (2 * shards, 2 * shards))
    row = lax.broadcasted_iota(jnp.int32, counts.shape, 0)
    col = lax.broadcasted_iota(jnp.int32, counts.shape, 1)
    counts = jnp.sum(jnp.where(row == col, counts, 0), axis=1, keepdims=True)
    blank = jnp.zeros((2 * shards, 32 - cap), jnp.int32)
    passage = jnp.concatenate([passage_ref[...], blank], axis=1)
    passage = jnp.concatenate([passage] * 4, axis=1)
    length = jnp.take_along_axis(jnp.broadcast_to(lengths, passage.shape), passage, axis=1)
    query = jnp.concatenate([jnp.concatenate([query_ref[...], blank], axis=1)] * 4, axis=1)
    lane = lax.broadcasted_iota(jnp.int32, passage.shape, 1)
    packed = jnp.where(lane < PASSAGE, query, jnp.where(lane < LENGTH, passage, jnp.where(lane < COUNT, length, counts)))
    packed = packed.reshape(shards, 2, 128)
    first = lax.axis_index("sub") == 0
    mine_ref[...] = jnp.where(first, packed[:, 0], packed[:, 1])
    theirs_ref[...] = jnp.where(first, packed[:, 1], packed[:, 0])
    for copy in own_copies:
        copy.wait()


def score_kernel(shards, calls, call, pack, cap, *refs):
    distances = calls[call]
    n = len(distances)
    p = 1 if call == 1 else n
    if call == 0:
        rows, refs = refs[:2], refs[2:]
        refs, (out_ref, *outs, query_ref, best_ref, row_sems) = refs[: p + 3], refs[p + 3 :]
        made = outs[: len(outs) // 2], outs[len(outs) // 2 :]
        lists = [(row_ref, total_ref, work_ref) for row_ref, total_ref, work_ref, *_ in made]
        copies = [pltpu.make_async_copy(row, each[0], row_sems.at[i]) for i, (row, each) in enumerate(zip(rows, made))]
        for copy in copies:
            copy.start()
    else:
        lists = [refs[:3], refs[3:6]]
        refs, (out_ref, query_ref, best_ref) = refs[6:-3], refs[-3:]
    pieces, passage_refs, add_ref, earlier = refs[:p], refs[p : p + 2], refs[p + 2], refs[p + 3 :]
    q_tok, width = query_ref.shape[2:]
    tok_slots = passage_refs[0].shape[1]
    per_source = best_ref.shape[0]
    lanes = pack * q_tok
    q_bits = q_tok.bit_length() - 1
    me, core = lax.axis_index("shard"), lax.axis_index("sub")
    if call == 1:
        query_ref[...] = pieces[0][...]
    else:
        for i, piece in enumerate(reversed(pieces)):
            query_ref[i] = piece[...]
    best_ref[...] = jnp.zeros_like(best_ref)
    token = lax.broadcasted_iota(jnp.int32, (tok_slots, lanes), 0)
    place = lax.shift_right_logical(lax.broadcasted_iota(jnp.int32, (1, lanes), 1), q_bits)
    blank = jnp.zeros((q_tok, width), query_ref.dtype)

    for which, passages in enumerate(passage_refs):
        meta_ref, total_ref, work_ref = lists[which]
        owner = core if which == 0 else 1 - core
        if call == 0:
            copies[which].wait()
            list_groups(tuple(map(len, calls)), pack, per_source, *made[which][:2], made[which][2:])
        total = total_ref[call]

        def one_step(first_group, groups):
            for j in range(groups):
                work = work_ref[first_group + j]
                i, g = lax.shift_right_logical(work, SHIFT), jnp.bitwise_and(work, (1 << SHIFT) - 1)
                shard = jnp.bitwise_xor(me, distance(call, i))
                rows, cols, limit = [], [], jnp.zeros((1, lanes), jnp.int32)
                for a in range(pack):
                    slot = g * pack + a
                    query, passage = meta_ref[shard, QUERY + slot], meta_ref[shard, PASSAGE + slot]
                    rows.append(jnp.concatenate([blank] * a + [query_ref[i, query]] + [blank] * (pack - 1 - a), axis=1))
                    cols.append(passages[passage])
                    limit = jnp.where(place == a, meta_ref[shard, LENGTH + slot], limit)
                sims = lax.dot_general(
                    jnp.concatenate(cols, axis=1), jnp.concatenate(rows, axis=0),
                    (((1,), (1,)), ((), ())), preferred_element_type=jnp.float32,
                )
                best = jnp.max(jnp.where(token < limit, sims, -1e30), axis=0, keepdims=True)
                best = jnp.where(place + g * pack < meta_ref[shard, COUNT], best, 0.0)
                best_ref[g, pl.ds(i * 2 + owner, 1), :] = best

        steps = lax.div(total + GROUPS - REST - 1, GROUPS)
        rest = total - steps * GROUPS

        @pl.loop(0, steps)
        def _(step):
            one_step(step * GROUPS, GROUPS)

        @pl.when(rest > REST // 2)
        def _():
            one_step(steps * GROUPS, REST)

        @pl.when((rest > 0) & (rest <= REST // 2))
        def _():
            one_step(steps * GROUPS, REST // 2)

    best = jnp.concatenate([best_ref[g] for g in range(per_source)], axis=1)
    high = best.astype(jnp.bfloat16)
    rest = best - high.astype(jnp.float32)
    middle = rest.astype(jnp.bfloat16)
    low = (rest - middle.astype(jnp.float32)).astype(jnp.bfloat16)
    parts = jnp.dot(jnp.concatenate([high, middle, low], axis=0), add_ref[...], preferred_element_type=jnp.float32)
    rows = best.shape[0]
    score = (parts[:rows] + parts[rows : 2 * rows] + parts[2 * rows :]) * (1.0 / q_tok)
    if call < 2:
        out_ref[...] = score[:, :cap]
        return
    for scores, at in zip((*(ref[...] for ref in earlier), score[:, :cap]), ((0, 1, *range(4, shards, 2)), (2, 3), distances)):
        for i, d in enumerate(at):
            out_ref[pl.ds((shards - 1 - jnp.bitwise_xor(me, d)) * 2, 2), :] = scores[2 * i : 2 * i + 2]


def pair_kernel(one_ref, other_ref, out_ref):
    out_ref[0] = one_ref[...]
    out_ref[1] = other_ref[...]


def order_kernel(back_ref, out_ref):
    shards = back_ref.shape[0] // 2
    for i in range(shards):
        out_ref[0, 2 * i : 2 * i + 2] = back_ref[2 * (shards - 1 - i) : 2 * (shards - i)]


def on_device(shards, queries, passages, passage_len, slot_query, slot_passage, slot_count):
    sources, _, cap = slot_query.shape
    q_dev, q_tok, width = queries.shape
    pack = 128 // q_tok
    per_source = -(-cap // pack)
    swap = [(0, 1), (1, 0)]
    vmem, hbm, smem, anywhere = (pl.BlockSpec(memory_space=space) for space in (pltpu.VMEM, pltpu.HBM, pltpu.SMEM, pl.ANY))
    params = pltpu.CompilerParams(vmem_limit_bytes=12 * 1024 * 1024)
    row = jax.ShapeDtypeStruct((shards, 128), jnp.int32)

    def placed(space, *arrays):
        return [pltpu.with_memory_space_constraint(x, space) for x in arrays]

    def swapped(piece, d):
        return lax.ppermute(piece, "shard", [(i, i ^ d) for i in range(shards)])

    pieces = [queries, swapped(queries, 1)] + [None] * (shards - 2)
    for d in range(4, shards, 2):
        pieces[d] = swapped(queries, d)
    other_passages = lax.ppermute(passages, "sub", swap)

    calls = ((0, 1, *range(4, shards, 2)), (2, 3), range(5, shards, 2))
    sizes = tuple(map(len, calls))
    listed = [
        pltpu.SMEM(row.shape, row.dtype),
        pltpu.SMEM((len(calls),), jnp.int32),
        *(pltpu.SMEM((n * per_source + 2 * GROUPS,), jnp.int32) for n in sizes),
    ]
    mine, theirs, own_queries, own_passages, add = pl.pallas_call(
        functools.partial(pack_kernel, shards),
        out_shape=[
            row, row, *(jax.ShapeDtypeStruct(x.shape, x.dtype) for x in (queries, passages)),
            jax.ShapeDtypeStruct((per_source * 128, 128), jnp.bfloat16),
        ],
        in_specs=[hbm] * 6,
        out_specs=[vmem] * 5,
        scratch_shapes=[
            pltpu.VMEM((sources, cap), jnp.int32),
            pltpu.VMEM((sources, cap), jnp.int32),
            pltpu.VMEM((sources,), jnp.int32),
            pltpu.VMEM(passage_len.shape, jnp.int32),
            pltpu.SemaphoreType.DMA((5,)),
            pltpu.SemaphoreType.DMA((CHUNKS,)),
        ],
        compiler_params=params,
    )(*placed(pltpu.HBM, slot_query.reshape(sources, cap), slot_passage.reshape(sources, cap), slot_count.reshape(sources), passage_len, queries, passages))
    both = pl.pallas_call(
        pair_kernel,
        out_shape=jax.ShapeDtypeStruct((2, *queries.shape), queries.dtype),
        in_specs=[vmem] * 2,
        out_specs=vmem,
        compiler_params=params,
    )(own_queries, pieces[1])
    both = swapped(both, 2)
    for d in range(5, shards, 2):
        pieces[d] = swapped(pieces[1], d - 1) if d == shards - 1 else swapped(pieces[d - 1], 1)
    theirs, _ = lax.optimization_barrier((theirs, other_passages))
    other = lax.ppermute(theirs, "sub", swap)

    def scored(parts, lists, *earlier):
        call = len(earlier)
        n = sizes[call]
        scores = jax.ShapeDtypeStruct((2 * n if call < 2 else sources, cap), jnp.float32)
        if call:
            given = [x for rows, totals, *works in lists for x in placed(pltpu.SMEM, rows, totals, works[call])]
        else:
            given = lists
        return pl.pallas_call(
            functools.partial(score_kernel, shards, calls, call, pack, cap),
            out_shape=scores if call else [scores, *listed, *listed],
            in_specs=([smem] * 6 if call else [anywhere] * 2) + [vmem] * (len(parts) + 3 + call),
            out_specs=vmem if call else [vmem] + [smem] * (2 * len(listed)),
            scratch_shapes=[
                pltpu.VMEM((n, *queries.shape), queries.dtype),
                pltpu.VMEM((per_source, 2 * n, 128), jnp.float32),
                *([] if call else [pltpu.SemaphoreType.DMA((2,))]),
            ],
            compiler_params=params,
            cost_estimate=pl.CostEstimate(flops=1_000_000_000, bytes_accessed=9_000_000, transcendentals=0),
        )(*given, *parts, *placed(pltpu.VMEM, own_passages, other_passages), add, *earlier)

    pieces[0] = own_queries
    near, _, far = calls
    first_scores, *made = scored([pieces[d] for d in reversed(near)], [mine, other])
    lists = made[: len(listed)], made[len(listed) :]
    next_scores = scored([both], lists, first_scores)
    scores = scored([pieces[d] for d in reversed(far)], lists, first_scores, next_scores)
    order = [list(reversed(range(shards)))]
    returned = lax.all_to_all(scores, "shard", split_axis=0, concat_axis=0, axis_index_groups=order, tiled=True)
    return pl.pallas_call(
        order_kernel,
        out_shape=jax.ShapeDtypeStruct((1, sources, cap), jnp.float32),
        in_specs=[vmem],
        out_specs=vmem,
        compiler_params=params,
    )(returned)


def solution(mesh):
    return jax.shard_map(
        functools.partial(on_device, mesh.shape["shard"]),
        mesh=mesh,
        in_specs=(
            P(("groups", "shard", "sub"), None, None),
            P(("shard", "sub"), None, None),
            P(("shard", "sub")),
            P("groups", ("shard", "sub"), None),
            P("groups", ("shard", "sub"), None),
            P("groups", ("shard", "sub")),
        ),
        out_specs=P(("groups", "shard", "sub"), None, None),
        check_vma=False,
    )
```

```python
import functools

import jax
import jax.numpy as jnp
from jax import lax
from jax.experimental import pallas as pl
from jax.experimental.pallas import tpu as pltpu
from jax.sharding import PartitionSpec as P

GROUPS = 8
CHUNKS = 8
SHIFT = 8
QUERY, PASSAGE, LENGTH, COUNT = 0, 32, 64, 96


def distance(call, i):
    return (jnp.where(i == 1, 1, i * 2), i + 2, i * 2 + 5)[call]


def list_groups(sizes, pack, per_source, row_ref, total_ref, work_refs):
    me = lax.axis_index("shard")
    for call, (n, work_ref) in enumerate(zip(sizes, work_refs)):

        def list_source(i, total):
            live = row_ref[jnp.bitwise_xor(me, distance(call, i)), COUNT]
            for g in range(per_source):
                work_ref[total + g] = (i << SHIFT) + g
            return total + lax.shift_right_logical(live + pack - 1, pack.bit_length() - 1)

        total = 0
        if n <= 8:
            for i in range(n):
                total = list_source(i, total)
        else:
            total = lax.fori_loop(0, n, list_source, 0)
        for g in range(GROUPS // 2 - 1):
            work_ref[total + g] = 0
        total_ref[call] = total


def pack_kernel(shards, *refs):
    query_hbm, passage_hbm, count_hbm, length_hbm, tokens_hbm, own_hbm, mine_ref, theirs_ref, tokens_ref, own_ref, add_ref = refs[:11]
    query_ref, passage_ref, count_ref, length_ref, sems, own_sems = refs[11:]
    copies = [
        pltpu.make_async_copy(src, dst, sems.at[i])
        for i, (src, dst) in enumerate(
            (
                (query_hbm, query_ref),
                (passage_hbm, passage_ref),
                (count_hbm, count_ref),
                (length_hbm, length_ref),
                (tokens_hbm, tokens_ref),
            )
        )
    ]
    size = own_ref.shape[0] // CHUNKS
    own_copies = [
        pltpu.make_async_copy(own_hbm.at[pl.ds(i * size, size)], own_ref.at[pl.ds(i * size, size)], own_sems.at[i])
        for i in range(CHUNKS)
    ]
    for copy in copies + own_copies:
        copy.start()
    row = lax.broadcasted_iota(jnp.int32, add_ref.shape, 0)
    col = lax.broadcasted_iota(jnp.int32, add_ref.shape, 1)
    q_bits = tokens_ref.shape[1].bit_length() - 1
    add_ref[...] = jnp.where(lax.shift_right_logical(row, q_bits) == col, 1.0, 0.0).astype(add_ref.dtype)
    for copy in copies:
        copy.wait()
    cap = query_ref.shape[1]
    lengths = length_ref[...].reshape(1, -1)
    counts = jnp.broadcast_to(count_ref[...].reshape(1, -1), (2 * shards, 2 * shards))
    row = lax.broadcasted_iota(jnp.int32, counts.shape, 0)
    col = lax.broadcasted_iota(jnp.int32, counts.shape, 1)
    counts = jnp.sum(jnp.where(row == col, counts, 0), axis=1, keepdims=True)
    blank = jnp.zeros((2 * shards, 32 - cap), jnp.int32)
    passage = jnp.concatenate([passage_ref[...], blank], axis=1)
    passage = jnp.concatenate([passage] * 4, axis=1)
    length = jnp.take_along_axis(jnp.broadcast_to(lengths, passage.shape), passage, axis=1)
    query = jnp.concatenate([jnp.concatenate([query_ref[...], blank], axis=1)] * 4, axis=1)
    lane = lax.broadcasted_iota(jnp.int32, passage.shape, 1)
    packed = jnp.where(lane < PASSAGE, query, jnp.where(lane < LENGTH, passage, jnp.where(lane < COUNT, length, counts)))
    packed = packed.reshape(shards, 2, 128)
    first = lax.axis_index("sub") == 0
    mine_ref[...] = jnp.where(first, packed[:, 0], packed[:, 1])
    theirs_ref[...] = jnp.where(first, packed[:, 1], packed[:, 0])
    for copy in own_copies:
        copy.wait()


def score_kernel(shards, calls, call, pack, cap, *refs):
    distances = calls[call]
    n = len(distances)
    p = 1 if call == 1 else n
    if call == 0:
        rows, refs = refs[:2], refs[2:]
        refs, (out_ref, *outs, query_ref, best_ref, row_sems) = refs[: p + 3], refs[p + 3 :]
        made = outs[: len(outs) // 2], outs[len(outs) // 2 :]
        lists = [(row_ref, total_ref, work_ref) for row_ref, total_ref, work_ref, *_ in made]
        copies = [pltpu.make_async_copy(row, each[0], row_sems.at[i]) for i, (row, each) in enumerate(zip(rows, made))]
        for copy in copies:
            copy.start()
    else:
        lists = [refs[:3], refs[3:6]]
        refs, (out_ref, query_ref, best_ref) = refs[6:-3], refs[-3:]
    pieces, passage_refs, add_ref, earlier = refs[:p], refs[p : p + 2], refs[p + 2], refs[p + 3 :]
    q_tok, width = query_ref.shape[2:]
    tok_slots = passage_refs[0].shape[1]
    per_source = best_ref.shape[0]
    lanes = pack * q_tok
    q_bits = q_tok.bit_length() - 1
    me, core = lax.axis_index("shard"), lax.axis_index("sub")
    if call == 1:
        query_ref[...] = pieces[0][...]
    else:
        for i, piece in enumerate(reversed(pieces)):
            query_ref[i] = piece[...]
    best_ref[...] = jnp.zeros_like(best_ref)
    token = lax.broadcasted_iota(jnp.int32, (tok_slots, lanes), 0)
    place = lax.shift_right_logical(lax.broadcasted_iota(jnp.int32, (1, lanes), 1), q_bits)
    blank = jnp.zeros((q_tok, width), query_ref.dtype)

    for which, passages in enumerate(passage_refs):
        meta_ref, total_ref, work_ref = lists[which]
        owner = core if which == 0 else 1 - core
        if call == 0:
            copies[which].wait()
            list_groups(tuple(map(len, calls)), pack, per_source, *made[which][:2], made[which][2:])
        total = total_ref[call]

        def one_step(first_group, groups):
            for j in range(groups):
                work = work_ref[first_group + j]
                i, g = lax.shift_right_logical(work, SHIFT), jnp.bitwise_and(work, (1 << SHIFT) - 1)
                shard = jnp.bitwise_xor(me, distance(call, i))
                rows, cols, limit = [], [], jnp.zeros((1, lanes), jnp.int32)
                for a in range(pack):
                    slot = g * pack + a
                    query, passage = meta_ref[shard, QUERY + slot], meta_ref[shard, PASSAGE + slot]
                    rows.append(jnp.concatenate([blank] * a + [query_ref[i, query]] + [blank] * (pack - 1 - a), axis=1))
                    cols.append(passages[passage])
                    limit = jnp.where(place == a, meta_ref[shard, LENGTH + slot], limit)
                sims = lax.dot_general(
                    jnp.concatenate(cols, axis=1), jnp.concatenate(rows, axis=0),
                    (((1,), (1,)), ((), ())), preferred_element_type=jnp.float32,
                )
                best = jnp.max(jnp.where(token < limit, sims, -1e30), axis=0, keepdims=True)
                best = jnp.where(place + g * pack < meta_ref[shard, COUNT], best, 0.0)
                best_ref[g, pl.ds(i * 2 + owner, 1), :] = best

        half = GROUPS // 2
        steps = lax.shift_right_logical(total + half - 1, GROUPS.bit_length() - 1)

        @pl.loop(0, steps)
        def _(step):
            one_step(step * GROUPS, GROUPS)

        @pl.when(total > steps * GROUPS)
        def _():
            one_step(steps * GROUPS, half)

    best = jnp.concatenate([best_ref[g] for g in range(per_source)], axis=1)
    high = best.astype(jnp.bfloat16)
    rest = best - high.astype(jnp.float32)
    middle = rest.astype(jnp.bfloat16)
    low = (rest - middle.astype(jnp.float32)).astype(jnp.bfloat16)
    parts = jnp.dot(jnp.concatenate([high, middle, low], axis=0), add_ref[...], preferred_element_type=jnp.float32)
    rows = best.shape[0]
    score = (parts[:rows] + parts[rows : 2 * rows] + parts[2 * rows :]) * (1.0 / q_tok)
    if call < 2:
        out_ref[...] = score[:, :cap]
        return
    for scores, at in zip((*(ref[...] for ref in earlier), score[:, :cap]), ((0, 1, *range(4, shards, 2)), (2, 3), distances)):
        for i, d in enumerate(at):
            out_ref[pl.ds((shards - 1 - jnp.bitwise_xor(me, d)) * 2, 2), :] = scores[2 * i : 2 * i + 2]


def pair_kernel(one_ref, other_ref, out_ref):
    out_ref[0] = one_ref[...]
    out_ref[1] = other_ref[...]


def order_kernel(back_ref, out_ref):
    shards = back_ref.shape[0] // 2
    for i in range(shards):
        out_ref[0, 2 * i : 2 * i + 2] = back_ref[2 * (shards - 1 - i) : 2 * (shards - i)]


def on_device(shards, queries, passages, passage_len, slot_query, slot_passage, slot_count):
    sources, _, cap = slot_query.shape
    q_dev, q_tok, width = queries.shape
    pack = 128 // q_tok
    per_source = -(-cap // pack)
    swap = [(0, 1), (1, 0)]
    vmem, hbm, smem, anywhere = (pl.BlockSpec(memory_space=space) for space in (pltpu.VMEM, pltpu.HBM, pltpu.SMEM, pl.ANY))
    params = pltpu.CompilerParams(vmem_limit_bytes=12 * 1024 * 1024)
    row = jax.ShapeDtypeStruct((shards, 128), jnp.int32)

    def placed(space, *arrays):
        return [pltpu.with_memory_space_constraint(x, space) for x in arrays]

    def swapped(piece, d):
        return lax.ppermute(piece, "shard", [(i, i ^ d) for i in range(shards)])

    pieces = [queries, swapped(queries, 1)] + [None] * (shards - 2)
    for d in range(4, shards, 2):
        pieces[d] = swapped(queries, d)
    other_passages = lax.ppermute(passages, "sub", swap)

    calls = ((0, 1, *range(4, shards, 2)), (2, 3), range(5, shards, 2))
    sizes = tuple(map(len, calls))
    listed = [
        pltpu.SMEM(row.shape, row.dtype),
        pltpu.SMEM((len(calls),), jnp.int32),
        *(pltpu.SMEM((n * per_source + 2 * GROUPS,), jnp.int32) for n in sizes),
    ]
    mine, theirs, own_queries, own_passages, add = pl.pallas_call(
        functools.partial(pack_kernel, shards),
        out_shape=[
            row, row, *(jax.ShapeDtypeStruct(x.shape, x.dtype) for x in (queries, passages)),
            jax.ShapeDtypeStruct((per_source * 128, 128), jnp.bfloat16),
        ],
        in_specs=[hbm] * 6,
        out_specs=[vmem] * 5,
        scratch_shapes=[
            pltpu.VMEM((sources, cap), jnp.int32),
            pltpu.VMEM((sources, cap), jnp.int32),
            pltpu.VMEM((sources,), jnp.int32),
            pltpu.VMEM(passage_len.shape, jnp.int32),
            pltpu.SemaphoreType.DMA((5,)),
            pltpu.SemaphoreType.DMA((CHUNKS,)),
        ],
        compiler_params=params,
    )(*placed(pltpu.HBM, slot_query.reshape(sources, cap), slot_passage.reshape(sources, cap), slot_count.reshape(sources), passage_len, queries, passages))
    both = pl.pallas_call(
        pair_kernel,
        out_shape=jax.ShapeDtypeStruct((2, *queries.shape), queries.dtype),
        in_specs=[vmem] * 2,
        out_specs=vmem,
        compiler_params=params,
    )(own_queries, pieces[1])
    both = swapped(both, 2)
    for d in range(5, shards, 2):
        pieces[d] = swapped(pieces[1], d - 1) if d == shards - 1 else swapped(pieces[d - 1], 1)
    theirs, _ = lax.optimization_barrier((theirs, other_passages))
    other = lax.ppermute(theirs, "sub", swap)

    def scored(parts, lists, *earlier):
        call = len(earlier)
        n = sizes[call]
        scores = jax.ShapeDtypeStruct((2 * n if call < 2 else sources, cap), jnp.float32)
        if call:
            given = [x for rows, totals, *works in lists for x in placed(pltpu.SMEM, rows, totals, works[call])]
        else:
            given = lists
        return pl.pallas_call(
            functools.partial(score_kernel, shards, calls, call, pack, cap),
            out_shape=scores if call else [scores, *listed, *listed],
            in_specs=([smem] * 6 if call else [anywhere] * 2) + [vmem] * (len(parts) + 3 + call),
            out_specs=vmem if call else [vmem] + [smem] * (2 * len(listed)),
            scratch_shapes=[
                pltpu.VMEM((n, *queries.shape), queries.dtype),
                pltpu.VMEM((per_source, 2 * n, 128), jnp.float32),
                *([] if call else [pltpu.SemaphoreType.DMA((2,))]),
            ],
            compiler_params=params,
            cost_estimate=pl.CostEstimate(flops=1_000_000_000, bytes_accessed=9_000_000, transcendentals=0),
        )(*given, *parts, *placed(pltpu.VMEM, own_passages, other_passages), add, *earlier)

    pieces[0] = own_queries
    near, _, far = calls
    first_scores, *made = scored([pieces[d] for d in reversed(near)], [mine, other])
    lists = made[: len(listed)], made[len(listed) :]
    next_scores = scored([both], lists, first_scores)
    scores = scored([pieces[d] for d in reversed(far)], lists, first_scores, next_scores)
    order = [list(reversed(range(shards)))]
    returned = lax.all_to_all(scores, "shard", split_axis=0, concat_axis=0, axis_index_groups=order, tiled=True)
    return pl.pallas_call(
        order_kernel,
        out_shape=jax.ShapeDtypeStruct((1, sources, cap), jnp.float32),
        in_specs=[vmem],
        out_specs=vmem,
        compiler_params=params,
    )(returned)


def solution(mesh):
    return jax.shard_map(
        functools.partial(on_device, mesh.shape["shard"]),
        mesh=mesh,
        in_specs=(
            P(("groups", "shard", "sub"), None, None),
            P(("shard", "sub"), None, None),
            P(("shard", "sub")),
            P("groups", ("shard", "sub"), None),
            P("groups", ("shard", "sub"), None),
            P("groups", ("shard", "sub")),
        ),
        out_specs=P(("groups", "shard", "sub"), None, None),
        check_vma=False,
    )
```
